32 devices in a mesh: layer: 4 (over x, core), sph: 8 (over z, y).
Axes of the slice: x: 2, y: 2, z: 4, core: 2. Of those that a mesh axis runs over, the one named last changes fastest.
Arguments:
- out_basis: float32 [4, 2, 2, 48, 512], P('layer'), may hold values from -0.875 to 0.875
- in_basis: float32 [4, 2, 48, 512], P('layer'), may hold values from -0.875 to 0.875
- tmatrix: float32 [4, 128, 2, 48, 48], P('layer', 'sph'), may hold values from -0.0078125 to 0.0078125
- sites: int32 [4, 128], P('layer', 'sph'), may hold values from 0 to 1023
- waves: int32 [2, 256], replicated, may hold values from -12 to 12
- layer_phase: float32 [4, 512], P('layer'), may hold values from -3.140625 to 3.140625
Outputs:
- film_reflection: float32 [2, 512, 512], P(None, 'sph', 'layer')
- film_transmission: float32 [2, 512, 512], P(None, 'sph', 'layer')
The draws below stay inside these ranges and needn't reach their ends.
All inputs are finite; a program needn't handle non-finite values.
Results may differ from the reference program's by a relative error of at most 0.025.
Values may be sent and summed in bfloat16 or wider, within the bound.
No kernel may reach another device: no remote copies, remote signals or barrier semaphores. Data moves between devices by JAX's collectives and lax.ppermute only.
A program may use at most 64 MiB of HBM per device.

```python
import math
import jax
import jax.numpy as jnp
from jax import lax

WAVES = 256
MULTI = 48
LATTICE = 32
W = 512
SPHERES = 128
LAYERS = 4


def with_ends(values, rng, low, top_value):
    longest = values.shape.index(max(values.shape))
    spots = []
    for shift in (0, 1):
        where = [jax.random.randint(jax.random.fold_in(rng, axis), (), 0, length) for axis, length in enumerate(values.shape)]
        where[longest] = (where[longest] + shift) % values.shape[longest]
        spots.append(tuple(where))
    return values.at[spots[0]].set(low).at[spots[1]].set(top_value)


def level_of(rng, extent, cuts, least, top_value):
    loudness = 1.0
    for axis_at, shards_of in cuts:
        draws = jax.random.uniform(jax.random.fold_in(jax.random.fold_in(rng, 6), axis_at), (shards_of,), jnp.float32, least / len(cuts), top_value / len(cuts))
        loudness = loudness * jnp.repeat(jnp.exp(draws), extent[axis_at] // shards_of).reshape((-1,) + (1,) * (len(extent) - 1 - axis_at))
    return loudness


def scatter_about(rng, shape, spread, reach, split=(), dtype=jnp.bfloat16):
    values = jax.random.normal(rng, shape, jnp.float32) * spread
    if len(split) > 0:
        values = level_of(rng, shape, split, -0.22, 0.18) * values
    return jnp.clip(values, min=-reach, max=reach).astype(dtype)


def setup_inputs(seed: int = 0) -> dict:
    keys = jax.random.split(jax.random.key(seed), 7)
    out_basis = scatter_about(keys[0], (LAYERS, 2, 2, MULTI, W), MULTI ** -0.5, 0.875, ((0, 4),), jnp.float32)
    in_basis = scatter_about(keys[1], (LAYERS, 2, MULTI, W), MULTI ** -0.5, 0.875, ((0, 4),), jnp.float32)
    tmatrix = scatter_about(keys[2], (LAYERS, SPHERES, 2, MULTI, MULTI), (0.15 / (SPHERES * W) ** 0.5), 0.0078125, ((0, 4), (1, 8)), jnp.float32)
    sites = with_ends(jax.random.randint(keys[3], (LAYERS, SPHERES), 0, LATTICE * LATTICE), jax.random.fold_in(keys[3], 1), 0, (LATTICE * LATTICE) - 1).astype(jnp.int32)
    waves = with_ends(jax.random.randint(keys[4], (2, WAVES), -12, 13), jax.random.fold_in(keys[4], 1), -12, 12).astype(jnp.int32)
    layer_phase = jnp.clip(jax.random.uniform(keys[5], (LAYERS, W), jnp.float32, -3.140625, 3.140625), -3.140625, 3.140625)
    return {"out_basis": out_basis, "in_basis": in_basis, "tmatrix": tmatrix, "sites": sites, "waves": waves, "layer_phase": layer_phase}


TWO_PI = 2.0 * math.pi


def wave_angles(site_list, waves):
    column = site_list // LATTICE
    along = site_list % LATTICE
    phase_index = (waves[0][None, :] * column[:, None] + waves[1][None, :] * along[:, None]) % LATTICE
    angles = phase_index.astype(jnp.float32) * (TWO_PI / LATTICE)
    return jnp.concatenate([angles, angles], axis=1)


def factors(out_layer, in_layer, tm_layer, angles):
    highest = lax.Precision.HIGHEST
    basis_re = out_layer[:, 0]
    basis_im = out_layer[:, 1]
    tmat_re = tm_layer[:, 0]
    tmat_im = tm_layer[:, 1]
    prod_re = jnp.einsum('kjw,sjm->ksmw', basis_re, tmat_re, precision=highest) - jnp.einsum('kjw,sjm->ksmw', basis_im, tmat_im, precision=highest)
    prod_im = jnp.einsum('kjw,sjm->ksmw', basis_re, tmat_im, precision=highest) + jnp.einsum('kjw,sjm->ksmw', basis_im, tmat_re, precision=highest)
    cosine = jnp.cos(angles)
    sine = jnp.sin(angles)
    left_re = prod_re * cosine[None, :, None, :] - prod_im * sine[None, :, None, :]
    left_im = prod_re * sine[None, :, None, :] + prod_im * cosine[None, :, None, :]
    right_re = in_layer[0][None] * cosine[:, None, :] + in_layer[1][None] * sine[:, None, :]
    right_im = in_layer[1][None] * cosine[:, None, :] - in_layer[0][None] * sine[:, None, :]
    inner = left_re.shape[1] * left_re.shape[2]
    width = left_re.shape[3]
    left_re = left_re.reshape(2, inner, width)
    left_im = left_im.reshape(2, inner, width)
    right_re = right_re.reshape(inner, width)
    right_im = right_im.reshape(inner, width)
    real_left = jnp.concatenate([left_re, -left_im], axis=1)
    imag_left = jnp.concatenate([left_re, left_im], axis=1)
    real_right = jnp.concatenate([right_re, right_im], axis=0)
    imag_right = jnp.concatenate([right_im, right_re], axis=0)
    return real_left, imag_left, real_right, imag_right


def project_rows(factor_set, start, count):
    real_left, imag_left, real_right, imag_right = factor_set
    highest = lax.Precision.HIGHEST
    pieces = []
    for kind in range(2):
        real_slice = lax.dynamic_slice_in_dim(real_left[kind], start, count, 1)
        imag_slice = lax.dynamic_slice_in_dim(imag_left[kind], start, count, 1)
        pieces.append(jnp.einsum('kr,kw->rw', real_slice, real_right, precision=highest))
        pieces.append(jnp.einsum('kr,kw->rw', imag_slice, imag_right, precision=highest))
    return jnp.concatenate(pieces, axis=1)


def narrow(matrix):
    return matrix.astype(jnp.bfloat16)


def complex_product(left, right):
    left_half = narrow(left)
    right_half = narrow(right)
    real_part = jnp.dot(left_half[0], right_half[0], preferred_element_type=jnp.float32) - jnp.dot(left_half[1], right_half[1], preferred_element_type=jnp.float32)
    imag_part = jnp.dot(left_half[0], right_half[1], preferred_element_type=jnp.float32) + jnp.dot(left_half[1], right_half[0], preferred_element_type=jnp.float32)
    return jnp.stack([real_part, imag_part])


def star(upper, lower):
    refl_a, trans_a, refl_a_back, trans_a_back = upper
    refl_b, trans_b, refl_b_back, trans_b_back = lower
    first_mix = complex_product(refl_a_back, refl_b)
    down_chain = trans_a + complex_product(first_mix, trans_a)
    bounce = complex_product(refl_b, down_chain)
    trans_new = complex_product(trans_b, down_chain)
    refl_new = refl_a + complex_product(trans_a_back, bounce)
    second_mix = complex_product(refl_b, refl_a_back)
    up_chain = trans_b_back + complex_product(second_mix, trans_b_back)
    back_bounce = complex_product(refl_a_back, up_chain)
    trans_back_new = complex_product(trans_a_back, up_chain)
    refl_back_new = refl_b_back + complex_product(trans_b, back_bounce)
    return (refl_new, trans_new, refl_back_new, trans_back_new)


def reference(out_basis, in_basis, tmatrix, sites, waves, layer_phase):
    width = 2 * WAVES
    identity = (jnp.arange(width)[:, None] == jnp.arange(width)[None, :]).astype(jnp.float32)
    stacks = []
    for layer in range(LAYERS):
        angles = wave_angles(sites[layer], waves)
        factor_set = factors(out_basis[layer], in_basis[layer], tmatrix[layer], angles)
        summed = project_rows(factor_set, 0, width)
        refl = jnp.stack([summed[:, :width], summed[:, width:2 * width]])
        trans_re = summed[:, 2 * width:3 * width] + identity * jnp.cos(layer_phase[layer])[None, :]
        trans_im = summed[:, 3 * width:] + identity * jnp.sin(layer_phase[layer])[None, :]
        trans = jnp.stack([trans_re, trans_im])
        stacks.append((refl, trans, refl, trans))
    while len(stacks) > 1:
        stacks = [star(stacks[2 * index], stacks[2 * index + 1]) for index in range(len(stacks) // 2)]
    return stacks[0][0], stacks[0][1]
```

```python
import functools
import math

import jax
import jax.numpy as jnp
from jax import lax
from jax.experimental import pallas as pl
from jax.experimental.pallas import tpu as pltpu
from jax.sharding import PartitionSpec as P

LATTICE = 32
TWO_PI = 2.0 * math.pi
F32 = jnp.float32
BF16 = jnp.bfloat16
VMEM = pl.BlockSpec(memory_space=pltpu.VMEM)
ANY = pl.BlockSpec(memory_space=pl.ANY)
SMEM = pl.BlockSpec(memory_space=pltpu.SMEM)
EXTRA = 16


def partner_2(value, axis, bit):
    mask = 2**bit
    pairs = [(source, source ^ mask) for source in range(lax.axis_size(axis))]
    return lax.ppermute(value, axis, pairs)


def wave_angles(site_list, waves):
    column = site_list // LATTICE
    along = site_list % LATTICE
    phase_index = (
        waves[0][None, :] * column[:, None] + waves[1][None, :] * along[:, None]
    ) % LATTICE
    angles = phase_index.astype(jnp.float32) * (TWO_PI / LATTICE)
    return jnp.concatenate([angles, angles], axis=1)


def factors(out_layer, in_layer, tm_layer, angles):
    highest = lax.Precision.HIGHEST
    basis_re = out_layer[:, 0]
    basis_im = out_layer[:, 1]
    tmat_re = tm_layer[:, 0]
    tmat_im = tm_layer[:, 1]
    prod_re = jnp.einsum("kjw,sjm->ksmw", basis_re, tmat_re, precision=highest) - jnp.einsum(
        "kjw,sjm->ksmw", basis_im, tmat_im, precision=highest
    )
    prod_im = jnp.einsum("kjw,sjm->ksmw", basis_re, tmat_im, precision=highest) + jnp.einsum(
        "kjw,sjm->ksmw", basis_im, tmat_re, precision=highest
    )
    cosine = jnp.cos(angles)
    sine = jnp.sin(angles)
    left_re = prod_re * cosine[None, :, None, :] - prod_im * sine[None, :, None, :]
    left_im = prod_re * sine[None, :, None, :] + prod_im * cosine[None, :, None, :]
    right_re = in_layer[0][None] * cosine[:, None, :] + in_layer[1][None] * sine[:, None, :]
    right_im = in_layer[1][None] * cosine[:, None, :] - in_layer[0][None] * sine[:, None, :]
    inner = left_re.shape[1] * left_re.shape[2]
    width = left_re.shape[3]
    left_re = left_re.reshape(2, inner, width)
    left_im = left_im.reshape(2, inner, width)
    right_re = right_re.reshape(inner, width)
    right_im = right_im.reshape(inner, width)
    real_left = jnp.concatenate([left_re, -left_im], axis=1)
    imag_left = jnp.concatenate([left_re, left_im], axis=1)
    real_right = jnp.concatenate([right_re, right_im], axis=0)
    imag_right = jnp.concatenate([right_im, right_re], axis=0)
    return (real_left, imag_left, real_right, imag_right)


def project_rows(factor_set):
    real_left, imag_left, real_right, imag_right = factor_set
    highest = lax.Precision.HIGHEST
    pieces = []
    for kind in range(2):
        real_slice = real_left[kind]
        imag_slice = imag_left[kind]
        pieces.append(jnp.einsum("kr,kw->rw", real_slice, real_right, precision=highest))
        pieces.append(jnp.einsum("kr,kw->rw", imag_slice, imag_right, precision=highest))
    return jnp.concatenate(pieces, axis=1)


def narrow(matrix):
    return matrix.astype(jnp.bfloat16)


def complex_product(left, right):
    left_half = narrow(left)
    right_half = narrow(right)
    real_part = jnp.dot(left_half[0], right_half[0], preferred_element_type=jnp.float32) - jnp.dot(
        left_half[1], right_half[1], preferred_element_type=jnp.float32
    )
    imag_part = jnp.dot(left_half[0], right_half[1], preferred_element_type=jnp.float32) + jnp.dot(
        left_half[1], right_half[0], preferred_element_type=jnp.float32
    )
    return jnp.stack([real_part, imag_part])


def merge_level(state, bit):
    partner = partner_2(state.astype(jnp.bfloat16), "layer", bit).astype(state.dtype)
    is_upper = lax.axis_index("layer") // (1 << bit) % 2 == 0
    upper = jnp.where(is_upper, state, partner)
    lower = jnp.where(is_upper, partner, state)
    refl_a, trans_a, refl_a_back, trans_a_back = (upper[0], upper[1], upper[2], upper[3])
    refl_b, trans_b, refl_b_back, trans_b_back = (lower[0], lower[1], lower[2], lower[3])
    first_left = jnp.where(is_upper, refl_a_back, refl_b)
    first_right = jnp.where(is_upper, refl_b, refl_a_back)
    chain_base = jnp.where(is_upper, trans_a, trans_b_back)
    across = jnp.where(is_upper, trans_b, trans_a_back)
    final_left = jnp.where(is_upper, trans_a_back, trans_b)
    addend = jnp.where(is_upper, refl_a, refl_b_back)
    full_right, full_base = (
        lax.all_gather(narrow(first_right), "sph", axis=1, tiled=True),
        lax.all_gather(narrow(chain_base), "sph", axis=1, tiled=True),
    )
    first_mix = complex_product(first_left, full_right)
    chain = chain_base + complex_product(first_mix, full_base)
    full_chain = lax.all_gather(narrow(chain), "sph", axis=1, tiled=True)
    bounce = complex_product(first_right, full_chain)
    own_trans = complex_product(across, full_chain)
    full_bounce = lax.all_gather(narrow(bounce), "sph", axis=1, tiled=True)
    own_refl = addend + complex_product(final_left, full_bounce)
    mine = jnp.stack([own_trans, own_refl])
    theirs = partner_2(mine.astype(jnp.bfloat16), "layer", bit).astype(mine.dtype)
    trans_new = jnp.where(is_upper, mine[0], theirs[0])
    refl_new = jnp.where(is_upper, mine[1], theirs[1])
    trans_back_new = jnp.where(is_upper, theirs[0], mine[0])
    refl_back_new = jnp.where(is_upper, theirs[1], mine[1])
    return jnp.stack([refl_new, trans_new, refl_back_new, trans_back_new])


def by_rows(out_basis, in_basis, tmatrix, sites, waves, layer_phase):
    width = 2 * waves.shape[1]
    rows = width // lax.axis_size("sph")
    angles = wave_angles(sites[0], waves)
    factor_set = factors(out_basis[0], in_basis[0], tmatrix[0], angles)
    summed = lax.psum_scatter(
        project_rows(factor_set).astype(jnp.bfloat16), "sph", scatter_dimension=0, tiled=True
    ).astype(jnp.float32)
    first_row = lax.axis_index("sph") * rows
    diagonal = ((first_row + jnp.arange(rows))[:, None] == jnp.arange(width)[None, :]).astype(
        jnp.float32
    )
    refl = jnp.stack([summed[:, :width], summed[:, width : 2 * width]])
    trans_re = summed[:, 2 * width : 3 * width] + diagonal * jnp.cos(layer_phase[0])[None, :]
    trans_im = summed[:, 3 * width :] + diagonal * jnp.sin(layer_phase[0])[None, :]
    trans = jnp.stack([trans_re, trans_im])
    state = jnp.stack([refl, trans, refl, trans])
    levels = lax.axis_size("layer").bit_length() - 1
    for bit in range(levels):
        state = merge_level(state, bit)
    columns = width // lax.axis_size("layer")
    first_column = lax.axis_index("layer") * columns
    own_refl = lax.dynamic_slice_in_dim(state[0], first_column, columns, 2)
    own_trans = lax.dynamic_slice_in_dim(state[1], first_column, columns, 2)
    return (own_refl, own_trans)


def mm(left, right):
    return jnp.dot(left, right, preferred_element_type=F32)


def mm_t(left, right):
    return lax.dot_general(left, right, (((0,), (0,)), ((), ())), preferred_element_type=F32)


def cmul(left, right):
    return (
        mm(left[0], right[0]) - mm(left[1], right[1]),
        mm(left[0], right[1]) + mm(left[1], right[0]),
    )


def half(pair):
    return (pair[0].astype(BF16), pair[1].astype(BF16))


def add(one, two):
    return (one[0] + two[0], one[1] + two[1])


def layer_kernel(count, spheres, multi, last, *refs):
    blocks = refs[:count]
    rest = list(refs[count:])
    out_tile, in_pair, wave_col = rest[:3]
    rest = rest[3:]
    if last:
        prev, phase_col, phase_row = rest[:3]
        rest = rest[3:]
    out = rest[0]
    rest = rest[1:]
    sum_1, sum_2, sum_3, cosine, sine, cos_t, sin_t = rest[:7]
    left_slots = (rest[7:10], rest[10:13])
    right_slots = (rest[13:16], rest[16:19])
    cos_e, sin_e = rest[19:21]
    depth = spheres * multi
    half_width = wave_col.shape[0]
    width = 2 * half_width
    lanes = cosine.shape[1]

    coords = None
    for index, block in enumerate(blocks):
        row = lax.broadcasted_iota(jnp.int32, (depth, lanes), 0)
        lane = lax.broadcasted_iota(jnp.int32, (depth, lanes), 1)
        pick = (row == (lane - spheres * index) * multi).astype(F32).astype(BF16)
        part = mm(block[2 * multi : 2 * multi + EXTRA, :], pick)
        coords = part if coords is None else coords + part
    turns = wave_col[:, 0:1] * coords[0:1, :] + wave_col[:, 1:2] * coords[1:2, :]
    turns = turns - LATTICE * jnp.floor(turns * (1.0 / LATTICE))
    angle = turns * (TWO_PI / LATTICE)
    cos_v = jnp.cos(angle)
    sin_v = jnp.sin(angle)
    cosine[...] = cos_v.astype(BF16)
    sine[...] = sin_v.astype(BF16)
    cos_t[...] = cos_v.T.astype(BF16)
    sin_t[...] = sin_v.T.astype(BF16)

    def spread(index):
        row = lax.broadcasted_iota(jnp.int32, (lanes, depth), 0) - spheres * index
        lane = lax.broadcasted_iota(jnp.int32, (lanes, depth), 1)
        inside = (lane >= row * multi) & (lane < row * multi + multi)
        pick = inside.astype(F32).astype(BF16)
        cos_e[...] = mm(cosine[...], pick)
        sin_e[...] = mm(sine[...], pick)

    def build_left(slot, part):
        kind, pol = part // 2, part % 2
        rows = pl.ds(pol * half_width, half_width)
        to = pl.ds(part * half_width, half_width)
        u_re = out_tile[kind, 0, rows, :].astype(F32)
        u_im = out_tile[kind, 1, rows, :].astype(F32)
        c, s = cos_e[...], sin_e[...]
        re = u_re * c - u_im * s
        im = u_re * s + u_im * c
        slot[0][to, :] = re.astype(BF16)
        slot[1][to, :] = im.astype(BF16)
        slot[2][to, :] = (re + im).astype(BF16)

    def build_right(slot, index, part, size):
        at = part * size
        row = lax.broadcasted_iota(jnp.int32, (size, lanes), 0) + at
        lane = lax.broadcasted_iota(jnp.int32, (size, lanes), 1) - spheres * index
        inside = (row >= lane * multi) & (row < lane * multi + multi)
        pick = inside.astype(F32).astype(BF16)
        c = mm(pick, cos_t[...])
        s = mm(pick, sin_t[...])
        both = mm_t(blocks[index][0 : 2 * multi, at : at + size], in_pair[...])
        for pol in range(2):
            lo = pol * half_width
            g_re = both[:, lo : lo + half_width]
            g_im = both[:, width + lo : width + lo + half_width]
            re = g_re * c + g_im * s
            im = g_im * c - g_re * s
            slot[0][at : at + size, lo : lo + half_width] = re.astype(BF16)
            slot[1][at : at + size, lo : lo + half_width] = im.astype(BF16)
            slot[2][at : at + size, lo : lo + half_width] = (re + im).astype(BF16)

    size = 256
    rights = depth // size

    spread(0)
    for part in range(4):
        build_left(left_slots[0], part)
    for part in range(rights):
        build_right(right_slots[0], 0, part, size)
    for index in range(count):
        now, later = index % 2, (index + 1) % 2
        if index + 1 < count:
            spread(index + 1)
        for part in range(4):
            rows = pl.ds(part * half_width, half_width)
            for total, left, right in zip(
                (sum_1, sum_2, sum_3), left_slots[now], right_slots[now]
            ):
                product = mm(left[rows, :], right[...])
                if index == 0:
                    total[rows, :] = product
                else:
                    total[rows, :] += product
            if index + 1 < count:
                build_left(left_slots[later], part)
                if part < rights:
                    build_right(right_slots[later], index + 1, part, size)

    for part in range(4):
        kind, pol = part // 2, part % 2
        rows = pl.ds(part * half_width, half_width)
        re = sum_1[rows, :] - sum_2[rows, :]
        im = sum_3[rows, :] - sum_1[rows, :] - sum_2[rows, :]
        if not last:
            out[0, rows, :] = re
            out[1, rows, :] = im
        else:
            re = re + prev[0, rows, :]
            im = im + prev[1, rows, :]
            if kind == 1:
                at = lax.broadcasted_iota(jnp.int32, (half_width, width), 0) + pol * half_width
                lane = lax.broadcasted_iota(jnp.int32, (half_width, width), 1)
                on = at == lane
                re = re + jnp.where(on, jnp.cos(phase_row[...]), 0.0)
                im = im + jnp.where(on, jnp.sin(phase_row[...]), 0.0)
            to = pl.ds(pol * half_width, half_width)
            out[2 * kind, to, :] = re.astype(BF16)
            out[2 * kind + 1, to, :] = im.astype(BF16)


def layer_sum(blocks, spheres, multi, out_tile, in_pair, wave_col, prev=None, phase=None):
    count = len(blocks)
    last = prev is not None
    depth = spheres * multi
    half_width = wave_col.shape[0]
    width = 2 * half_width
    lanes = max(128, count * spheres)
    operands = list(blocks) + [out_tile, in_pair, wave_col]
    if last:
        operands += [prev, phase.reshape(-1, 1), phase.reshape(1, -1)]
        shape = jax.ShapeDtypeStruct((4, width, width), BF16)
    else:
        shape = jax.ShapeDtypeStruct((2, 2 * width, width), F32)
    scratch = [pltpu.VMEM((2 * width, width), F32)] * 3
    scratch += [pltpu.VMEM((half_width, lanes), BF16)] * 2
    scratch += [pltpu.VMEM((lanes, half_width), BF16)] * 2
    scratch += [pltpu.VMEM((2 * width, depth), BF16)] * 6
    scratch += [pltpu.VMEM((depth, width), BF16)] * 6
    scratch += [pltpu.VMEM((half_width, depth), F32)] * 2
    flops = count * 3 * 2 * 2 * width * width * depth
    return pl.pallas_call(
        functools.partial(layer_kernel, count, spheres, multi, last),
        out_shape=shape,
        in_specs=[VMEM] * len(operands),
        out_specs=VMEM,
        scratch_shapes=scratch,
        compiler_params=pltpu.CompilerParams(vmem_limit_bytes=56 * 2**20),
        cost_estimate=pl.CostEstimate(flops=flops, bytes_accessed=2**23, transcendentals=0),
        name="layer_sum",
    )(*operands)


def form_kernel(rows, place, own, other, s_out, h_out, k_out, u, v):
    width = own.shape[1]
    quarter = width // 4
    mine_is_u = place[0]
    core = place[1]
    first_row = pl.multiple_of(place[2] * rows, rows)

    @pl.when(mine_is_u == 1)
    def _():
        u[...] = own[...]
        v[...] = other[...]

    @pl.when(mine_is_u == 0)
    def _():
        u[...] = other[...]
        v[...] = own[...]

    r_u, t_u = (u[0], u[1]), (u[2], u[3])
    r_v, t_v = (v[0], v[1]), (v[2], v[3])

    near = pl.ds(pl.multiple_of(core * quarter, quarter), quarter)
    far = pl.ds(pl.multiple_of((core + 2) * quarter, quarter), quarter)

    def columns(ref, at):
        return jnp.concatenate([ref[at, :, near], ref[at, :, far]], axis=1)

    base = (columns(v, 2), columns(v, 3))
    chain = cmul(r_u, base)
    chain = cmul(r_v, half(chain))
    chain = half((base[0] + chain[0], base[1] + chain[1]))
    here = cmul(t_u, chain)
    my = pl.ds(first_row, rows)
    row_t = (v[2, my, :], v[3, my, :])
    w_1 = half(cmul(row_t, r_u))
    k_part = cmul(w_1, chain)
    for side in range(2):
        at = slice(side * quarter, (side + 1) * quarter)
        cols = near if side == 0 else far
        for c in range(2):
            h_out[side, c] = here[c][:, at].astype(BF16)
            k_out[side, c] = (v[c, my, cols].astype(F32) + k_part[c][:, at]).astype(BF16)

    w_2 = cmul(w_1, r_v)
    w_2 = half((row_t[0] + w_2[0], row_t[1] + w_2[1]))
    g_rows = half(cmul(w_2, t_u))

    mine = pl.ds(pl.multiple_of(core * 2 * quarter, 2 * quarter), 2 * quarter)
    base = (u[2, :, mine], u[3, :, mine])
    up = cmul(r_v, base)
    again = cmul(r_u, half(up))
    again = cmul(r_v, half(again))
    up = half(add(up, again))
    back = cmul(t_u, up)
    for c in range(2):
        s_out[c, 0:width, :] = (u[c, :, mine].astype(F32) + back[c]).astype(BF16)
        s_out[c, width : width + rows, :] = g_rows[c][:, 0 : 2 * quarter]
        s_out[c, width + rows : width + 2 * rows, :] = g_rows[c][:, 2 * quarter :]


def form(place, own, other, rows):
    width = own.shape[1]
    return pl.pallas_call(
        functools.partial(form_kernel, rows),
        out_shape=(
            jax.ShapeDtypeStruct((2, width + 2 * rows, width // 2), BF16),
            jax.ShapeDtypeStruct((2, 2, width, width // 4), BF16),
            jax.ShapeDtypeStruct((2, 2, rows, width // 4), BF16),
        ),
        in_specs=[SMEM, VMEM, VMEM],
        out_specs=(VMEM, VMEM, VMEM),
        scratch_shapes=[pltpu.VMEM(own.shape, BF16)] * 2,
        compiler_params=pltpu.CompilerParams(vmem_limit_bytes=56 * 2**20),
        cost_estimate=pl.CostEstimate(flops=2**32, bytes_accessed=2**23, transcendentals=0),
        name="form",
    )(place, own, other)


def join_kernel(rows, place, s_mine, s_side, s_far, s_far_side, h, k, refl, trans, sides):
    width = h.shape[1]
    lower = place[0]
    core = place[1]
    sides[lower, core] = s_mine[...]
    sides[lower, 1 - core] = s_side[...]
    sides[1 - lower, core] = s_far[...]
    sides[1 - lower, 1 - core] = s_far_side[...]

    def rows_of(side):
        return tuple(
            jnp.concatenate(
                [
                    sides[side, 0, c, width : width + rows, :],
                    sides[side, 0, c, width + rows : width + 2 * rows, :],
                ],
                axis=1,
            )
            for c in range(2)
        )

    def times(pair, side):
        parts = [
            cmul(pair, (sides[side, h_, 0, 0:width, :], sides[side, h_, 1, 0:width, :]))
            for h_ in range(2)
        ]
        return tuple(jnp.concatenate([parts[0][c], parts[1][c]], axis=1) for c in range(2))

    from_above = rows_of(0)
    from_below = rows_of(1)
    second = half(times(from_above, 1))
    both = tuple(jnp.concatenate([from_below[c], second[c]], axis=0) for c in range(2))
    chain = times(half(times(both, 0)), 1)
    chain = half(tuple(both[c].astype(F32) + chain[c] for c in range(2)))
    result = cmul(chain, (h[0], h[1]))
    for c in range(2):
        trans[c] = result[c][0:rows]
        refl[c] = k[c].astype(F32) + result[c][rows : 2 * rows]


def join(place, s_mine, s_side, s_far, s_far_side, h, k, rows):
    columns = h.shape[2]
    shape = jax.ShapeDtypeStruct((2, rows, columns), F32)
    return pl.pallas_call(
        functools.partial(join_kernel, rows),
        out_shape=(shape, shape),
        in_specs=[SMEM] + [VMEM] * 6,
        out_specs=(VMEM, VMEM),
        scratch_shapes=[pltpu.VMEM((2, 2) + s_mine.shape, BF16)],
        compiler_params=pltpu.CompilerParams(vmem_limit_bytes=56 * 2**20),
        cost_estimate=pl.CostEstimate(flops=2**30, bytes_accessed=2**22, transcendentals=0),
        name="join",
    )(place, s_mine, s_side, s_far, s_far_side, h, k)


def whole_layers(inner, out_basis, in_basis, tmatrix, sites, waves, layer_phase):
    spheres, multi = tmatrix.shape[1], tmatrix.shape[3]
    half_width = waves.shape[1]
    width = 2 * half_width
    groups = lax.axis_size("sph")
    outer = groups // inner
    rows = width // groups
    layer = lax.axis_index("layer")

    depth = spheres * multi
    block = tmatrix[0].astype(BF16).transpose(1, 3, 0, 2).reshape(2 * multi, depth)
    coords = jnp.stack([sites[0] // LATTICE, sites[0] % LATTICE]).astype(BF16)
    coords = jnp.broadcast_to(coords[:, :, None], (2, spheres, multi)).reshape(2, depth)
    block = jnp.concatenate([block, coords, jnp.zeros((EXTRA - 2, depth), BF16)], axis=0)

    def shifted(value, far, side):
        pairs = [
            (g, ((g // inner + far) % outer) * inner + (g % inner + side) % inner)
            for g in range(groups)
        ]
        return lax.ppermute(value, "sph", pairs)

    order = sorted(
        ((far, side) for far in range(outer) for side in range(inner)),
        key=lambda at: (min(at[0], outer - at[0]) * 2 + at[1]),
    )
    blocks = [block if at == (0, 0) else shifted(block, *at) for at in order]

    turned = out_basis[0].astype(BF16).transpose(0, 1, 3, 2)
    out_tile = jnp.tile(turned, (1, 1, 1, spheres))
    b_re, b_im = in_basis[0, 0], in_basis[0, 1]
    in_pair = jnp.concatenate(
        [jnp.concatenate([b_re, b_im], axis=1), jnp.concatenate([-b_im, b_re], axis=1)], axis=0
    ).astype(BF16)
    wave_col = waves.astype(F32).T
    first = groups // 2
    part = layer_sum(blocks[:first], spheres, multi, out_tile, in_pair, wave_col)
    own = layer_sum(
        blocks[first:], spheres, multi, out_tile, in_pair, wave_col, part, layer_phase[0]
    )

    other = lax.ppermute(own, "layer", [(at, at ^ 1) for at in range(4)])
    core, lower = layer % 2, layer // 2
    mine_is_u = jnp.where(core != lower, 1, 0)
    place = jnp.stack([mine_is_u, core, lax.axis_index("sph")]).astype(jnp.int32)
    s_mine, h_both, k_both = form(place, own, other, rows)
    h_sent = lax.ppermute(h_both[1], "layer", [(0, 2), (1, 3)])
    k_sent = lax.ppermute(k_both[1], "layer", [(0, 2), (1, 3)])
    s_far = lax.ppermute(s_mine, "layer", [(at, at ^ 2) for at in range(4)])
    s_side = lax.ppermute(s_mine, "layer", [(at, at ^ 1) for at in range(4)])
    s_far_side = lax.ppermute(s_far, "layer", [(at, at ^ 1) for at in range(4)])
    h = jnp.where(lower == 0, h_both[0], h_sent)
    k = jnp.where(lower == 0, k_both[0], k_sent)
    place = jnp.stack([lower, core]).astype(jnp.int32)
    return join(place, s_mine, s_side, s_far, s_far_side, h, k, rows)


def solution(mesh):
    in_specs = (
        P("layer", None, None, None, None),
        P("layer", None, None, None),
        P("layer", "sph", None, None, None),
        P("layer", "sph"),
        P(),
        P("layer", None),
    )
    out_specs = (P(None, "sph", "layer"), P(None, "sph", "layer"))
    on_device = by_rows
    if mesh.shape["layer"] == 4 and mesh.shape["sph"] == 8:
        on_device = functools.partial(whole_layers, 2)
    return jax.shard_map(
        on_device, mesh=mesh, in_specs=in_specs, out_specs=out_specs, check_vma=False
    )
```

```python
import functools
import math

import jax
import jax.numpy as jnp
from jax import lax
from jax.experimental import pallas as pl
from jax.experimental.pallas import tpu as pltpu
from jax.sharding import PartitionSpec as P

LATTICE = 32
TWO_PI = 2.0 * math.pi
F32 = jnp.float32
BF16 = jnp.bfloat16
VMEM = pl.BlockSpec(memory_space=pltpu.VMEM)
ANY = pl.BlockSpec(memory_space=pl.ANY)
SMEM = pl.BlockSpec(memory_space=pltpu.SMEM)
EXTRA = 16


def partner_2(value, axis, bit):
    mask = 2**bit
    pairs = [(source, source ^ mask) for source in range(lax.axis_size(axis))]
    return lax.ppermute(value, axis, pairs)


def wave_angles(site_list, waves):
    column = site_list // LATTICE
    along = site_list % LATTICE
    phase_index = (
        waves[0][None, :] * column[:, None] + waves[1][None, :] * along[:, None]
    ) % LATTICE
    angles = phase_index.astype(jnp.float32) * (TWO_PI / LATTICE)
    return jnp.concatenate([angles, angles], axis=1)


def factors(out_layer, in_layer, tm_layer, angles):
    highest = lax.Precision.HIGHEST
    basis_re = out_layer[:, 0]
    basis_im = out_layer[:, 1]
    tmat_re = tm_layer[:, 0]
    tmat_im = tm_layer[:, 1]
    prod_re = jnp.einsum("kjw,sjm->ksmw", basis_re, tmat_re, precision=highest) - jnp.einsum(
        "kjw,sjm->ksmw", basis_im, tmat_im, precision=highest
    )
    prod_im = jnp.einsum("kjw,sjm->ksmw", basis_re, tmat_im, precision=highest) + jnp.einsum(
        "kjw,sjm->ksmw", basis_im, tmat_re, precision=highest
    )
    cosine = jnp.cos(angles)
    sine = jnp.sin(angles)
    left_re = prod_re * cosine[None, :, None, :] - prod_im * sine[None, :, None, :]
    left_im = prod_re * sine[None, :, None, :] + prod_im * cosine[None, :, None, :]
    right_re = in_layer[0][None] * cosine[:, None, :] + in_layer[1][None] * sine[:, None, :]
    right_im = in_layer[1][None] * cosine[:, None, :] - in_layer[0][None] * sine[:, None, :]
    inner = left_re.shape[1] * left_re.shape[2]
    width = left_re.shape[3]
    left_re = left_re.reshape(2, inner, width)
    left_im = left_im.reshape(2, inner, width)
    right_re = right_re.reshape(inner, width)
    right_im = right_im.reshape(inner, width)
    real_left = jnp.concatenate([left_re, -left_im], axis=1)
    imag_left = jnp.concatenate([left_re, left_im], axis=1)
    real_right = jnp.concatenate([right_re, right_im], axis=0)
    imag_right = jnp.concatenate([right_im, right_re], axis=0)
    return (real_left, imag_left, real_right, imag_right)


def project_rows(factor_set):
    real_left, imag_left, real_right, imag_right = factor_set
    highest = lax.Precision.HIGHEST
    pieces = []
    for kind in range(2):
        real_slice = real_left[kind]
        imag_slice = imag_left[kind]
        pieces.append(jnp.einsum("kr,kw->rw", real_slice, real_right, precision=highest))
        pieces.append(jnp.einsum("kr,kw->rw", imag_slice, imag_right, precision=highest))
    return jnp.concatenate(pieces, axis=1)


def narrow(matrix):
    return matrix.astype(jnp.bfloat16)


def complex_product(left, right):
    left_half = narrow(left)
    right_half = narrow(right)
    real_part = jnp.dot(left_half[0], right_half[0], preferred_element_type=jnp.float32) - jnp.dot(
        left_half[1], right_half[1], preferred_element_type=jnp.float32
    )
    imag_part = jnp.dot(left_half[0], right_half[1], preferred_element_type=jnp.float32) + jnp.dot(
        left_half[1], right_half[0], preferred_element_type=jnp.float32
    )
    return jnp.stack([real_part, imag_part])


def merge_level(state, bit):
    partner = partner_2(state.astype(jnp.bfloat16), "layer", bit).astype(state.dtype)
    is_upper = lax.axis_index("layer") // (1 << bit) % 2 == 0
    upper = jnp.where(is_upper, state, partner)
    lower = jnp.where(is_upper, partner, state)
    refl_a, trans_a, refl_a_back, trans_a_back = (upper[0], upper[1], upper[2], upper[3])
    refl_b, trans_b, refl_b_back, trans_b_back = (lower[0], lower[1], lower[2], lower[3])
    first_left = jnp.where(is_upper, refl_a_back, refl_b)
    first_right = jnp.where(is_upper, refl_b, refl_a_back)
    chain_base = jnp.where(is_upper, trans_a, trans_b_back)
    across = jnp.where(is_upper, trans_b, trans_a_back)
    final_left = jnp.where(is_upper, trans_a_back, trans_b)
    addend = jnp.where(is_upper, refl_a, refl_b_back)
    full_right, full_base = (
        lax.all_gather(narrow(first_right), "sph", axis=1, tiled=True),
        lax.all_gather(narrow(chain_base), "sph", axis=1, tiled=True),
    )
    first_mix = complex_product(first_left, full_right)
    chain = chain_base + complex_product(first_mix, full_base)
    full_chain = lax.all_gather(narrow(chain), "sph", axis=1, tiled=True)
    bounce = complex_product(first_right, full_chain)
    own_trans = complex_product(across, full_chain)
    full_bounce = lax.all_gather(narrow(bounce), "sph", axis=1, tiled=True)
    own_refl = addend + complex_product(final_left, full_bounce)
    mine = jnp.stack([own_trans, own_refl])
    theirs = partner_2(mine.astype(jnp.bfloat16), "layer", bit).astype(mine.dtype)
    trans_new = jnp.where(is_upper, mine[0], theirs[0])
    refl_new = jnp.where(is_upper, mine[1], theirs[1])
    trans_back_new = jnp.where(is_upper, theirs[0], mine[0])
    refl_back_new = jnp.where(is_upper, theirs[1], mine[1])
    return jnp.stack([refl_new, trans_new, refl_back_new, trans_back_new])


def by_rows(out_basis, in_basis, tmatrix, sites, waves, layer_phase):
    width = 2 * waves.shape[1]
    rows = width // lax.axis_size("sph")
    angles = wave_angles(sites[0], waves)
    factor_set = factors(out_basis[0], in_basis[0], tmatrix[0], angles)
    summed = lax.psum_scatter(
        project_rows(factor_set).astype(jnp.bfloat16), "sph", scatter_dimension=0, tiled=True
    ).astype(jnp.float32)
    first_row = lax.axis_index("sph") * rows
    diagonal = ((first_row + jnp.arange(rows))[:, None] == jnp.arange(width)[None, :]).astype(
        jnp.float32
    )
    refl = jnp.stack([summed[:, :width], summed[:, width : 2 * width]])
    trans_re = summed[:, 2 * width : 3 * width] + diagonal * jnp.cos(layer_phase[0])[None, :]
    trans_im = summed[:, 3 * width :] + diagonal * jnp.sin(layer_phase[0])[None, :]
    trans = jnp.stack([trans_re, trans_im])
    state = jnp.stack([refl, trans, refl, trans])
    levels = lax.axis_size("layer").bit_length() - 1
    for bit in range(levels):
        state = merge_level(state, bit)
    columns = width // lax.axis_size("layer")
    first_column = lax.axis_index("layer") * columns
    own_refl = lax.dynamic_slice_in_dim(state[0], first_column, columns, 2)
    own_trans = lax.dynamic_slice_in_dim(state[1], first_column, columns, 2)
    return (own_refl, own_trans)


def mm(left, right):
    return jnp.dot(left, right, preferred_element_type=F32)


def mm_t(left, right):
    return lax.dot_general(left, right, (((0,), (0,)), ((), ())), preferred_element_type=F32)


def cmul(left, right):
    return (
        mm(left[0], right[0]) - mm(left[1], right[1]),
        mm(left[0], right[1]) + mm(left[1], right[0]),
    )


def half(pair):
    return (pair[0].astype(BF16), pair[1].astype(BF16))


def add(one, two):
    return (one[0] + two[0], one[1] + two[1])


def circle(turns):
    turn = turns * (1.0 / LATTICE)
    turn = turn - jnp.floor(turn)
    quarter = jnp.floor(turn * 4.0 + 0.5)
    x = (turn - quarter * 0.25) * TWO_PI
    y = x * x
    sin = x * (1.0 + y * (-1.0 / 6 + y * (1.0 / 120 + y * (-1.0 / 5040 + y * (1.0 / 362880)))))
    cos = 1.0 + y * (-0.5 + y * (1.0 / 24 + y * (-1.0 / 720 + y * (1.0 / 40320))))
    odd = (quarter == 1.0) | (quarter == 3.0)
    cos, sin = jnp.where(odd, sin, cos), jnp.where(odd, cos, sin)
    cos = jnp.where((quarter == 1.0) | (quarter == 2.0), -cos, cos)
    sin = jnp.where((quarter == 2.0) | (quarter == 3.0), -sin, sin)
    return cos, sin


def layer_kernel(count, spheres, multi, last, *refs):
    sent = refs[:count]
    rest = list(refs[count:])
    tile_hbm, in_pair, wave_col = rest[:3]
    rest = rest[3:]
    if last:
        prev_hbm, phase_row = rest[:2]
        rest = rest[2:]
    out = rest[0]
    rest = rest[1:]
    sum_1, sum_2, sum_3, cos_t, sin_t = rest[:5]
    left_slots = (rest[5:8], rest[8:11])
    right_slots = (rest[11:14], rest[14:17])
    spread_slots = (rest[17:19], rest[19:21])
    out_tile, tile_here, cos_s, sin_s, blocks_here, block_sem = rest[21:27]
    blocks = [blocks_here.at[index] for index in range(count)]
    copies = [
        pltpu.make_async_copy(sent[index], blocks_here.at[index], block_sem.at[index])
        for index in range(count)
    ]
    for copy in copies:
        copy.start()
    tile_copy = pltpu.make_async_copy(tile_hbm, out_tile, tile_here)
    tile_copy.start()
    if last:
        prev, arrived = rest[27:]
        fetch = pltpu.make_async_copy(prev_hbm, prev, arrived)
        fetch.start()
    depth = spheres * multi
    half_width = wave_col.shape[0]
    width = 2 * half_width
    lanes = cos_t.shape[0]
    parts = 2
    tall = 2 * width // parts
    few, size = spheres // parts, depth // parts

    for copy in copies:
        copy.wait()
    coords = None
    for index, block in enumerate(blocks):
        row = lax.broadcasted_iota(jnp.int32, (depth, lanes), 0)
        lane = lax.broadcasted_iota(jnp.int32, (depth, lanes), 1)
        pick = (row == (lane - spheres * index) * multi).astype(F32).astype(BF16)
        part = mm(block[2 * multi : 2 * multi + EXTRA, :], pick)
        coords = part if coords is None else coords + part
    turns = wave_col[:, 0:1] * coords[0:1, :] + wave_col[:, 1:2] * coords[1:2, :]
    cos_v, sin_v = circle(turns)
    for index in range(count):
        at = slice(spheres * index, spheres * (index + 1))
        cos_s[index] = cos_v[:, at].astype(BF16)
        sin_s[index] = sin_v[:, at].astype(BF16)
    cos_t[...] = cos_v.T
    sin_t[...] = sin_v.T
    row = lax.broadcasted_iota(jnp.int32, (spheres, depth), 0)
    lane = lax.broadcasted_iota(jnp.int32, (spheres, depth), 1)
    inside = (lane >= row * multi) & (lane < row * multi + multi)
    pick_s = inside.astype(F32).astype(BF16)

    def spread(slot, index, at, many):
        rows = pl.ds(at, many)
        slot[0][rows, :] = mm(cos_s[index, rows, :], pick_s).astype(BF16)
        slot[1][rows, :] = mm(sin_s[index, rows, :], pick_s).astype(BF16)

    def build_left(slot, phases, part):
        c, s = phases[0][...], phases[1][...]
        for pol in range(tall // half_width):
            at = part * tall + pol * half_width
            rows = pl.ds(pl.multiple_of(at, half_width), half_width)
            u_re = out_tile[0, rows, :]
            u_im = out_tile[1, rows, :]
            re = u_re * c - u_im * s
            im = u_re * s + u_im * c
            slot[0][rows, :] = re
            slot[1][rows, :] = im
            slot[2][rows, :] = re + im

    def build_right(slot, index, part):
        both = mm_t(
            blocks[index][0 : 2 * multi, pl.ds(pl.multiple_of(part * size, 128), size)],
            in_pair[...],
        )
        for k in range(few):
            at = spheres * index + part * few + k
            c = cos_t[pl.ds(at, 1), :]
            s = sin_t[pl.ds(at, 1), :]
            to = pl.ds(pl.multiple_of(part * size + k * multi, multi), multi)
            for pol in range(2):
                lo = pol * half_width
                g_re = both[k * multi : (k + 1) * multi, lo : lo + half_width]
                g_im = both[k * multi : (k + 1) * multi, width + lo : width + lo + half_width]
                re = g_re * c + g_im * s
                im = g_im * c - g_re * s
                slot[0][to, lo : lo + half_width] = re.astype(BF16)
                slot[1][to, lo : lo + half_width] = im.astype(BF16)
                slot[2][to, lo : lo + half_width] = (re + im).astype(BF16)

    spread(spread_slots[0], 0, 0, half_width)
    if count > 1:
        spread(spread_slots[1], 1, 0, half_width)

    tile_copy.wait()

    @pl.loop(0, parts)
    def _(part):
        build_left(left_slots[0], spread_slots[0], part)
        build_right(right_slots[0], 0, part)

    for index in range(count):
        now, later = index % 2, (index + 1) % 2

        @pl.loop(0, parts)
        def _(part):
            rows = pl.ds(pl.multiple_of(part * tall, tall), tall)
            for total, left, right in zip(
                (sum_1, sum_2, sum_3), left_slots[now], right_slots[now]
            ):
                product = mm(left[rows, :], right[...])
                if index == 0:
                    total[rows, :] = product
                else:
                    total[rows, :] += product
            if index + 1 < count:
                build_left(left_slots[later], spread_slots[later], part)
                build_right(right_slots[later], index + 1, part)
            if index + 2 < count:
                many = half_width // parts
                spread(spread_slots[now], index + 2, pl.multiple_of(part * many, many), many)

    if last:
        fetch.wait()
    for part in range(4):
        kind, pol = part // 2, part % 2
        rows = pl.ds(part * half_width, half_width)
        re = sum_1[rows, :] - sum_2[rows, :]
        im = sum_3[rows, :] - sum_1[rows, :] - sum_2[rows, :]
        if not last:
            out[0, rows, :] = re
            out[1, rows, :] = im
        else:
            re = re + prev[0, rows, :]
            im = im + prev[1, rows, :]
            if kind == 1:
                at = lax.broadcasted_iota(jnp.int32, (half_width, width), 0) + pol * half_width
                lane = lax.broadcasted_iota(jnp.int32, (half_width, width), 1)
                on = at == lane
                re = re + jnp.where(on, jnp.cos(phase_row[...]), 0.0)
                im = im + jnp.where(on, jnp.sin(phase_row[...]), 0.0)
            to = pl.ds(pol * half_width, half_width)
            out[2 * kind, to, :] = re.astype(BF16)
            out[2 * kind + 1, to, :] = im.astype(BF16)


def layer_sum(blocks, spheres, multi, out_tile, in_pair, wave_col, prev=None, phase=None):
    count = len(blocks)
    last = prev is not None
    depth = spheres * multi
    half_width = wave_col.shape[0]
    width = 2 * half_width
    lanes = max(128, count * spheres)
    operands = list(blocks) + [out_tile, in_pair, wave_col]
    specs = [ANY] * (count + 1) + [VMEM, VMEM]
    if last:
        operands += [prev, phase.reshape(1, -1)]
        specs += [ANY, VMEM]
        shape = jax.ShapeDtypeStruct((4, width, width), BF16)
    else:
        shape = jax.ShapeDtypeStruct((2, 2 * width, width), F32)
    scratch = [pltpu.VMEM((2 * width, width), F32)] * 3
    scratch += [pltpu.VMEM((lanes, half_width), F32)] * 2
    scratch += [pltpu.VMEM((2 * width, depth), BF16)] * 6
    scratch += [pltpu.VMEM((depth, width), BF16)] * 6
    scratch += [pltpu.VMEM((half_width, depth), BF16)] * 4
    scratch += [pltpu.VMEM(out_tile.shape, BF16), pltpu.SemaphoreType.DMA]
    scratch += [pltpu.VMEM((count, half_width, spheres), BF16)] * 2
    scratch += [pltpu.VMEM((count,) + blocks[0].shape, BF16)]
    scratch += [pltpu.SemaphoreType.DMA((count,))]
    if last:
        scratch += [pltpu.VMEM((2, 2 * width, width), F32), pltpu.SemaphoreType.DMA]
    flops = count * 3 * 2 * 2 * width * width * depth
    return pl.pallas_call(
        functools.partial(layer_kernel, count, spheres, multi, last),
        out_shape=shape,
        in_specs=specs,
        out_specs=VMEM,
        scratch_shapes=scratch,
        compiler_params=pltpu.CompilerParams(vmem_limit_bytes=40 * 2**20),
        cost_estimate=pl.CostEstimate(flops=flops, bytes_accessed=2**23, transcendentals=0),
        name="layer_sum",
    )(*operands)


def form_kernel(rows, place, own, other, s_out, h_near, u, v, sems):
    width = own.shape[1]
    quarter = width // 4
    mine_is_u = place[0]
    core = place[1]
    first_row = pl.multiple_of(place[2] * rows, rows)

    def take(to, source, at):
        return pltpu.make_async_copy(source, to, sems.at[at])

    @pl.when(mine_is_u == 1)
    def _():
        take(u, own, 0).start()
        take(v, other, 1).start()

    @pl.when(mine_is_u == 0)
    def _():
        take(u, other, 0).start()
        take(v, own, 1).start()

    take(u, own, 0).wait()
    take(v, own, 1).wait()
    r_u, t_u = (u[0], u[1]), (u[2], u[3])
    r_v, t_v = (v[0], v[1]), (v[2], v[3])

    near = pl.ds(pl.multiple_of(core * quarter, quarter), quarter)
    far = pl.ds(pl.multiple_of((core + 2) * quarter, quarter), quarter)

    def columns(ref, at):
        return jnp.concatenate([ref[at, :, near], ref[at, :, far]], axis=1)

    base = (columns(v, 2), columns(v, 3))
    chain = cmul(r_u, base)
    chain = cmul(r_v, half(chain))
    chain = half((base[0] + chain[0], base[1] + chain[1]))
    here = cmul(t_u, chain)
    my = pl.ds(first_row, rows)
    row_t = (v[2, my, :], v[3, my, :])
    w_1 = half(cmul(row_t, r_u))
    k_part = cmul(w_1, chain)
    for side in range(2):
        at = slice(side * quarter, (side + 1) * quarter)
        cols = near if side == 0 else far
        for c in range(2):
            h_side = here[c][:, at].astype(BF16)
            k_side = (v[c, my, cols].astype(F32) + k_part[c][:, at]).astype(BF16)
            if side == 0:
                h_near[c, 0:width, :] = h_side
                h_near[c, width : width + rows, :] = k_side
            else:
                put = width + 2 * rows
                cut = width // 2
                s_out[c, put : put + cut, 0:quarter] = h_side[0:cut]
                s_out[c, put : put + cut, quarter : 2 * quarter] = h_side[cut:]
                put = put + cut
                cut = rows // 2
                s_out[c, put : put + cut, 0:quarter] = k_side[0:cut]
                s_out[c, put : put + cut, quarter : 2 * quarter] = k_side[cut:]

    w_2 = cmul(w_1, r_v)
    w_2 = half((row_t[0] + w_2[0], row_t[1] + w_2[1]))
    g_rows = half(cmul(w_2, t_u))

    mine = pl.ds(pl.multiple_of(core * 2 * quarter, 2 * quarter), 2 * quarter)
    base = (u[2, :, mine], u[3, :, mine])
    up = cmul(r_v, base)
    again = cmul(r_u, half(up))
    again = cmul(r_v, half(again))
    up = half(add(up, again))
    back = cmul(t_u, up)
    for c in range(2):
        s_out[c, 0:width, :] = (u[c, :, mine].astype(F32) + back[c]).astype(BF16)
        s_out[c, width : width + rows, :] = g_rows[c][:, 0 : 2 * quarter]
        s_out[c, width + rows : width + 2 * rows, :] = g_rows[c][:, 2 * quarter :]


def form(place, own, other, rows):
    width = own.shape[1]
    return pl.pallas_call(
        functools.partial(form_kernel, rows),
        out_shape=(
            jax.ShapeDtypeStruct((2, 3 * width // 2 + 5 * rows // 2, width // 2), BF16),
            jax.ShapeDtypeStruct((2, width + rows, width // 4), BF16),
        ),
        in_specs=[SMEM, ANY, ANY],
        out_specs=(VMEM, VMEM),
        scratch_shapes=[pltpu.VMEM(own.shape, BF16)] * 2 + [pltpu.SemaphoreType.DMA((2,))],
        compiler_params=pltpu.CompilerParams(vmem_limit_bytes=28 * 2**20),
        cost_estimate=pl.CostEstimate(flops=2**32, bytes_accessed=2**23, transcendentals=0),
        name="form",
    )(place, own, other)


def join_kernel(
    rows, place, s_mine, s_side, s_far, s_far_side, h_near, refl, trans, sides, h, sems
):
    width = h.shape[1] - rows
    lower = place[3]
    core = place[1]
    copies = [
        pltpu.make_async_copy(source, sides.at[side, part], sems.at[at])
        for at, (source, side, part) in enumerate(
            (
                (s_mine, lower, core),
                (s_side, lower, 1 - core),
                (s_far, 1 - lower, core),
                (s_far_side, 1 - lower, 1 - core),
            )
        )
    ]
    for copy in copies:
        copy.start()

    @pl.when(lower == 0)
    def _():
        near = pltpu.make_async_copy(h_near, h, sems.at[4])
        near.start()
        near.wait()

    for copy in copies:
        copy.wait()

    @pl.when(lower == 1)
    def _():
        quarter = h.shape[2]
        put = width + 2 * rows
        for c in range(2):
            for at, cut in ((0, width // 2), (width, rows // 2)):
                frm = put + at // 2
                for lane in range(2):
                    h[c, at + lane * cut : at + (lane + 1) * cut, :] = sides[
                        0, core, c, frm : frm + cut, lane * quarter : (lane + 1) * quarter
                    ]

    def rows_of(side):
        return tuple(
            jnp.concatenate(
                [
                    sides[side, 0, c, width : width + rows, :],
                    sides[side, 0, c, width + rows : width + 2 * rows, :],
                ],
                axis=1,
            )
            for c in range(2)
        )

    def times(pair, side):
        parts = [
            cmul(pair, (sides[side, h_, 0, 0:width, :], sides[side, h_, 1, 0:width, :]))
            for h_ in range(2)
        ]
        return tuple(jnp.concatenate([parts[0][c], parts[1][c]], axis=1) for c in range(2))

    from_above = rows_of(0)
    from_below = rows_of(1)
    second = half(times(from_above, 1))
    both = tuple(jnp.concatenate([from_below[c], second[c]], axis=0) for c in range(2))
    chain = times(half(times(both, 0)), 1)
    chain = half(tuple(both[c].astype(F32) + chain[c] for c in range(2)))
    result = cmul(chain, (h[0, 0:width, :], h[1, 0:width, :]))
    for c in range(2):
        trans[c] = result[c][0:rows]
        refl[c] = h[c, width : width + rows, :].astype(F32) + result[c][rows : 2 * rows]


def join(place, s_mine, s_side, s_far, s_far_side, h_near, rows):
    columns = h_near.shape[2]
    shape = jax.ShapeDtypeStruct((2, rows, columns), F32)
    return pl.pallas_call(
        functools.partial(join_kernel, rows),
        out_shape=(shape, shape),
        in_specs=[SMEM] + [ANY] * 5,
        out_specs=(VMEM, VMEM),
        scratch_shapes=[
            pltpu.VMEM((2, 2) + s_mine.shape, BF16),
            pltpu.VMEM(h_near.shape, BF16),
            pltpu.SemaphoreType.DMA((5,)),
        ],
        compiler_params=pltpu.CompilerParams(vmem_limit_bytes=20 * 2**20),
        cost_estimate=pl.CostEstimate(flops=2**30, bytes_accessed=2**22, transcendentals=0),
        name="join",
    )(place, s_mine, s_side, s_far, s_far_side, h_near)


def whole_layers(inner, out_basis, in_basis, tmatrix, sites, waves, layer_phase):
    spheres, multi = tmatrix.shape[1], tmatrix.shape[3]
    half_width = waves.shape[1]
    width = 2 * half_width
    groups = lax.axis_size("sph")
    outer = groups // inner
    rows = width // groups
    layer = lax.axis_index("layer")

    depth = spheres * multi
    block = tmatrix[0].astype(BF16).transpose(1, 3, 0, 2).reshape(2 * multi, depth)
    coords = jnp.stack([sites[0] // LATTICE, sites[0] % LATTICE]).astype(BF16)
    coords = jnp.broadcast_to(coords[:, :, None], (2, spheres, multi)).reshape(2, depth)
    block = jnp.concatenate([block, coords, jnp.zeros((EXTRA - 2, depth), BF16)], axis=0)

    def shifted(value, far, side):
        pairs = [
            (g, ((g // inner + far) % outer) * inner + (g % inner + side) % inner)
            for g in range(groups)
        ]
        return lax.ppermute(value, "sph", pairs)

    near = [shifted(block, 0, 1), shifted(block, 1, 0), shifted(block, outer - 1, 0)]
    near = lax.optimization_barrier((block, *near))
    block = near[0]
    far = [shifted(block, 2, 0), shifted(near[2], 0, 1), shifted(near[3], 0, 1)]
    far += [shifted(block, 2, 1)]

    turned = out_basis[0].astype(BF16).transpose(1, 0, 3, 2).reshape(2, 2 * width, multi)
    out_tile = jnp.tile(turned, (1, 1, spheres))
    b_re, b_im = in_basis[0, 0], in_basis[0, 1]
    in_pair = jnp.concatenate(
        [jnp.concatenate([b_re, b_im], axis=1), jnp.concatenate([-b_im, b_re], axis=1)], axis=0
    ).astype(BF16)
    wave_col = waves.astype(F32).T
    part = layer_sum(near, spheres, multi, out_tile, in_pair, wave_col)
    own = layer_sum(far, spheres, multi, out_tile, in_pair, wave_col, part, layer_phase[0])

    other = lax.ppermute(own, "layer", [(at, at ^ 1) for at in range(4)])
    core, lower = layer % 2, layer // 2
    mine_is_u = jnp.where(core != lower, 1, 0)
    place = jnp.stack([mine_is_u, core, lax.axis_index("sph"), lower]).astype(jnp.int32)
    s_mine, h_near = form(place, own, other, rows)
    s_far = lax.ppermute(s_mine, "layer", [(at, at ^ 2) for at in range(4)])
    s_side = lax.ppermute(s_mine, "layer", [(at, at ^ 1) for at in range(4)])
    s_far_side = lax.ppermute(s_far, "layer", [(at, at ^ 1) for at in range(4)])
    return join(place, s_mine, s_side, s_far, s_far_side, h_near, rows)


def solution(mesh):
    in_specs = (
        P("layer", None, None, None, None),
        P("layer", None, None, None),
        P("layer", "sph", None, None, None),
        P("layer", "sph"),
        P(),
        P("layer", None),
    )
    out_specs = (P(None, "sph", "layer"), P(None, "sph", "layer"))
    on_device = by_rows
    if mesh.shape["layer"] == 4 and mesh.shape["sph"] == 8:
        on_device = functools.partial(whole_layers, 2)
    return jax.shard_map(
        on_device, mesh=mesh, in_specs=in_specs, out_specs=out_specs, check_vma=False
    )
```

```python
import functools
import math

import jax
import jax.numpy as jnp
from jax import lax
from jax.experimental import pallas as pl
from jax.experimental.pallas import tpu as pltpu
from jax.sharding import PartitionSpec as P

LATTICE = 32
TWO_PI = 2.0 * math.pi
F32 = jnp.float32
BF16 = jnp.bfloat16
VMEM = pl.BlockSpec(memory_space=pltpu.VMEM)
ANY = pl.BlockSpec(memory_space=pl.ANY)
SMEM = pl.BlockSpec(memory_space=pltpu.SMEM)
EXTRA = 16


def partner_2(value, axis, bit):
    mask = 2**bit
    pairs = [(source, source ^ mask) for source in range(lax.axis_size(axis))]
    return lax.ppermute(value, axis, pairs)


def wave_angles(site_list, waves):
    column = site_list // LATTICE
    along = site_list % LATTICE
    phase_index = (
        waves[0][None, :] * column[:, None] + waves[1][None, :] * along[:, None]
    ) % LATTICE
    angles = phase_index.astype(jnp.float32) * (TWO_PI / LATTICE)
    return jnp.concatenate([angles, angles], axis=1)


def factors(out_layer, in_layer, tm_layer, angles):
    highest = lax.Precision.HIGHEST
    basis_re = out_layer[:, 0]
    basis_im = out_layer[:, 1]
    tmat_re = tm_layer[:, 0]
    tmat_im = tm_layer[:, 1]
    prod_re = jnp.einsum("kjw,sjm->ksmw", basis_re, tmat_re, precision=highest) - jnp.einsum(
        "kjw,sjm->ksmw", basis_im, tmat_im, precision=highest
    )
    prod_im = jnp.einsum("kjw,sjm->ksmw", basis_re, tmat_im, precision=highest) + jnp.einsum(
        "kjw,sjm->ksmw", basis_im, tmat_re, precision=highest
    )
    cosine = jnp.cos(angles)
    sine = jnp.sin(angles)
    left_re = prod_re * cosine[None, :, None, :] - prod_im * sine[None, :, None, :]
    left_im = prod_re * sine[None, :, None, :] + prod_im * cosine[None, :, None, :]
    right_re = in_layer[0][None] * cosine[:, None, :] + in_layer[1][None] * sine[:, None, :]
    right_im = in_layer[1][None] * cosine[:, None, :] - in_layer[0][None] * sine[:, None, :]
    inner = left_re.shape[1] * left_re.shape[2]
    width = left_re.shape[3]
    left_re = left_re.reshape(2, inner, width)
    left_im = left_im.reshape(2, inner, width)
    right_re = right_re.reshape(inner, width)
    right_im = right_im.reshape(inner, width)
    real_left = jnp.concatenate([left_re, -left_im], axis=1)
    imag_left = jnp.concatenate([left_re, left_im], axis=1)
    real_right = jnp.concatenate([right_re, right_im], axis=0)
    imag_right = jnp.concatenate([right_im, right_re], axis=0)
    return (real_left, imag_left, real_right, imag_right)


def project_rows(factor_set):
    real_left, imag_left, real_right, imag_right = factor_set
    highest = lax.Precision.HIGHEST
    pieces = []
    for kind in range(2):
        real_slice = real_left[kind]
        imag_slice = imag_left[kind]
        pieces.append(jnp.einsum("kr,kw->rw", real_slice, real_right, precision=highest))
        pieces.append(jnp.einsum("kr,kw->rw", imag_slice, imag_right, precision=highest))
    return jnp.concatenate(pieces, axis=1)


def narrow(matrix):
    return matrix.astype(jnp.bfloat16)


def complex_product(left, right):
    left_half = narrow(left)
    right_half = narrow(right)
    real_part = jnp.dot(left_half[0], right_half[0], preferred_element_type=jnp.float32) - jnp.dot(
        left_half[1], right_half[1], preferred_element_type=jnp.float32
    )
    imag_part = jnp.dot(left_half[0], right_half[1], preferred_element_type=jnp.float32) + jnp.dot(
        left_half[1], right_half[0], preferred_element_type=jnp.float32
    )
    return jnp.stack([real_part, imag_part])


def merge_level(state, bit):
    partner = partner_2(state.astype(jnp.bfloat16), "layer", bit).astype(state.dtype)
    is_upper = lax.axis_index("layer") // (1 << bit) % 2 == 0
    upper = jnp.where(is_upper, state, partner)
    lower = jnp.where(is_upper, partner, state)
    refl_a, trans_a, refl_a_back, trans_a_back = (upper[0], upper[1], upper[2], upper[3])
    refl_b, trans_b, refl_b_back, trans_b_back = (lower[0], lower[1], lower[2], lower[3])
    first_left = jnp.where(is_upper, refl_a_back, refl_b)
    first_right = jnp.where(is_upper, refl_b, refl_a_back)
    chain_base = jnp.where(is_upper, trans_a, trans_b_back)
    across = jnp.where(is_upper, trans_b, trans_a_back)
    final_left = jnp.where(is_upper, trans_a_back, trans_b)
    addend = jnp.where(is_upper, refl_a, refl_b_back)
    full_right, full_base = (
        lax.all_gather(narrow(first_right), "sph", axis=1, tiled=True),
        lax.all_gather(narrow(chain_base), "sph", axis=1, tiled=True),
    )
    first_mix = complex_product(first_left, full_right)
    chain = chain_base + complex_product(first_mix, full_base)
    full_chain = lax.all_gather(narrow(chain), "sph", axis=1, tiled=True)
    bounce = complex_product(first_right, full_chain)
    own_trans = complex_product(across, full_chain)
    full_bounce = lax.all_gather(narrow(bounce), "sph", axis=1, tiled=True)
    own_refl = addend + complex_product(final_left, full_bounce)
    mine = jnp.stack([own_trans, own_refl])
    theirs = partner_2(mine.astype(jnp.bfloat16), "layer", bit).astype(mine.dtype)
    trans_new = jnp.where(is_upper, mine[0], theirs[0])
    refl_new = jnp.where(is_upper, mine[1], theirs[1])
    trans_back_new = jnp.where(is_upper, theirs[0], mine[0])
    refl_back_new = jnp.where(is_upper, theirs[1], mine[1])
    return jnp.stack([refl_new, trans_new, refl_back_new, trans_back_new])


def by_rows(out_basis, in_basis, tmatrix, sites, waves, layer_phase):
    width = 2 * waves.shape[1]
    rows = width // lax.axis_size("sph")
    angles = wave_angles(sites[0], waves)
    factor_set = factors(out_basis[0], in_basis[0], tmatrix[0], angles)
    summed = lax.psum_scatter(
        project_rows(factor_set).astype(jnp.bfloat16), "sph", scatter_dimension=0, tiled=True
    ).astype(jnp.float32)
    first_row = lax.axis_index("sph") * rows
    diagonal = ((first_row + jnp.arange(rows))[:, None] == jnp.arange(width)[None, :]).astype(
        jnp.float32
    )
    refl = jnp.stack([summed[:, :width], summed[:, width : 2 * width]])
    trans_re = summed[:, 2 * width : 3 * width] + diagonal * jnp.cos(layer_phase[0])[None, :]
    trans_im = summed[:, 3 * width :] + diagonal * jnp.sin(layer_phase[0])[None, :]
    trans = jnp.stack([trans_re, trans_im])
    state = jnp.stack([refl, trans, refl, trans])
    levels = lax.axis_size("layer").bit_length() - 1
    for bit in range(levels):
        state = merge_level(state, bit)
    columns = width // lax.axis_size("layer")
    first_column = lax.axis_index("layer") * columns
    own_refl = lax.dynamic_slice_in_dim(state[0], first_column, columns, 2)
    own_trans = lax.dynamic_slice_in_dim(state[1], first_column, columns, 2)
    return (own_refl, own_trans)


def mm(left, right):
    return jnp.dot(left, right, preferred_element_type=F32)


def mm_t(left, right):
    return lax.dot_general(left, right, (((0,), (0,)), ((), ())), preferred_element_type=F32)


def cmul(left, right):
    return (
        mm(left[0], right[0]) - mm(left[1], right[1]),
        mm(left[0], right[1]) + mm(left[1], right[0]),
    )


def half(pair):
    return (pair[0].astype(BF16), pair[1].astype(BF16))


def add(one, two):
    return (one[0] + two[0], one[1] + two[1])


def circle(turns):
    turn = turns * (1.0 / LATTICE)
    turn = turn - jnp.floor(turn)
    quarter = jnp.floor(turn * 4.0 + 0.5)
    x = (turn - quarter * 0.25) * TWO_PI
    y = x * x
    sin = x * (1.0 + y * (-1.0 / 6 + y * (1.0 / 120 + y * (-1.0 / 5040 + y * (1.0 / 362880)))))
    cos = 1.0 + y * (-0.5 + y * (1.0 / 24 + y * (-1.0 / 720 + y * (1.0 / 40320))))
    odd = (quarter == 1.0) | (quarter == 3.0)
    cos, sin = jnp.where(odd, sin, cos), jnp.where(odd, cos, sin)
    cos = jnp.where((quarter == 1.0) | (quarter == 2.0), -cos, cos)
    sin = jnp.where((quarter == 2.0) | (quarter == 3.0), -sin, sin)
    return cos, sin


def layer_kernel(count, spheres, multi, last, *refs):
    sent = refs[:count]
    rest = list(refs[count:])
    out_basis, in_basis, waves = rest[:3]
    rest = rest[3:]
    if last:
        prev_hbm, phase_row = rest[:2]
        rest = rest[2:]
    out = rest[0]
    rest = rest[1:]
    sum_1, sum_2, sum_3, cos_t, sin_t = rest[:5]
    left_slots = (rest[5:8], rest[8:11])
    right_slots = (rest[11:14], rest[14:17])
    spread_slots = (rest[17:19], rest[19:21])
    out_tile, in_pair, cos_s, sin_s, blocks_here, block_sem = rest[21:27]
    blocks = [blocks_here.at[index] for index in range(count)]
    copies = [
        pltpu.make_async_copy(sent[index], blocks_here.at[index], block_sem.at[index])
        for index in range(count)
    ]
    for copy in copies:
        copy.start()
    if last:
        prev, arrived = rest[27:]
        fetch = pltpu.make_async_copy(prev_hbm, prev, arrived)
        fetch.start()
    depth = spheres * multi
    half_width = waves.shape[1]
    width = 2 * half_width
    lanes = cos_t.shape[0]
    parts = 1
    tall = 2 * width // parts
    few, size = spheres // parts, depth // parts

    row = lax.broadcasted_iota(jnp.int32, (multi, depth), 0).astype(F32)
    lane = lax.broadcasted_iota(jnp.int32, (multi, depth), 1).astype(F32)
    lane = lane - multi * jnp.floor((lane + 0.5) * (1.0 / multi))
    pick = (row == lane).astype(F32).astype(BF16)
    for kind in range(2):
        for c in range(2):
            tile = mm_t(out_basis[kind, c].astype(BF16), pick)
            out_tile[c, kind * width : (kind + 1) * width, :] = tile.astype(BF16)
    b_re, b_im = in_basis[0].astype(BF16), in_basis[1].astype(BF16)
    in_pair[0:multi, 0:width] = b_re
    in_pair[0:multi, width : 2 * width] = b_im
    in_pair[multi : 2 * multi, 0:width] = -b_im
    in_pair[multi : 2 * multi, width : 2 * width] = b_re
    for copy in copies:
        copy.wait()
    coords = None
    for index, block in enumerate(blocks):
        row = lax.broadcasted_iota(jnp.int32, (depth, lanes), 0)
        lane = lax.broadcasted_iota(jnp.int32, (depth, lanes), 1)
        pick = (row == (lane - spheres * index) * multi).astype(F32).astype(BF16)
        part = mm(block[2 * multi : 2 * multi + EXTRA, :], pick)
        coords = part if coords is None else coords + part
    pads = jnp.zeros((EXTRA - 2, half_width), F32)
    both = jnp.concatenate([waves[...].astype(F32), pads], axis=0).astype(BF16)
    turns = mm_t(both, coords.astype(BF16))
    cos_v, sin_v = circle(turns)
    for index in range(count):
        at = slice(spheres * index, spheres * (index + 1))
        cos_s[index] = cos_v[:, at].astype(BF16)
        sin_s[index] = sin_v[:, at].astype(BF16)
    cos_t[...] = cos_v.T
    sin_t[...] = sin_v.T
    row = lax.broadcasted_iota(jnp.int32, (spheres, depth), 0)
    lane = lax.broadcasted_iota(jnp.int32, (spheres, depth), 1)
    inside = (lane >= row * multi) & (lane < row * multi + multi)
    pick_s = inside.astype(F32).astype(BF16)

    def spread(slot, index, at, many):
        rows = pl.ds(at, many)
        slot[0][rows, :] = mm(cos_s[index, rows, :], pick_s).astype(BF16)
        slot[1][rows, :] = mm(sin_s[index, rows, :], pick_s).astype(BF16)

    def build_left(slot, phases, part, piece):
        low = (piece * tall // 8) % half_width
        many = tall // 8
        c, s = phases[0][low : low + many, :], phases[1][low : low + many, :]
        rows = pl.ds(pl.multiple_of(part * tall + piece * many, many), many)
        u_re = out_tile[0, rows, :]
        u_im = out_tile[1, rows, :]
        re = u_re * c - u_im * s
        im = u_re * s + u_im * c
        slot[0][rows, :] = re
        slot[1][rows, :] = im
        slot[2][rows, :] = re + im

    def build_right(slot, index, part, piece):
        many = size // 6
        base = part * size + piece * many
        both = mm_t(
            blocks[index][0 : 2 * multi, pl.ds(pl.multiple_of(base, 128), many)], in_pair[...]
        )
        done = 0
        while done < many:
            k = (piece * many + done) // multi
            stop = min((k + 1) * multi - piece * many, many)
            at = spheres * index + part * few + k
            c = cos_t[pl.ds(at, 1), :]
            s = sin_t[pl.ds(at, 1), :]
            to = pl.ds(pl.multiple_of(base + done, 16), stop - done)
            for pol in range(2):
                lo = pol * half_width
                g_re = both[done:stop, lo : lo + half_width]
                g_im = both[done:stop, width + lo : width + lo + half_width]
                re = g_re * c + g_im * s
                im = g_im * c - g_re * s
                slot[0][to, lo : lo + half_width] = re.astype(BF16)
                slot[1][to, lo : lo + half_width] = im.astype(BF16)
                slot[2][to, lo : lo + half_width] = (re + im).astype(BF16)
            done = stop

    def tasks_of(slot_left, phases, slot_right, index, part):
        lefts = [
            functools.partial(build_left, slot_left, phases, part, piece)
            for piece in range(8)
        ]
        rights = [
            functools.partial(build_right, slot_right, index, part, piece)
            for piece in range(6)
        ]
        tasks = []
        while lefts or rights:
            tasks += lefts[:1] + rights[:1]
            lefts, rights = lefts[1:], rights[1:]
        return tasks

    spread(spread_slots[0], 0, 0, half_width)
    if count > 1:
        spread(spread_slots[1], 1, 0, half_width)

    @pl.loop(0, parts)
    def _(part):
        for task in tasks_of(left_slots[0], spread_slots[0], right_slots[0], 0, part):
            task()

    for index in range(count):
        now, later = index % 2, (index + 1) % 2

        @pl.loop(0, parts)
        def _(part):
            tasks = []
            if index + 1 < count:
                tasks = tasks_of(
                    left_slots[later], spread_slots[later], right_slots[later], index + 1, part
                )
            if index + 2 < count:
                many = half_width // parts
                at = pl.multiple_of(part * many, many)
                tasks.append(functools.partial(spread, spread_slots[now], index + 2, at, many))
            rows = pl.ds(pl.multiple_of(part * tall, tall), tall)
            pieces = [
                (total, left, right, slice(lane * 256, (lane + 1) * 256))
                for total, left, right in zip(
                    (sum_1, sum_2, sum_3), left_slots[now], right_slots[now]
                )
                for lane in range(width // 256)
            ]
            for at, (total, left, right, cols) in enumerate(pieces):
                product = mm(left[rows, :], right[:, cols])
                if index == 0:
                    total[rows, cols] = product
                else:
                    total[rows, cols] += product
                share = -(-len(tasks) // (len(pieces) - at))
                for task in tasks[:share]:
                    task()
                tasks = tasks[share:]

    if last:
        fetch.wait()
    for part in range(4):
        kind, pol = part // 2, part % 2
        rows = pl.ds(part * half_width, half_width)
        re = sum_1[rows, :] - sum_2[rows, :]
        im = sum_3[rows, :] - sum_1[rows, :] - sum_2[rows, :]
        if not last:
            out[0, rows, :] = re
            out[1, rows, :] = im
        else:
            re = re + prev[0, rows, :]
            im = im + prev[1, rows, :]
            if kind == 1:
                at = lax.broadcasted_iota(jnp.int32, (half_width, width), 0) + pol * half_width
                lane = lax.broadcasted_iota(jnp.int32, (half_width, width), 1)
                on = at == lane
                re = re + jnp.where(on, jnp.cos(phase_row[...]), 0.0)
                im = im + jnp.where(on, jnp.sin(phase_row[...]), 0.0)
            to = pl.ds(pol * half_width, half_width)
            out[2 * kind, to, :] = re.astype(BF16)
            out[2 * kind + 1, to, :] = im.astype(BF16)


def pack_kernel(tmatrix, sites, out):
    spheres, _, multi, _ = tmatrix.shape
    depth = spheres * multi
    for c in range(2):
        flat = tmatrix[:, c].reshape(depth, multi)
        out[c * multi : (c + 1) * multi, :] = flat.T.astype(BF16)
    row = lax.broadcasted_iota(jnp.int32, (spheres, depth), 0)
    lane = lax.broadcasted_iota(jnp.int32, (spheres, depth), 1)
    inside = (lane >= row * multi) & (lane < row * multi + multi)
    pick = inside.astype(F32).astype(BF16)
    site = sites[...].astype(F32)
    column = jnp.floor((site + 0.5) * (1.0 / LATTICE))
    along = site - LATTICE * column
    both = jnp.concatenate([column, along, jnp.zeros((EXTRA - 2, spheres), F32)], axis=0)
    out[2 * multi : 2 * multi + EXTRA, :] = mm(both.astype(BF16), pick).astype(BF16)


def pack(tmatrix, sites):
    spheres, _, multi, _ = tmatrix.shape
    return pl.pallas_call(
        pack_kernel,
        out_shape=jax.ShapeDtypeStruct((2 * multi + EXTRA, spheres * multi), BF16),
        in_specs=[VMEM, VMEM],
        out_specs=VMEM,
        name="pack",
    )(tmatrix, sites)


def layer_sum(blocks, spheres, multi, out_basis, in_basis, waves, prev=None, phase=None):
    count = len(blocks)
    last = prev is not None
    depth = spheres * multi
    half_width = waves.shape[1]
    width = 2 * half_width
    lanes = max(128, count * spheres)
    operands = list(blocks) + [out_basis, in_basis, waves]
    specs = [ANY] * count + [VMEM] * 3
    if last:
        operands += [prev, phase.reshape(1, -1)]
        specs += [ANY, VMEM]
        shape = jax.ShapeDtypeStruct((4, width, width), BF16)
    else:
        shape = jax.ShapeDtypeStruct((2, 2 * width, width), F32)
    scratch = [pltpu.VMEM((2 * width, width), F32)] * 3
    scratch += [pltpu.VMEM((lanes, half_width), F32)] * 2
    scratch += [pltpu.VMEM((2 * width, depth), BF16)] * 6
    scratch += [pltpu.VMEM((depth, width), BF16)] * 6
    scratch += [pltpu.VMEM((half_width, depth), BF16)] * 4
    scratch += [pltpu.VMEM((2, 2 * width, depth), BF16), pltpu.VMEM((2 * multi, 2 * width), BF16)]
    scratch += [pltpu.VMEM((count, half_width, spheres), BF16)] * 2
    scratch += [pltpu.VMEM((count,) + blocks[0].shape, BF16)]
    scratch += [pltpu.SemaphoreType.DMA((count,))]
    if last:
        scratch += [pltpu.VMEM((2, 2 * width, width), F32), pltpu.SemaphoreType.DMA]
    flops = count * 3 * 2 * 2 * width * width * depth
    return pl.pallas_call(
        functools.partial(layer_kernel, count, spheres, multi, last),
        out_shape=shape,
        in_specs=specs,
        out_specs=VMEM,
        scratch_shapes=scratch,
        compiler_params=pltpu.CompilerParams(vmem_limit_bytes=40 * 2**20),
        cost_estimate=pl.CostEstimate(flops=flops, bytes_accessed=2**23, transcendentals=0),
        name="layer_sum",
    )(*operands)


def form_kernel(rows, place, own, other, s_out, h_near, u, v, sems):
    width = own.shape[1]
    quarter = width // 4
    mine_is_u = place[0]
    core = place[1]
    first_row = pl.multiple_of(place[2] * rows, rows)

    def take(to, source, at):
        return pltpu.make_async_copy(source, to, sems.at[at])

    @pl.when(mine_is_u == 1)
    def _():
        take(u, own, 0).start()
        take(v, other, 1).start()

    @pl.when(mine_is_u == 0)
    def _():
        take(u, other, 0).start()
        take(v, own, 1).start()

    take(u, own, 0).wait()
    take(v, own, 1).wait()
    r_u, t_u = (u[0], u[1]), (u[2], u[3])
    r_v, t_v = (v[0], v[1]), (v[2], v[3])

    near = pl.ds(pl.multiple_of(core * quarter, quarter), quarter)
    far = pl.ds(pl.multiple_of((core + 2) * quarter, quarter), quarter)

    def columns(ref, at):
        return jnp.concatenate([ref[at, :, near], ref[at, :, far]], axis=1)

    base = (columns(v, 2), columns(v, 3))
    chain = cmul(r_u, base)
    chain = cmul(r_v, half(chain))
    chain = half((base[0] + chain[0], base[1] + chain[1]))
    here = cmul(t_u, chain)
    my = pl.ds(first_row, rows)
    row_t = (v[2, my, :], v[3, my, :])
    w_1 = half(cmul(row_t, r_u))
    k_part = cmul(w_1, chain)
    for side in range(2):
        at = slice(side * quarter, (side + 1) * quarter)
        cols = near if side == 0 else far
        for c in range(2):
            h_side = here[c][:, at].astype(BF16)
            k_side = (v[c, my, cols].astype(F32) + k_part[c][:, at]).astype(BF16)
            if side == 0:
                h_near[c, 0:width, :] = h_side
                h_near[c, width : width + rows, :] = k_side
            else:
                put = width + 2 * rows
                cut = width // 2
                s_out[c, put : put + cut, 0:quarter] = h_side[0:cut]
                s_out[c, put : put + cut, quarter : 2 * quarter] = h_side[cut:]
                put = put + cut
                cut = rows // 2
                s_out[c, put : put + cut, 0:quarter] = k_side[0:cut]
                s_out[c, put : put + cut, quarter : 2 * quarter] = k_side[cut:]

    w_2 = cmul(w_1, r_v)
    w_2 = half((row_t[0] + w_2[0], row_t[1] + w_2[1]))
    g_rows = half(cmul(w_2, t_u))

    mine = pl.ds(pl.multiple_of(core * 2 * quarter, 2 * quarter), 2 * quarter)
    base = (u[2, :, mine], u[3, :, mine])
    up = cmul(r_v, base)
    again = cmul(r_u, half(up))
    again = cmul(r_v, half(again))
    up = half(add(up, again))
    back = cmul(t_u, up)
    for c in range(2):
        s_out[c, 0:width, :] = (u[c, :, mine].astype(F32) + back[c]).astype(BF16)
        s_out[c, width : width + rows, :] = g_rows[c][:, 0 : 2 * quarter]
        s_out[c, width + rows : width + 2 * rows, :] = g_rows[c][:, 2 * quarter :]


def form(place, own, other, rows):
    width = own.shape[1]
    return pl.pallas_call(
        functools.partial(form_kernel, rows),
        out_shape=(
            jax.ShapeDtypeStruct((2, 3 * width // 2 + 5 * rows // 2, width // 2), BF16),
            jax.ShapeDtypeStruct((2, width + rows, width // 4), BF16),
        ),
        in_specs=[SMEM, ANY, ANY],
        out_specs=(VMEM, VMEM),
        scratch_shapes=[pltpu.VMEM(own.shape, BF16)] * 2 + [pltpu.SemaphoreType.DMA((2,))],
        compiler_params=pltpu.CompilerParams(vmem_limit_bytes=28 * 2**20),
        cost_estimate=pl.CostEstimate(flops=2**32, bytes_accessed=2**23, transcendentals=0),
        name="form",
    )(place, own, other)


def join_kernel(
    rows, place, s_mine, s_side, s_far, s_far_side, h_near, refl, trans, sides, h, sems
):
    width = h.shape[1] - rows
    lower = place[3]
    core = place[1]
    copies = [
        pltpu.make_async_copy(source, sides.at[side, part], sems.at[at])
        for at, (source, side, part) in enumerate(
            (
                (s_mine, lower, core),
                (s_side, lower, 1 - core),
                (s_far, 1 - lower, core),
                (s_far_side, 1 - lower, 1 - core),
            )
        )
    ]
    for copy in copies:
        copy.start()

    @pl.when(lower == 0)
    def _():
        near = pltpu.make_async_copy(h_near, h, sems.at[4])
        near.start()
        near.wait()

    for copy in copies:
        copy.wait()

    @pl.when(lower == 1)
    def _():
        quarter = h.shape[2]
        put = width + 2 * rows
        for c in range(2):
            for at, cut in ((0, width // 2), (width, rows // 2)):
                frm = put + at // 2
                for lane in range(2):
                    h[c, at + lane * cut : at + (lane + 1) * cut, :] = sides[
                        0, core, c, frm : frm + cut, lane * quarter : (lane + 1) * quarter
                    ]

    def rows_of(side):
        return tuple(
            jnp.concatenate(
                [
                    sides[side, 0, c, width : width + rows, :],
                    sides[side, 0, c, width + rows : width + 2 * rows, :],
                ],
                axis=1,
            )
            for c in range(2)
        )

    def times(pair, side):
        parts = [
            cmul(pair, (sides[side, h_, 0, 0:width, :], sides[side, h_, 1, 0:width, :]))
            for h_ in range(2)
        ]
        return tuple(jnp.concatenate([parts[0][c], parts[1][c]], axis=1) for c in range(2))

    from_above = rows_of(0)
    from_below = rows_of(1)
    second = half(times(from_above, 1))
    both = tuple(jnp.concatenate([from_below[c], second[c]], axis=0) for c in range(2))
    chain = times(half(times(both, 0)), 1)
    chain = half(tuple(both[c].astype(F32) + chain[c] for c in range(2)))
    result = cmul(chain, (h[0, 0:width, :], h[1, 0:width, :]))
    for c in range(2):
        trans[c] = result[c][0:rows]
        refl[c] = h[c, width : width + rows, :].astype(F32) + result[c][rows : 2 * rows]


def join(place, s_mine, s_side, s_far, s_far_side, h_near, rows):
    columns = h_near.shape[2]
    shape = jax.ShapeDtypeStruct((2, rows, columns), F32)
    return pl.pallas_call(
        functools.partial(join_kernel, rows),
        out_shape=(shape, shape),
        in_specs=[SMEM] + [ANY] * 5,
        out_specs=(VMEM, VMEM),
        scratch_shapes=[
            pltpu.VMEM((2, 2) + s_mine.shape, BF16),
            pltpu.VMEM(h_near.shape, BF16),
            pltpu.SemaphoreType.DMA((5,)),
        ],
        compiler_params=pltpu.CompilerParams(vmem_limit_bytes=20 * 2**20),
        cost_estimate=pl.CostEstimate(flops=2**30, bytes_accessed=2**22, transcendentals=0),
        name="join",
    )(place, s_mine, s_side, s_far, s_far_side, h_near)


def whole_layers(inner, out_basis, in_basis, tmatrix, sites, waves, layer_phase):
    spheres, multi = tmatrix.shape[1], tmatrix.shape[3]
    half_width = waves.shape[1]
    width = 2 * half_width
    groups = lax.axis_size("sph")
    outer = groups // inner
    rows = width // groups
    layer = lax.axis_index("layer")

    block = pack(tmatrix[0], sites)

    def shifted(value, far, side):
        pairs = [
            (g, ((g // inner + far) % outer) * inner + (g % inner + side) % inner)
            for g in range(groups)
        ]
        return lax.ppermute(value, "sph", pairs)

    near = [shifted(block, 0, 1), shifted(block, 1, 0), shifted(block, outer - 1, 0)]
    near = [block, *near]
    far = [shifted(block, 2, 0), shifted(near[2], 0, 1), shifted(near[3], 0, 1)]
    far += [shifted(block, 2, 1)]

    part = layer_sum(near, spheres, multi, out_basis[0], in_basis[0], waves)
    own = layer_sum(far, spheres, multi, out_basis[0], in_basis[0], waves, part, layer_phase[0])

    other = lax.ppermute(own, "layer", [(at, at ^ 1) for at in range(4)])
    core, lower = layer % 2, layer // 2
    mine_is_u = jnp.where(core != lower, 1, 0)
    place = jnp.stack([mine_is_u, core, lax.axis_index("sph"), lower]).astype(jnp.int32)
    s_mine, h_near = form(place, own, other, rows)
    s_far = lax.ppermute(s_mine, "layer", [(at, at ^ 2) for at in range(4)])
    s_side = lax.ppermute(s_mine, "layer", [(at, at ^ 1) for at in range(4)])
    s_far_side = lax.ppermute(s_far, "layer", [(at, at ^ 1) for at in range(4)])
    return join(place, s_mine, s_side, s_far, s_far_side, h_near, rows)


def solution(mesh):
    in_specs = (
        P("layer", None, None, None, None),
        P("layer", None, None, None),
        P("layer", "sph", None, None, None),
        P("layer", "sph"),
        P(),
        P("layer", None),
    )
    out_specs = (P(None, "sph", "layer"), P(None, "sph", "layer"))
    on_device = by_rows
    if mesh.shape["layer"] == 4 and mesh.shape["sph"] == 8:
        on_device = functools.partial(whole_layers, 2)
    return jax.shard_map(
        on_device, mesh=mesh, in_specs=in_specs, out_specs=out_specs, check_vma=False
    )
```

```python
import functools
import math

import jax
import jax.numpy as jnp
from jax import lax
from jax.experimental import pallas as pl
from jax.experimental.pallas import tpu as pltpu
from jax.sharding import PartitionSpec as P

LATTICE = 32
TWO_PI = 2.0 * math.pi
F32 = jnp.float32
BF16 = jnp.bfloat16
VMEM = pl.BlockSpec(memory_space=pltpu.VMEM)
ANY = pl.BlockSpec(memory_space=pl.ANY)
SMEM = pl.BlockSpec(memory_space=pltpu.SMEM)
EXTRA = 16


def partner_2(value, axis, bit):
    mask = 2**bit
    pairs = [(source, source ^ mask) for source in range(lax.axis_size(axis))]
    return lax.ppermute(value, axis, pairs)


def wave_angles(site_list, waves):
    column = site_list // LATTICE
    along = site_list % LATTICE
    phase_index = (
        waves[0][None, :] * column[:, None] + waves[1][None, :] * along[:, None]
    ) % LATTICE
    angles = phase_index.astype(jnp.float32) * (TWO_PI / LATTICE)
    return jnp.concatenate([angles, angles], axis=1)


def factors(out_layer, in_layer, tm_layer, angles):
    highest = lax.Precision.HIGHEST
    basis_re = out_layer[:, 0]
    basis_im = out_layer[:, 1]
    tmat_re = tm_layer[:, 0]
    tmat_im = tm_layer[:, 1]
    prod_re = jnp.einsum("kjw,sjm->ksmw", basis_re, tmat_re, precision=highest) - jnp.einsum(
        "kjw,sjm->ksmw", basis_im, tmat_im, precision=highest
    )
    prod_im = jnp.einsum("kjw,sjm->ksmw", basis_re, tmat_im, precision=highest) + jnp.einsum(
        "kjw,sjm->ksmw", basis_im, tmat_re, precision=highest
    )
    cosine = jnp.cos(angles)
    sine = jnp.sin(angles)
    left_re = prod_re * cosine[None, :, None, :] - prod_im * sine[None, :, None, :]
    left_im = prod_re * sine[None, :, None, :] + prod_im * cosine[None, :, None, :]
    right_re = in_layer[0][None] * cosine[:, None, :] + in_layer[1][None] * sine[:, None, :]
    right_im = in_layer[1][None] * cosine[:, None, :] - in_layer[0][None] * sine[:, None, :]
    inner = left_re.shape[1] * left_re.shape[2]
    width = left_re.shape[3]
    left_re = left_re.reshape(2, inner, width)
    left_im = left_im.reshape(2, inner, width)
    right_re = right_re.reshape(inner, width)
    right_im = right_im.reshape(inner, width)
    real_left = jnp.concatenate([left_re, -left_im], axis=1)
    imag_left = jnp.concatenate([left_re, left_im], axis=1)
    real_right = jnp.concatenate([right_re, right_im], axis=0)
    imag_right = jnp.concatenate([right_im, right_re], axis=0)
    return (real_left, imag_left, real_right, imag_right)


def project_rows(factor_set):
    real_left, imag_left, real_right, imag_right = factor_set
    highest = lax.Precision.HIGHEST
    pieces = []
    for kind in range(2):
        real_slice = real_left[kind]
        imag_slice = imag_left[kind]
        pieces.append(jnp.einsum("kr,kw->rw", real_slice, real_right, precision=highest))
        pieces.append(jnp.einsum("kr,kw->rw", imag_slice, imag_right, precision=highest))
    return jnp.concatenate(pieces, axis=1)


def narrow(matrix):
    return matrix.astype(jnp.bfloat16)


def complex_product(left, right):
    left_half = narrow(left)
    right_half = narrow(right)
    real_part = jnp.dot(left_half[0], right_half[0], preferred_element_type=jnp.float32) - jnp.dot(
        left_half[1], right_half[1], preferred_element_type=jnp.float32
    )
    imag_part = jnp.dot(left_half[0], right_half[1], preferred_element_type=jnp.float32) + jnp.dot(
        left_half[1], right_half[0], preferred_element_type=jnp.float32
    )
    return jnp.stack([real_part, imag_part])


def merge_level(state, bit):
    partner = partner_2(state.astype(jnp.bfloat16), "layer", bit).astype(state.dtype)
    is_upper = lax.axis_index("layer") // (1 << bit) % 2 == 0
    upper = jnp.where(is_upper, state, partner)
    lower = jnp.where(is_upper, partner, state)
    refl_a, trans_a, refl_a_back, trans_a_back = (upper[0], upper[1], upper[2], upper[3])
    refl_b, trans_b, refl_b_back, trans_b_back = (lower[0], lower[1], lower[2], lower[3])
    first_left = jnp.where(is_upper, refl_a_back, refl_b)
    first_right = jnp.where(is_upper, refl_b, refl_a_back)
    chain_base = jnp.where(is_upper, trans_a, trans_b_back)
    across = jnp.where(is_upper, trans_b, trans_a_back)
    final_left = jnp.where(is_upper, trans_a_back, trans_b)
    addend = jnp.where(is_upper, refl_a, refl_b_back)
    full_right, full_base = (
        lax.all_gather(narrow(first_right), "sph", axis=1, tiled=True),
        lax.all_gather(narrow(chain_base), "sph", axis=1, tiled=True),
    )
    first_mix = complex_product(first_left, full_right)
    chain = chain_base + complex_product(first_mix, full_base)
    full_chain = lax.all_gather(narrow(chain), "sph", axis=1, tiled=True)
    bounce = complex_product(first_right, full_chain)
    own_trans = complex_product(across, full_chain)
    full_bounce = lax.all_gather(narrow(bounce), "sph", axis=1, tiled=True)
    own_refl = addend + complex_product(final_left, full_bounce)
    mine = jnp.stack([own_trans, own_refl])
    theirs = partner_2(mine.astype(jnp.bfloat16), "layer", bit).astype(mine.dtype)
    trans_new = jnp.where(is_upper, mine[0], theirs[0])
    refl_new = jnp.where(is_upper, mine[1], theirs[1])
    trans_back_new = jnp.where(is_upper, theirs[0], mine[0])
    refl_back_new = jnp.where(is_upper, theirs[1], mine[1])
    return jnp.stack([refl_new, trans_new, refl_back_new, trans_back_new])


def by_rows(out_basis, in_basis, tmatrix, sites, waves, layer_phase):
    width = 2 * waves.shape[1]
    rows = width // lax.axis_size("sph")
    angles = wave_angles(sites[0], waves)
    factor_set = factors(out_basis[0], in_basis[0], tmatrix[0], angles)
    summed = lax.psum_scatter(
        project_rows(factor_set).astype(jnp.bfloat16), "sph", scatter_dimension=0, tiled=True
    ).astype(jnp.float32)
    first_row = lax.axis_index("sph") * rows
    diagonal = ((first_row + jnp.arange(rows))[:, None] == jnp.arange(width)[None, :]).astype(
        jnp.float32
    )
    refl = jnp.stack([summed[:, :width], summed[:, width : 2 * width]])
    trans_re = summed[:, 2 * width : 3 * width] + diagonal * jnp.cos(layer_phase[0])[None, :]
    trans_im = summed[:, 3 * width :] + diagonal * jnp.sin(layer_phase[0])[None, :]
    trans = jnp.stack([trans_re, trans_im])
    state = jnp.stack([refl, trans, refl, trans])
    levels = lax.axis_size("layer").bit_length() - 1
    for bit in range(levels):
        state = merge_level(state, bit)
    columns = width // lax.axis_size("layer")
    first_column = lax.axis_index("layer") * columns
    own_refl = lax.dynamic_slice_in_dim(state[0], first_column, columns, 2)
    own_trans = lax.dynamic_slice_in_dim(state[1], first_column, columns, 2)
    return (own_refl, own_trans)


def mm(left, right):
    return jnp.dot(left, right, preferred_element_type=F32)


def mm_t(left, right):
    return lax.dot_general(left, right, (((0,), (0,)), ((), ())), preferred_element_type=F32)


def cmul(left, right):
    return (
        mm(left[0], right[0]) - mm(left[1], right[1]),
        mm(left[0], right[1]) + mm(left[1], right[0]),
    )


def half(pair):
    return (pair[0].astype(BF16), pair[1].astype(BF16))


def add(one, two):
    return (one[0] + two[0], one[1] + two[1])


def circle(turns):
    turn = turns * (1.0 / LATTICE)
    turn = turn - jnp.floor(turn)
    quarter = jnp.floor(turn * 4.0 + 0.5)
    x = (turn - quarter * 0.25) * TWO_PI
    y = x * x
    sin = x * (1.0 + y * (-1.0 / 6 + y * (1.0 / 120 + y * (-1.0 / 5040 + y * (1.0 / 362880)))))
    cos = 1.0 + y * (-0.5 + y * (1.0 / 24 + y * (-1.0 / 720 + y * (1.0 / 40320))))
    odd = (quarter == 1.0) | (quarter == 3.0)
    cos, sin = jnp.where(odd, sin, cos), jnp.where(odd, cos, sin)
    cos = jnp.where((quarter == 1.0) | (quarter == 2.0), -cos, cos)
    sin = jnp.where((quarter == 2.0) | (quarter == 3.0), -sin, sin)
    return cos, sin


def layer_kernel(count, spheres, multi, last, *refs):
    sent = refs[:count]
    rest = list(refs[count:])
    out_tile, in_pair, waves = rest[:3]
    rest = rest[3:]
    if last:
        prev_hbm, phase_row = rest[:2]
        rest = rest[2:]
    out = rest[0]
    rest = rest[1:]
    sum_1, sum_2, sum_3, cos_t, sin_t = rest[:5]
    left_slots = (rest[5:8], rest[8:11])
    right_slots = (rest[11:14], rest[14:17])
    spread_slots = (rest[17:19], rest[19:21])
    cos_s, sin_s, blocks_here, block_sem = rest[21:25]
    blocks = [blocks_here.at[index] for index in range(count)]
    copies = [
        pltpu.make_async_copy(sent[index], blocks_here.at[index], block_sem.at[index])
        for index in range(count)
    ]
    for copy in copies:
        copy.start()
    if last:
        prev, arrived = rest[25:]
        fetch = pltpu.make_async_copy(prev_hbm, prev, arrived)
        fetch.start()
    depth = spheres * multi
    half_width = waves.shape[1]
    width = 2 * half_width
    lanes = cos_t.shape[0]
    parts = 1
    tall = 2 * width // parts
    few, size = spheres // parts, depth // parts

    for copy in copies:
        copy.wait()
    coords = None
    for index, block in enumerate(blocks):
        row = lax.broadcasted_iota(jnp.int32, (depth, lanes), 0)
        lane = lax.broadcasted_iota(jnp.int32, (depth, lanes), 1)
        pick = (row == (lane - spheres * index) * multi).astype(F32).astype(BF16)
        part = mm(block[2 * multi : 2 * multi + EXTRA, :], pick)
        coords = part if coords is None else coords + part
    turns = mm_t(waves[...], coords.astype(BF16))
    cos_v, sin_v = circle(turns)
    for index in range(count):
        at = slice(spheres * index, spheres * (index + 1))
        cos_s[index] = cos_v[:, at].astype(BF16)
        sin_s[index] = sin_v[:, at].astype(BF16)
    cos_t[...] = cos_v.T
    sin_t[...] = sin_v.T
    row = lax.broadcasted_iota(jnp.int32, (spheres, depth), 0)
    lane = lax.broadcasted_iota(jnp.int32, (spheres, depth), 1)
    inside = (lane >= row * multi) & (lane < row * multi + multi)
    pick_s = inside.astype(F32).astype(BF16)

    def spread(slot, index, at, many):
        rows = pl.ds(at, many)
        slot[0][rows, :] = mm(cos_s[index, rows, :], pick_s).astype(BF16)
        slot[1][rows, :] = mm(sin_s[index, rows, :], pick_s).astype(BF16)

    def build_left(slot, phases, part, piece):
        low = (piece * tall // 8) % half_width
        many = tall // 8
        c, s = phases[0][low : low + many, :], phases[1][low : low + many, :]
        rows = pl.ds(part * tall + piece * many, many)
        u_re = out_tile[0, rows, :]
        u_im = out_tile[1, rows, :]
        re = u_re * c - u_im * s
        im = u_re * s + u_im * c
        slot[0][rows, :] = re
        slot[1][rows, :] = im
        slot[2][rows, :] = re + im

    def build_right(slot, index, part, piece):
        many = size // 6
        base = part * size + piece * many
        both = mm_t(
            blocks_here[index, 0 : 2 * multi, pl.ds(base, many)], in_pair[...]
        )
        done = 0
        while done < many:
            k = (piece * many + done) // multi
            stop = min((k + 1) * multi - piece * many, many)
            at = spheres * index + part * few + k
            c = cos_t[pl.ds(at, 1), :]
            s = sin_t[pl.ds(at, 1), :]
            to = pl.ds(base + done, stop - done)
            for pol in range(2):
                lo = pol * half_width
                g_re = both[done:stop, lo : lo + half_width]
                g_im = both[done:stop, width + lo : width + lo + half_width]
                re = g_re * c + g_im * s
                im = g_im * c - g_re * s
                slot[0][to, lo : lo + half_width] = re.astype(BF16)
                slot[1][to, lo : lo + half_width] = im.astype(BF16)
                slot[2][to, lo : lo + half_width] = (re + im).astype(BF16)
            done = stop

    def tasks_of(slot_left, phases, slot_right, index, part):
        lefts = [
            functools.partial(build_left, slot_left, phases, part, piece)
            for piece in range(8)
        ]
        rights = [
            functools.partial(build_right, slot_right, index, part, piece)
            for piece in range(6)
        ]
        tasks = []
        while lefts or rights:
            tasks += lefts[:1] + rights[:1]
            lefts, rights = lefts[1:], rights[1:]
        return tasks

    spread(spread_slots[0], 0, 0, half_width)
    if count > 1:
        spread(spread_slots[1], 1, 0, half_width)

    for task in tasks_of(left_slots[0], spread_slots[0], right_slots[0], 0, 0):
        task()
    for total in (sum_1, sum_2, sum_3):
        total[...] = jnp.zeros(total.shape, F32)

    @pl.loop(0, count // 2)
    def _(pair):
        for now in range(2):
            later = 1 - now
            index = 2 * pair + now
            after = jnp.minimum(index + 1, count - 1)
            tasks = tasks_of(left_slots[later], spread_slots[later], right_slots[later], after, 0)
            after = jnp.minimum(index + 2, count - 1)
            tasks.append(functools.partial(spread, spread_slots[now], after, 0, half_width))
            pieces = [
                (total, left, right, slice(lane * 256, (lane + 1) * 256))
                for total, left, right in zip(
                    (sum_1, sum_2, sum_3), left_slots[now], right_slots[now]
                )
                for lane in range(width // 256)
            ]
            for at, (total, left, right, cols) in enumerate(pieces):
                total[:, cols] += mm(left[...], right[:, cols])
                share = -(-len(tasks) // (len(pieces) - at))
                for task in tasks[:share]:
                    task()
                tasks = tasks[share:]

    if last:
        fetch.wait()
    for part in range(4):
        kind, pol = part // 2, part % 2
        rows = pl.ds(part * half_width, half_width)
        re = sum_1[rows, :] - sum_2[rows, :]
        im = sum_3[rows, :] - sum_1[rows, :] - sum_2[rows, :]
        if not last:
            out[0, rows, :] = re
            out[1, rows, :] = im
        else:
            re = re + prev[0, rows, :]
            im = im + prev[1, rows, :]
            if kind == 1:
                at = lax.broadcasted_iota(jnp.int32, (half_width, width), 0) + pol * half_width
                lane = lax.broadcasted_iota(jnp.int32, (half_width, width), 1)
                on = at == lane
                re = re + jnp.where(on, jnp.cos(phase_row[...]), 0.0)
                im = im + jnp.where(on, jnp.sin(phase_row[...]), 0.0)
            to = pl.ds(pol * half_width, half_width)
            out[2 * kind, to, :] = re.astype(BF16)
            out[2 * kind + 1, to, :] = im.astype(BF16)


def pack_kernel(tmatrix, sites, out):
    spheres, _, multi, _ = tmatrix.shape
    depth = spheres * multi
    for c in range(2):
        flat = tmatrix[:, c].reshape(depth, multi)
        out[c * multi : (c + 1) * multi, :] = flat.T.astype(BF16)
    row = lax.broadcasted_iota(jnp.int32, (spheres, depth), 0)
    lane = lax.broadcasted_iota(jnp.int32, (spheres, depth), 1)
    inside = (lane >= row * multi) & (lane < row * multi + multi)
    pick = inside.astype(F32).astype(BF16)
    site = sites[...].astype(F32)
    column = jnp.floor((site + 0.5) * (1.0 / LATTICE))
    along = site - LATTICE * column
    both = jnp.concatenate([column, along, jnp.zeros((EXTRA - 2, spheres), F32)], axis=0)
    out[2 * multi : 2 * multi + EXTRA, :] = mm(both.astype(BF16), pick).astype(BF16)


def pack(tmatrix, sites):
    spheres, _, multi, _ = tmatrix.shape
    return pl.pallas_call(
        pack_kernel,
        out_shape=jax.ShapeDtypeStruct((2 * multi + EXTRA, spheres * multi), BF16),
        in_specs=[VMEM, VMEM],
        out_specs=VMEM,
        name="pack",
    )(tmatrix, sites)


def prepare_kernel(depth, out_basis, in_basis, waves, out_tile, in_pair, waves_pad):
    multi, width = in_basis.shape[1], in_basis.shape[2]
    row = lax.broadcasted_iota(jnp.int32, (multi, depth), 0).astype(F32)
    lane = lax.broadcasted_iota(jnp.int32, (multi, depth), 1).astype(F32)
    lane = lane - multi * jnp.floor((lane + 0.5) * (1.0 / multi))
    pick = (row == lane).astype(F32).astype(BF16)
    for kind in range(2):
        for c in range(2):
            tile = mm_t(out_basis[kind, c].astype(BF16), pick)
            out_tile[c, kind * width : (kind + 1) * width, :] = tile.astype(BF16)
    b_re, b_im = in_basis[0].astype(BF16), in_basis[1].astype(BF16)
    in_pair[0:multi, 0:width] = b_re
    in_pair[0:multi, width : 2 * width] = b_im
    in_pair[multi : 2 * multi, 0:width] = -b_im
    in_pair[multi : 2 * multi, width : 2 * width] = b_re
    pads = jnp.zeros((EXTRA - 2, width // 2), F32)
    waves_pad[...] = jnp.concatenate([waves[...].astype(F32), pads], axis=0).astype(BF16)


def prepare(out_basis, in_basis, waves, spheres):
    multi, width = in_basis.shape[1], in_basis.shape[2]
    depth = spheres * multi
    return pl.pallas_call(
        functools.partial(prepare_kernel, depth),
        out_shape=(
            jax.ShapeDtypeStruct((2, 2 * width, depth), BF16),
            jax.ShapeDtypeStruct((2 * multi, 2 * width), BF16),
            jax.ShapeDtypeStruct((EXTRA, width // 2), BF16),
        ),
        in_specs=[VMEM] * 3,
        out_specs=(VMEM,) * 3,
        compiler_params=pltpu.CompilerParams(vmem_limit_bytes=16 * 2**20),
        cost_estimate=pl.CostEstimate(flops=2**31, bytes_accessed=2**22, transcendentals=0),
        name="prepare",
    )(out_basis, in_basis, waves)


def layer_sum(blocks, spheres, multi, out_tile, in_pair, waves, prev=None, phase=None):
    count = len(blocks)
    last = prev is not None
    depth = spheres * multi
    half_width = waves.shape[1]
    width = 2 * half_width
    lanes = max(128, count * spheres)
    operands = list(blocks) + [out_tile, in_pair, waves]
    specs = [ANY] * count + [VMEM] * 3
    if last:
        operands += [prev, phase.reshape(1, -1)]
        specs += [ANY, VMEM]
        shape = jax.ShapeDtypeStruct((4, width, width), BF16)
    else:
        shape = jax.ShapeDtypeStruct((2, 2 * width, width), F32)
    scratch = [pltpu.VMEM((2 * width, width), F32)] * 3
    scratch += [pltpu.VMEM((lanes, half_width), F32)] * 2
    scratch += [pltpu.VMEM((2 * width, depth), BF16)] * 6
    scratch += [pltpu.VMEM((depth, width), BF16)] * 6
    scratch += [pltpu.VMEM((half_width, depth), BF16)] * 4
    scratch += [pltpu.VMEM((count, half_width, spheres), BF16)] * 2
    scratch += [pltpu.VMEM((count,) + blocks[0].shape, BF16)]
    scratch += [pltpu.SemaphoreType.DMA((count,))]
    if last:
        scratch += [pltpu.VMEM((2, 2 * width, width), F32), pltpu.SemaphoreType.DMA]
    flops = count * 3 * 2 * 2 * width * width * depth
    return pl.pallas_call(
        functools.partial(layer_kernel, count, spheres, multi, last),
        out_shape=shape,
        in_specs=specs,
        out_specs=VMEM,
        scratch_shapes=scratch,
        compiler_params=pltpu.CompilerParams(vmem_limit_bytes=40 * 2**20),
        cost_estimate=pl.CostEstimate(flops=flops, bytes_accessed=2**23, transcendentals=0),
        name="layer_sum",
    )(*operands)


def take_pair(place, own, other, u, v, sems):
    def take(to, source, at):
        return pltpu.make_async_copy(source, to, sems.at[at])

    @pl.when(place[0] == 1)
    def _():
        take(u, own, 0).start()
        take(v, other, 1).start()

    @pl.when(place[0] == 0)
    def _():
        take(u, other, 0).start()
        take(v, own, 1).start()

    take(u, own, 0).wait()
    take(v, own, 1).wait()
    return (u[0], u[1]), (u[2], u[3]), (v[0], v[1]), (v[2], v[3])


def back_kernel(place, own, other, s_out, u, v, sems):
    side = own.shape[1] // 2
    r_u, t_u, r_v, _ = take_pair(place, own, other, u, v, sems)
    mine = pl.ds(pl.multiple_of(place[1] * side, side), side)
    base = (u[2, :, mine], u[3, :, mine])
    up = cmul(r_v, base)
    again = cmul(r_u, half(up))
    again = cmul(r_v, half(again))
    up = half(add(up, again))
    back = cmul(t_u, up)
    for c in range(2):
        s_out[c] = (u[c, :, mine].astype(F32) + back[c]).astype(BF16)


def rows_kernel(rows, place, own, other, after, h_near, h_far, u, v, sems):
    del after
    width = own.shape[1]
    quarter = width // 4
    core = place[1]
    r_u, t_u, r_v, _ = take_pair(place, own, other, u, v, sems)
    near = pl.ds(pl.multiple_of(core * quarter, quarter), quarter)
    far = pl.ds(pl.multiple_of((core + 2) * quarter, quarter), quarter)

    def columns(ref, at):
        return jnp.concatenate([ref[at, :, near], ref[at, :, far]], axis=1)

    base = (columns(v, 2), columns(v, 3))
    chain = cmul(r_u, base)
    chain = cmul(r_v, half(chain))
    chain = half((base[0] + chain[0], base[1] + chain[1]))
    here = cmul(t_u, chain)
    my = pl.ds(pl.multiple_of(place[2] * rows, rows), rows)
    row_t = (v[2, my, :], v[3, my, :])
    w_1 = half(cmul(row_t, r_u))
    k_part = cmul(w_1, chain)
    w_2 = cmul(w_1, r_v)
    w_2 = half((row_t[0] + w_2[0], row_t[1] + w_2[1]))
    g_rows = half(cmul(w_2, t_u))
    for side, (to, cols) in enumerate(((h_near, near), (h_far, far))):
        at = slice(side * quarter, (side + 1) * quarter)
        for c in range(2):
            to[c, 0:width, :] = here[c][:, at].astype(BF16)
            k_side = v[c, my, cols].astype(F32) + k_part[c][:, at]
            to[c, width : width + rows, :] = k_side.astype(BF16)
            for q in range(4):
                put = width + rows + q * rows
                to[c, put : put + rows, :] = g_rows[c][:, q * quarter : (q + 1) * quarter]


def form(place, own, other, rows):
    width = own.shape[1]
    scratch = [pltpu.VMEM(own.shape, BF16)] * 2 + [pltpu.SemaphoreType.DMA((2,))]
    params = pltpu.CompilerParams(vmem_limit_bytes=24 * 2**20)
    back = pl.pallas_call(
        back_kernel,
        out_shape=jax.ShapeDtypeStruct((2, width, width // 2), BF16),
        in_specs=[SMEM, ANY, ANY],
        out_specs=VMEM,
        scratch_shapes=scratch,
        compiler_params=params,
        cost_estimate=pl.CostEstimate(flops=2**32, bytes_accessed=2**23, transcendentals=0),
        name="back",
    )(place, own, other)
    shape = jax.ShapeDtypeStruct((2, width + 5 * rows, width // 4), BF16)
    near, far = pl.pallas_call(
        functools.partial(rows_kernel, rows),
        out_shape=(shape, shape),
        in_specs=[SMEM, ANY, ANY, ANY],
        out_specs=(VMEM, VMEM),
        scratch_shapes=scratch,
        compiler_params=params,
        cost_estimate=pl.CostEstimate(flops=2**32, bytes_accessed=2**23, transcendentals=0),
        name="rows",
    )(place, own, other, back)
    return back, near, far


def join_kernel(
    rows, place, s_mine, s_side, s_far, s_far_side, h_near, h_sent, refl, trans, sides, h, sems
):
    width = sides.shape[3]
    lower, core = place[3], place[1]
    moves = (
        (s_mine, sides.at[lower, core]),
        (s_side, sides.at[lower, 1 - core]),
        (s_far, sides.at[1 - lower, core]),
        (s_far_side, sides.at[1 - lower, 1 - core]),
        (h_near, h.at[lower]),
        (h_sent, h.at[1 - lower]),
    )
    copies = [pltpu.make_async_copy(*move, sems.at[at]) for at, move in enumerate(moves)]
    for copy in copies:
        copy.start()
    for copy in copies:
        copy.wait()

    def rows_of(side):
        return tuple(
            jnp.concatenate(
                [
                    h[side, c, width + rows + q * rows : width + 2 * rows + q * rows, :]
                    for q in range(4)
                ],
                axis=1,
            )
            for c in range(2)
        )

    def times(pair, side):
        parts = [
            cmul(pair, (sides[side, at, 0], sides[side, at, 1]))
            for at in range(2)
        ]
        return tuple(jnp.concatenate([parts[0][c], parts[1][c]], axis=1) for c in range(2))

    from_above = rows_of(0)
    from_below = rows_of(1)
    second = half(times(from_above, 1))
    both = tuple(jnp.concatenate([from_below[c], second[c]], axis=0) for c in range(2))
    chain = times(half(times(both, 0)), 1)
    chain = half(tuple(both[c].astype(F32) + chain[c] for c in range(2)))
    result = cmul(chain, (h[0, 0, 0:width, :], h[0, 1, 0:width, :]))
    for c in range(2):
        trans[c] = result[c][0:rows]
        refl[c] = h[0, c, width : width + rows, :].astype(F32) + result[c][rows : 2 * rows]


def join(place, s_mine, s_side, s_far, s_far_side, h_near, h_sent, rows):
    columns = h_near.shape[2]
    shape = jax.ShapeDtypeStruct((2, rows, columns), F32)
    return pl.pallas_call(
        functools.partial(join_kernel, rows),
        out_shape=(shape, shape),
        in_specs=[SMEM] + [ANY] * 6,
        out_specs=(VMEM, VMEM),
        scratch_shapes=[
            pltpu.VMEM((2, 2) + s_mine.shape, BF16),
            pltpu.VMEM((2,) + h_near.shape, BF16),
            pltpu.SemaphoreType.DMA((6,)),
        ],
        compiler_params=pltpu.CompilerParams(vmem_limit_bytes=20 * 2**20),
        cost_estimate=pl.CostEstimate(flops=2**30, bytes_accessed=2**22, transcendentals=0),
        name="join",
    )(place, s_mine, s_side, s_far, s_far_side, h_near, h_sent)


def whole_layers(inner, out_basis, in_basis, tmatrix, sites, waves, layer_phase):
    spheres, multi = tmatrix.shape[1], tmatrix.shape[3]
    half_width = waves.shape[1]
    width = 2 * half_width
    groups = lax.axis_size("sph")
    outer = groups // inner
    rows = width // groups
    layer = lax.axis_index("layer")

    block = pack(tmatrix[0], sites)

    def shifted(value, far, side):
        pairs = [
            (g, ((g // inner + far) % outer) * inner + (g % inner + side) % inner)
            for g in range(groups)
        ]
        return lax.ppermute(value, "sph", pairs)

    near = [shifted(block, 0, 1), shifted(block, 1, 0), shifted(block, outer - 1, 0)]
    near = [block, *near]
    far = [shifted(block, 2, 0), shifted(near[2], 0, 1), shifted(near[3], 0, 1)]
    far += [shifted(block, 2, 1)]

    ready = prepare(out_basis[0], in_basis[0], waves, spheres)
    part = layer_sum(near, spheres, multi, *ready)
    own = layer_sum(far, spheres, multi, *ready, part, layer_phase[0])

    other = lax.ppermute(own, "layer", [(at, at ^ 1) for at in range(4)])
    core, lower = layer % 2, layer // 2
    mine_is_u = jnp.where(core != lower, 1, 0)
    place = jnp.stack([mine_is_u, core, lax.axis_index("sph"), lower]).astype(jnp.int32)
    s_mine, h_near, h_far = form(place, own, other, rows)
    s_far = lax.ppermute(s_mine, "layer", [(at, at ^ 2) for at in range(4)])
    h_sent = lax.ppermute(h_far, "layer", [(at ^ 2, at) for at in range(4)])
    s_side = lax.ppermute(s_mine, "layer", [(at, at ^ 1) for at in range(4)])
    s_far, h_near = lax.optimization_barrier((s_far, h_near))
    s_far_side = lax.ppermute(s_far, "layer", [(at, at ^ 1) for at in range(4)])
    return join(place, s_mine, s_side, s_far, s_far_side, h_near, h_sent, rows)


def solution(mesh):
    in_specs = (
        P("layer", None, None, None, None),
        P("layer", None, None, None),
        P("layer", "sph", None, None, None),
        P("layer", "sph"),
        P(),
        P("layer", None),
    )
    out_specs = (P(None, "sph", "layer"), P(None, "sph", "layer"))
    on_device = by_rows
    if mesh.shape["layer"] == 4 and mesh.shape["sph"] == 8:
        on_device = functools.partial(whole_layers, 2)
    return jax.shard_map(
        on_device, mesh=mesh, in_specs=in_specs, out_specs=out_specs, check_vma=False
    )
```

```python
import functools
import math

import jax
import jax.numpy as jnp
from jax import lax
from jax.experimental import pallas as pl
from jax.experimental.pallas import tpu as pltpu
from jax.sharding import PartitionSpec as P

LATTICE = 32
TWO_PI = 2.0 * math.pi
F32 = jnp.float32
BF16 = jnp.bfloat16
VMEM = pl.BlockSpec(memory_space=pltpu.VMEM)
ANY = pl.BlockSpec(memory_space=pl.ANY)
SMEM = pl.BlockSpec(memory_space=pltpu.SMEM)
EXTRA = 16


def partner_2(value, axis, bit):
    mask = 2**bit
    pairs = [(source, source ^ mask) for source in range(lax.axis_size(axis))]
    return lax.ppermute(value, axis, pairs)


def wave_angles(site_list, waves):
    column = site_list // LATTICE
    along = site_list % LATTICE
    phase_index = (
        waves[0][None, :] * column[:, None] + waves[1][None, :] * along[:, None]
    ) % LATTICE
    angles = phase_index.astype(jnp.float32) * (TWO_PI / LATTICE)
    return jnp.concatenate([angles, angles], axis=1)


def factors(out_layer, in_layer, tm_layer, angles):
    highest = lax.Precision.HIGHEST
    basis_re = out_layer[:, 0]
    basis_im = out_layer[:, 1]
    tmat_re = tm_layer[:, 0]
    tmat_im = tm_layer[:, 1]
    prod_re = jnp.einsum("kjw,sjm->ksmw", basis_re, tmat_re, precision=highest) - jnp.einsum(
        "kjw,sjm->ksmw", basis_im, tmat_im, precision=highest
    )
    prod_im = jnp.einsum("kjw,sjm->ksmw", basis_re, tmat_im, precision=highest) + jnp.einsum(
        "kjw,sjm->ksmw", basis_im, tmat_re, precision=highest
    )
    cosine = jnp.cos(angles)
    sine = jnp.sin(angles)
    left_re = prod_re * cosine[None, :, None, :] - prod_im * sine[None, :, None, :]
    left_im = prod_re * sine[None, :, None, :] + prod_im * cosine[None, :, None, :]
    right_re = in_layer[0][None] * cosine[:, None, :] + in_layer[1][None] * sine[:, None, :]
    right_im = in_layer[1][None] * cosine[:, None, :] - in_layer[0][None] * sine[:, None, :]
    inner = left_re.shape[1] * left_re.shape[2]
    width = left_re.shape[3]
    left_re = left_re.reshape(2, inner, width)
    left_im = left_im.reshape(2, inner, width)
    right_re = right_re.reshape(inner, width)
    right_im = right_im.reshape(inner, width)
    real_left = jnp.concatenate([left_re, -left_im], axis=1)
    imag_left = jnp.concatenate([left_re, left_im], axis=1)
    real_right = jnp.concatenate([right_re, right_im], axis=0)
    imag_right = jnp.concatenate([right_im, right_re], axis=0)
    return (real_left, imag_left, real_right, imag_right)


def project_rows(factor_set):
    real_left, imag_left, real_right, imag_right = factor_set
    highest = lax.Precision.HIGHEST
    pieces = []
    for kind in range(2):
        real_slice = real_left[kind]
        imag_slice = imag_left[kind]
        pieces.append(jnp.einsum("kr,kw->rw", real_slice, real_right, precision=highest))
        pieces.append(jnp.einsum("kr,kw->rw", imag_slice, imag_right, precision=highest))
    return jnp.concatenate(pieces, axis=1)


def narrow(matrix):
    return matrix.astype(jnp.bfloat16)


def complex_product(left, right):
    left_half = narrow(left)
    right_half = narrow(right)
    real_part = jnp.dot(left_half[0], right_half[0], preferred_element_type=jnp.float32) - jnp.dot(
        left_half[1], right_half[1], preferred_element_type=jnp.float32
    )
    imag_part = jnp.dot(left_half[0], right_half[1], preferred_element_type=jnp.float32) + jnp.dot(
        left_half[1], right_half[0], preferred_element_type=jnp.float32
    )
    return jnp.stack([real_part, imag_part])


def merge_level(state, bit):
    partner = partner_2(state.astype(jnp.bfloat16), "layer", bit).astype(state.dtype)
    is_upper = lax.axis_index("layer") // (1 << bit) % 2 == 0
    upper = jnp.where(is_upper, state, partner)
    lower = jnp.where(is_upper, partner, state)
    refl_a, trans_a, refl_a_back, trans_a_back = (upper[0], upper[1], upper[2], upper[3])
    refl_b, trans_b, refl_b_back, trans_b_back = (lower[0], lower[1], lower[2], lower[3])
    first_left = jnp.where(is_upper, refl_a_back, refl_b)
    first_right = jnp.where(is_upper, refl_b, refl_a_back)
    chain_base = jnp.where(is_upper, trans_a, trans_b_back)
    across = jnp.where(is_upper, trans_b, trans_a_back)
    final_left = jnp.where(is_upper, trans_a_back, trans_b)
    addend = jnp.where(is_upper, refl_a, refl_b_back)
    full_right, full_base = (
        lax.all_gather(narrow(first_right), "sph", axis=1, tiled=True),
        lax.all_gather(narrow(chain_base), "sph", axis=1, tiled=True),
    )
    first_mix = complex_product(first_left, full_right)
    chain = chain_base + complex_product(first_mix, full_base)
    full_chain = lax.all_gather(narrow(chain), "sph", axis=1, tiled=True)
    bounce = complex_product(first_right, full_chain)
    own_trans = complex_product(across, full_chain)
    full_bounce = lax.all_gather(narrow(bounce), "sph", axis=1, tiled=True)
    own_refl = addend + complex_product(final_left, full_bounce)
    mine = jnp.stack([own_trans, own_refl])
    theirs = partner_2(mine.astype(jnp.bfloat16), "layer", bit).astype(mine.dtype)
    trans_new = jnp.where(is_upper, mine[0], theirs[0])
    refl_new = jnp.where(is_upper, mine[1], theirs[1])
    trans_back_new = jnp.where(is_upper, theirs[0], mine[0])
    refl_back_new = jnp.where(is_upper, theirs[1], mine[1])
    return jnp.stack([refl_new, trans_new, refl_back_new, trans_back_new])


def by_rows(out_basis, in_basis, tmatrix, sites, waves, layer_phase):
    width = 2 * waves.shape[1]
    rows = width // lax.axis_size("sph")
    angles = wave_angles(sites[0], waves)
    factor_set = factors(out_basis[0], in_basis[0], tmatrix[0], angles)
    summed = lax.psum_scatter(
        project_rows(factor_set).astype(jnp.bfloat16), "sph", scatter_dimension=0, tiled=True
    ).astype(jnp.float32)
    first_row = lax.axis_index("sph") * rows
    diagonal = ((first_row + jnp.arange(rows))[:, None] == jnp.arange(width)[None, :]).astype(
        jnp.float32
    )
    refl = jnp.stack([summed[:, :width], summed[:, width : 2 * width]])
    trans_re = summed[:, 2 * width : 3 * width] + diagonal * jnp.cos(layer_phase[0])[None, :]
    trans_im = summed[:, 3 * width :] + diagonal * jnp.sin(layer_phase[0])[None, :]
    trans = jnp.stack([trans_re, trans_im])
    state = jnp.stack([refl, trans, refl, trans])
    levels = lax.axis_size("layer").bit_length() - 1
    for bit in range(levels):
        state = merge_level(state, bit)
    columns = width // lax.axis_size("layer")
    first_column = lax.axis_index("layer") * columns
    own_refl = lax.dynamic_slice_in_dim(state[0], first_column, columns, 2)
    own_trans = lax.dynamic_slice_in_dim(state[1], first_column, columns, 2)
    return (own_refl, own_trans)


def mm(left, right):
    return jnp.dot(left, right, preferred_element_type=F32)


def mm_t(left, right):
    return lax.dot_general(left, right, (((0,), (0,)), ((), ())), preferred_element_type=F32)


def cmul(left, right):
    return (
        mm(left[0], right[0]) - mm(left[1], right[1]),
        mm(left[0], right[1]) + mm(left[1], right[0]),
    )


def half(pair):
    return (pair[0].astype(BF16), pair[1].astype(BF16))


def add(one, two):
    return (one[0] + two[0], one[1] + two[1])


def circle(turns):
    turn = turns * (1.0 / LATTICE)
    turn = turn - jnp.floor(turn)
    quarter = jnp.floor(turn * 4.0 + 0.5)
    x = (turn - quarter * 0.25) * TWO_PI
    y = x * x
    sin = x * (1.0 + y * (-1.0 / 6 + y * (1.0 / 120 + y * (-1.0 / 5040 + y * (1.0 / 362880)))))
    cos = 1.0 + y * (-0.5 + y * (1.0 / 24 + y * (-1.0 / 720 + y * (1.0 / 40320))))
    odd = (quarter == 1.0) | (quarter == 3.0)
    cos, sin = jnp.where(odd, sin, cos), jnp.where(odd, cos, sin)
    cos = jnp.where((quarter == 1.0) | (quarter == 2.0), -cos, cos)
    sin = jnp.where((quarter == 2.0) | (quarter == 3.0), -sin, sin)
    return cos, sin


def layer_kernel(count, spheres, multi, last, *refs):
    sent = refs[:count]
    rest = list(refs[count:])
    out_tile, in_pair, waves = rest[:3]
    rest = rest[3:]
    if last:
        prev_hbm, phase_row = rest[:2]
        rest = rest[2:]
    out = rest[0]
    rest = rest[1:]
    sum_1, sum_2, sum_3, cos_t, sin_t = rest[:5]
    left_slots = (rest[5:8], rest[8:11])
    right_slots = (rest[11:14], rest[14:17])
    spread_slots = (rest[17:19], rest[19:21])
    cos_s, sin_s, blocks_here, block_sem = rest[21:25]
    blocks = [blocks_here.at[index] for index in range(count)]
    copies = [
        pltpu.make_async_copy(sent[index], blocks_here.at[index], block_sem.at[index])
        for index in range(count)
    ]
    for copy in copies:
        copy.start()
    if last:
        prev, arrived = rest[25:]
        fetch = pltpu.make_async_copy(prev_hbm, prev, arrived)
        fetch.start()
    depth = spheres * multi
    half_width = waves.shape[1]
    width = 2 * half_width
    lanes = cos_t.shape[0]
    parts = 1
    tall = 2 * width // parts
    few, size = spheres // parts, depth // parts

    for copy in copies:
        copy.wait()
    coords = None
    for index, block in enumerate(blocks):
        row = lax.broadcasted_iota(jnp.int32, (depth, lanes), 0)
        lane = lax.broadcasted_iota(jnp.int32, (depth, lanes), 1)
        pick = (row == (lane - spheres * index) * multi).astype(F32).astype(BF16)
        part = mm(block[2 * multi : 2 * multi + EXTRA, :], pick)
        coords = part if coords is None else coords + part
    turns = mm_t(waves[...], coords.astype(BF16))
    cos_v, sin_v = circle(turns)
    for index in range(count):
        at = slice(spheres * index, spheres * (index + 1))
        cos_s[index] = cos_v[:, at].astype(BF16)
        sin_s[index] = sin_v[:, at].astype(BF16)
    cos_t[...] = cos_v.T
    sin_t[...] = sin_v.T
    row = lax.broadcasted_iota(jnp.int32, (spheres, depth), 0)
    lane = lax.broadcasted_iota(jnp.int32, (spheres, depth), 1)
    inside = (lane >= row * multi) & (lane < row * multi + multi)
    pick_s = inside.astype(F32).astype(BF16)

    def spread(slot, index, at, many):
        rows = pl.ds(at, many)
        slot[0][rows, :] = mm(cos_s[index, rows, :], pick_s).astype(BF16)
        slot[1][rows, :] = mm(sin_s[index, rows, :], pick_s).astype(BF16)

    def build_left(slot, phases, part, piece):
        low = (piece * tall // 8) % half_width
        many = tall // 8
        c, s = phases[0][low : low + many, :], phases[1][low : low + many, :]
        rows = pl.ds(part * tall + piece * many, many)
        u_re = out_tile[0, rows, :]
        u_im = out_tile[1, rows, :]
        re = u_re * c - u_im * s
        im = u_re * s + u_im * c
        slot[0][rows, :] = re
        slot[1][rows, :] = im
        slot[2][rows, :] = re + im

    def build_right(slot, index, part, piece):
        many = size // 6
        base = part * size + piece * many
        both = mm_t(
            blocks_here[index, 0 : 2 * multi, pl.ds(base, many)], in_pair[...]
        )
        done = 0
        while done < many:
            k = (piece * many + done) // multi
            stop = min((k + 1) * multi - piece * many, many)
            at = spheres * index + part * few + k
            c = cos_t[pl.ds(at, 1), :]
            s = sin_t[pl.ds(at, 1), :]
            to = pl.ds(base + done, stop - done)
            for pol in range(2):
                lo = pol * half_width
                g_re = both[done:stop, lo : lo + half_width]
                g_im = both[done:stop, width + lo : width + lo + half_width]
                re = g_re * c + g_im * s
                im = g_im * c - g_re * s
                slot[0][to, lo : lo + half_width] = re.astype(BF16)
                slot[1][to, lo : lo + half_width] = im.astype(BF16)
                slot[2][to, lo : lo + half_width] = (re + im).astype(BF16)
            done = stop

    def tasks_of(slot_left, phases, slot_right, index, part):
        lefts = [
            functools.partial(build_left, slot_left, phases, part, piece)
            for piece in range(8)
        ]
        rights = [
            functools.partial(build_right, slot_right, index, part, piece)
            for piece in range(6)
        ]
        tasks = []
        while lefts or rights:
            tasks += lefts[:1] + rights[:1]
            lefts, rights = lefts[1:], rights[1:]
        return tasks

    spread(spread_slots[0], 0, 0, half_width)
    if count > 1:
        spread(spread_slots[1], 1, 0, half_width)

    for task in tasks_of(left_slots[0], spread_slots[0], right_slots[0], 0, 0):
        task()
    @pl.loop(0, count // 2)
    def _(pair):
        for now in range(2):
            later = 1 - now
            index = 2 * pair + now
            after = jnp.minimum(index + 1, count - 1)
            tasks = tasks_of(left_slots[later], spread_slots[later], right_slots[later], after, 0)
            after = jnp.minimum(index + 2, count - 1)
            tasks.append(functools.partial(spread, spread_slots[now], after, 0, half_width))
            pieces = [
                (total, left, right, slice(lane * 256, (lane + 1) * 256))
                for total, left, right in zip(
                    (sum_1, sum_2, sum_3), left_slots[now], right_slots[now]
                )
                for lane in range(width // 256)
            ]
            for at, (total, left, right, cols) in enumerate(pieces):
                before = total[:, cols]
                if now == 0:
                    before = jnp.where(pair > 0, before, 0.0)
                total[:, cols] = before + mm(left[...], right[:, cols])
                share = -(-len(tasks) // (len(pieces) - at))
                for task in tasks[:share]:
                    task()
                tasks = tasks[share:]

    if last:
        fetch.wait()
    for part in range(4):
        kind, pol = part // 2, part % 2
        rows = pl.ds(part * half_width, half_width)
        re = sum_1[rows, :] - sum_2[rows, :]
        im = sum_3[rows, :] - sum_1[rows, :] - sum_2[rows, :]
        if not last:
            out[0, rows, :] = re
            out[1, rows, :] = im
        else:
            re = re + prev[0, rows, :]
            im = im + prev[1, rows, :]
            if kind == 1:
                at = lax.broadcasted_iota(jnp.int32, (half_width, width), 0) + pol * half_width
                lane = lax.broadcasted_iota(jnp.int32, (half_width, width), 1)
                on = at == lane
                re = re + jnp.where(on, jnp.cos(phase_row[...]), 0.0)
                im = im + jnp.where(on, jnp.sin(phase_row[...]), 0.0)
            to = pl.ds(pol * half_width, half_width)
            out[2 * kind, to, :] = re.astype(BF16)
            out[2 * kind + 1, to, :] = im.astype(BF16)


def pack_kernel(tmatrix, sites, out):
    spheres, _, multi, _ = tmatrix.shape
    depth = spheres * multi
    for c in range(2):
        flat = tmatrix[:, c].reshape(depth, multi)
        out[c * multi : (c + 1) * multi, :] = flat.T.astype(BF16)
    row = lax.broadcasted_iota(jnp.int32, (spheres, depth), 0)
    lane = lax.broadcasted_iota(jnp.int32, (spheres, depth), 1)
    inside = (lane >= row * multi) & (lane < row * multi + multi)
    pick = inside.astype(F32).astype(BF16)
    site = sites[...].astype(F32)
    column = jnp.floor((site + 0.5) * (1.0 / LATTICE))
    along = site - LATTICE * column
    both = jnp.concatenate([column, along, jnp.zeros((EXTRA - 2, spheres), F32)], axis=0)
    out[2 * multi : 2 * multi + EXTRA, :] = mm(both.astype(BF16), pick).astype(BF16)


def pack(tmatrix, sites):
    spheres, _, multi, _ = tmatrix.shape
    return pl.pallas_call(
        pack_kernel,
        out_shape=jax.ShapeDtypeStruct((2 * multi + EXTRA, spheres * multi), BF16),
        in_specs=[VMEM, VMEM],
        out_specs=VMEM,
        name="pack",
    )(tmatrix, sites)


def prepare_kernel(depth, out_basis, in_basis, waves, out_tile, in_pair, waves_pad):
    multi, width = in_basis.shape[1], in_basis.shape[2]
    row = lax.broadcasted_iota(jnp.int32, (multi, depth), 0).astype(F32)
    lane = lax.broadcasted_iota(jnp.int32, (multi, depth), 1).astype(F32)
    lane = lane - multi * jnp.floor((lane + 0.5) * (1.0 / multi))
    pick = (row == lane).astype(F32).astype(BF16)
    for kind in range(2):
        for c in range(2):
            tile = mm_t(out_basis[kind, c].astype(BF16), pick)
            out_tile[c, kind * width : (kind + 1) * width, :] = tile.astype(BF16)
    b_re, b_im = in_basis[0].astype(BF16), in_basis[1].astype(BF16)
    in_pair[0:multi, 0:width] = b_re
    in_pair[0:multi, width : 2 * width] = b_im
    in_pair[multi : 2 * multi, 0:width] = -b_im
    in_pair[multi : 2 * multi, width : 2 * width] = b_re
    pads = jnp.zeros((EXTRA - 2, width // 2), F32)
    waves_pad[...] = jnp.concatenate([waves[...].astype(F32), pads], axis=0).astype(BF16)


def prepare(out_basis, in_basis, waves, spheres):
    multi, width = in_basis.shape[1], in_basis.shape[2]
    depth = spheres * multi
    return pl.pallas_call(
        functools.partial(prepare_kernel, depth),
        out_shape=(
            jax.ShapeDtypeStruct((2, 2 * width, depth), BF16),
            jax.ShapeDtypeStruct((2 * multi, 2 * width), BF16),
            jax.ShapeDtypeStruct((EXTRA, width // 2), BF16),
        ),
        in_specs=[VMEM] * 3,
        out_specs=(VMEM,) * 3,
        compiler_params=pltpu.CompilerParams(vmem_limit_bytes=16 * 2**20),
        cost_estimate=pl.CostEstimate(flops=2**31, bytes_accessed=2**22, transcendentals=0),
        name="prepare",
    )(out_basis, in_basis, waves)


def layer_sum(blocks, spheres, multi, out_tile, in_pair, waves, prev=None, phase=None):
    count = len(blocks)
    last = prev is not None
    depth = spheres * multi
    half_width = waves.shape[1]
    width = 2 * half_width
    lanes = max(128, count * spheres)
    operands = list(blocks) + [out_tile, in_pair, waves]
    specs = [ANY] * count + [VMEM] * 3
    if last:
        operands += [prev, phase.reshape(1, -1)]
        specs += [ANY, VMEM]
        shape = jax.ShapeDtypeStruct((4, width, width), BF16)
    else:
        shape = jax.ShapeDtypeStruct((2, 2 * width, width), F32)
    scratch = [pltpu.VMEM((2 * width, width), F32)] * 3
    scratch += [pltpu.VMEM((lanes, half_width), F32)] * 2
    scratch += [pltpu.VMEM((2 * width, depth), BF16)] * 6
    scratch += [pltpu.VMEM((depth, width), BF16)] * 6
    scratch += [pltpu.VMEM((half_width, depth), BF16)] * 4
    scratch += [pltpu.VMEM((count, half_width, spheres), BF16)] * 2
    scratch += [pltpu.VMEM((count,) + blocks[0].shape, BF16)]
    scratch += [pltpu.SemaphoreType.DMA((count,))]
    if last:
        scratch += [pltpu.VMEM((2, 2 * width, width), F32), pltpu.SemaphoreType.DMA]
    flops = count * 3 * 2 * 2 * width * width * depth
    return pl.pallas_call(
        functools.partial(layer_kernel, count, spheres, multi, last),
        out_shape=shape,
        in_specs=specs,
        out_specs=VMEM,
        scratch_shapes=scratch,
        compiler_params=pltpu.CompilerParams(vmem_limit_bytes=40 * 2**20),
        cost_estimate=pl.CostEstimate(flops=flops, bytes_accessed=2**23, transcendentals=0),
        name="layer_sum",
    )(*operands)


def take_pair(place, own, other, u, v, sems):
    def take(to, source, at):
        return pltpu.make_async_copy(source, to, sems.at[at])

    @pl.when(place[0] == 1)
    def _():
        take(u, own, 0).start()
        take(v, other, 1).start()

    @pl.when(place[0] == 0)
    def _():
        take(u, other, 0).start()
        take(v, own, 1).start()

    take(u, own, 0).wait()
    take(v, own, 1).wait()
    return (u[0], u[1]), (u[2], u[3]), (v[0], v[1]), (v[2], v[3])


def back_kernel(place, own, other, s_out, s_send, u, v, sems):
    side = own.shape[1] // 2
    r_u, t_u, r_v, _ = take_pair(place, own, other, u, v, sems)
    mine = pl.ds(pl.multiple_of(place[1] * side, side), side)
    base = (u[2, :, mine], u[3, :, mine])
    up = cmul(r_v, base)
    again = cmul(r_u, half(up))
    again = cmul(r_v, half(again))
    up = half(add(up, again))
    back = cmul(t_u, up)
    for c in range(2):
        s_out[c] = (u[c, :, mine].astype(F32) + back[c]).astype(BF16)
        s_send[c] = s_out[c, pl.ds(pl.multiple_of(place[4] * side, side), side), :]


def rows_kernel(rows, place, own, other, after, h_near, h_far, u, v, sems):
    del after
    width = own.shape[1]
    quarter = width // 4
    core = place[1]
    r_u, t_u, r_v, _ = take_pair(place, own, other, u, v, sems)
    near = pl.ds(pl.multiple_of(core * quarter, quarter), quarter)
    far = pl.ds(pl.multiple_of((core + 2) * quarter, quarter), quarter)

    def columns(ref, at):
        return jnp.concatenate([ref[at, :, near], ref[at, :, far]], axis=1)

    base = (columns(v, 2), columns(v, 3))
    chain = cmul(r_u, base)
    chain = cmul(r_v, half(chain))
    chain = half((base[0] + chain[0], base[1] + chain[1]))
    here = cmul(t_u, chain)
    my = pl.ds(pl.multiple_of(place[2] * rows, rows), rows)
    row_t = (v[2, my, :], v[3, my, :])
    w_1 = half(cmul(row_t, r_u))
    k_part = cmul(w_1, chain)
    w_2 = cmul(w_1, r_v)
    w_2 = half((row_t[0] + w_2[0], row_t[1] + w_2[1]))
    g_rows = half(cmul(w_2, t_u))
    for side, (to, cols) in enumerate(((h_near, near), (h_far, far))):
        at = slice(side * quarter, (side + 1) * quarter)
        for c in range(2):
            to[c, 0:width, :] = here[c][:, at].astype(BF16)
            k_side = v[c, my, cols].astype(F32) + k_part[c][:, at]
            to[c, width : width + rows, :] = k_side.astype(BF16)
            for q in range(4):
                put = width + rows + q * rows
                to[c, put : put + rows, :] = g_rows[c][:, q * quarter : (q + 1) * quarter]


def form(place, own, other, rows):
    width = own.shape[1]
    scratch = [pltpu.VMEM(own.shape, BF16)] * 2 + [pltpu.SemaphoreType.DMA((2,))]
    params = pltpu.CompilerParams(vmem_limit_bytes=24 * 2**20)
    back, send = pl.pallas_call(
        back_kernel,
        out_shape=(
            jax.ShapeDtypeStruct((2, width, width // 2), BF16),
            jax.ShapeDtypeStruct((2, width // 2, width // 2), BF16),
        ),
        in_specs=[SMEM, ANY, ANY],
        out_specs=(VMEM, VMEM),
        scratch_shapes=scratch,
        compiler_params=params,
        cost_estimate=pl.CostEstimate(flops=2**32, bytes_accessed=2**23, transcendentals=0),
        name="back",
    )(place, own, other)
    shape = jax.ShapeDtypeStruct((2, width + 5 * rows, width // 4), BF16)
    near, far = pl.pallas_call(
        functools.partial(rows_kernel, rows),
        out_shape=(shape, shape),
        in_specs=[SMEM, ANY, ANY, ANY],
        out_specs=(VMEM, VMEM),
        scratch_shapes=scratch,
        compiler_params=params,
        cost_estimate=pl.CostEstimate(flops=2**32, bytes_accessed=2**23, transcendentals=0),
        name="rows",
    )(place, own, other, back)
    return back, send, near, far


def join_kernel(
    rows, place, s_mine, s_side, q_0, q_1, q_2, q_3, h_near, h_sent, refl, trans, sides, h, sems
):
    width = sides.shape[3]
    lower, core = place[3], place[1]
    many = width // 2
    this = pl.ds(pl.multiple_of(place[4] * many, many), many)
    that = pl.ds(pl.multiple_of((1 - place[4]) * many, many), many)
    moves = (
        (s_mine, sides.at[lower, core]),
        (s_side, sides.at[lower, 1 - core]),
        (q_0, sides.at[1 - lower, core, :, this, :]),
        (q_1, sides.at[1 - lower, core, :, that, :]),
        (q_2, sides.at[1 - lower, 1 - core, :, this, :]),
        (q_3, sides.at[1 - lower, 1 - core, :, that, :]),
        (h_near, h.at[lower]),
        (h_sent, h.at[1 - lower]),
    )
    copies = [pltpu.make_async_copy(*move, sems.at[at]) for at, move in enumerate(moves)]
    for copy in copies:
        copy.start()
    for copy in copies:
        copy.wait()

    def rows_of(side):
        return tuple(
            jnp.concatenate(
                [
                    h[side, c, width + rows + q * rows : width + 2 * rows + q * rows, :]
                    for q in range(4)
                ],
                axis=1,
            )
            for c in range(2)
        )

    def times(pair, side):
        parts = [
            cmul(pair, (sides[side, at, 0], sides[side, at, 1]))
            for at in range(2)
        ]
        return tuple(jnp.concatenate([parts[0][c], parts[1][c]], axis=1) for c in range(2))

    from_above = rows_of(0)
    from_below = rows_of(1)
    second = half(times(from_above, 1))
    both = tuple(jnp.concatenate([from_below[c], second[c]], axis=0) for c in range(2))
    chain = times(half(times(both, 0)), 1)
    chain = half(tuple(both[c].astype(F32) + chain[c] for c in range(2)))
    result = cmul(chain, (h[0, 0, 0:width, :], h[0, 1, 0:width, :]))
    for c in range(2):
        trans[c] = result[c][0:rows]
        refl[c] = h[0, c, width : width + rows, :].astype(F32) + result[c][rows : 2 * rows]


def join(place, s_mine, s_side, quarters, h_near, h_sent, rows):
    columns = h_near.shape[2]
    shape = jax.ShapeDtypeStruct((2, rows, columns), F32)
    return pl.pallas_call(
        functools.partial(join_kernel, rows),
        out_shape=(shape, shape),
        in_specs=[SMEM] + [ANY] * 8,
        out_specs=(VMEM, VMEM),
        scratch_shapes=[
            pltpu.VMEM((2, 2) + s_mine.shape, BF16),
            pltpu.VMEM((2,) + h_near.shape, BF16),
            pltpu.SemaphoreType.DMA((8,)),
        ],
        compiler_params=pltpu.CompilerParams(vmem_limit_bytes=20 * 2**20),
        cost_estimate=pl.CostEstimate(flops=2**30, bytes_accessed=2**22, transcendentals=0),
        name="join",
    )(place, s_mine, s_side, *quarters, h_near, h_sent)


def whole_layers(inner, out_basis, in_basis, tmatrix, sites, waves, layer_phase):
    spheres, multi = tmatrix.shape[1], tmatrix.shape[3]
    half_width = waves.shape[1]
    width = 2 * half_width
    groups = lax.axis_size("sph")
    outer = groups // inner
    rows = width // groups
    layer = lax.axis_index("layer")

    block = pack(tmatrix[0], sites)

    def shifted(value, far, side):
        pairs = [
            (g, ((g // inner + far) % outer) * inner + (g % inner + side) % inner)
            for g in range(groups)
        ]
        return lax.ppermute(value, "sph", pairs)

    near = [shifted(block, 0, 1), shifted(block, 1, 0), shifted(block, outer - 1, 0)]
    near = [block, *near]
    tile, pair, waves_pad = prepare(out_basis[0], in_basis[0], waves, spheres)
    late, waves_pad = lax.optimization_barrier((block, waves_pad))
    ready = (tile, pair, waves_pad)
    far = [shifted(late, 2, 0), shifted(near[2], 0, 1), shifted(near[3], 0, 1)]
    far += [shifted(late, 2, 1)]

    part = layer_sum(near, spheres, multi, *ready)
    own = layer_sum(far, spheres, multi, *ready, part, layer_phase[0])

    other = lax.ppermute(own, "layer", [(at, at ^ 1) for at in range(4)])
    core, lower = layer % 2, layer // 2
    mine_is_u = jnp.where(core != lower, 1, 0)
    group = lax.axis_index("sph")
    side = group % inner
    place = jnp.stack([mine_is_u, core, group, lower, side]).astype(jnp.int32)
    s_mine, s_send, h_near, h_far = form(place, own, other, rows)

    def crossed(value, bit):
        return lax.ppermute(value, "layer", [(at, at ^ bit) for at in range(4)])

    s_far = crossed(s_send, 2)
    h_sent = crossed(h_far, 2)
    s_side = crossed(s_mine, 1)
    s_far, h_near = lax.optimization_barrier((s_far, h_near))
    s_next = shifted(s_far, 0, 1)
    quarters = (s_far, s_next, crossed(s_far, 1), crossed(s_next, 1))
    return join(place, s_mine, s_side, quarters, h_near, h_sent, rows)


def solution(mesh):
    in_specs = (
        P("layer", None, None, None, None),
        P("layer", None, None, None),
        P("layer", "sph", None, None, None),
        P("layer", "sph"),
        P(),
        P("layer", None),
    )
    out_specs = (P(None, "sph", "layer"), P(None, "sph", "layer"))
    on_device = by_rows
    if mesh.shape["layer"] == 4 and mesh.shape["sph"] == 8:
        on_device = functools.partial(whole_layers, 2)
    return jax.shard_map(
        on_device, mesh=mesh, in_specs=in_specs, out_specs=out_specs, check_vma=False
    )
```

```python
import functools
import math

import jax
import jax.numpy as jnp
from jax import lax
from jax.experimental import pallas as pl
from jax.experimental.pallas import tpu as pltpu
from jax.sharding import PartitionSpec as P

LATTICE = 32
TWO_PI = 2.0 * math.pi
F32 = jnp.float32
BF16 = jnp.bfloat16
VMEM = pl.BlockSpec(memory_space=pltpu.VMEM)
ANY = pl.BlockSpec(memory_space=pl.ANY)
SMEM = pl.BlockSpec(memory_space=pltpu.SMEM)
EXTRA = 16


def partner_2(value, axis, bit):
    mask = 2**bit
    pairs = [(source, source ^ mask) for source in range(lax.axis_size(axis))]
    return lax.ppermute(value, axis, pairs)


def wave_angles(site_list, waves):
    column = site_list // LATTICE
    along = site_list % LATTICE
    phase_index = (
        waves[0][None, :] * column[:, None] + waves[1][None, :] * along[:, None]
    ) % LATTICE
    angles = phase_index.astype(jnp.float32) * (TWO_PI / LATTICE)
    return jnp.concatenate([angles, angles], axis=1)


def factors(out_layer, in_layer, tm_layer, angles):
    highest = lax.Precision.HIGHEST
    basis_re = out_layer[:, 0]
    basis_im = out_layer[:, 1]
    tmat_re = tm_layer[:, 0]
    tmat_im = tm_layer[:, 1]
    prod_re = jnp.einsum("kjw,sjm->ksmw", basis_re, tmat_re, precision=highest) - jnp.einsum(
        "kjw,sjm->ksmw", basis_im, tmat_im, precision=highest
    )
    prod_im = jnp.einsum("kjw,sjm->ksmw", basis_re, tmat_im, precision=highest) + jnp.einsum(
        "kjw,sjm->ksmw", basis_im, tmat_re, precision=highest
    )
    cosine = jnp.cos(angles)
    sine = jnp.sin(angles)
    left_re = prod_re * cosine[None, :, None, :] - prod_im * sine[None, :, None, :]
    left_im = prod_re * sine[None, :, None, :] + prod_im * cosine[None, :, None, :]
    right_re = in_layer[0][None] * cosine[:, None, :] + in_layer[1][None] * sine[:, None, :]
    right_im = in_layer[1][None] * cosine[:, None, :] - in_layer[0][None] * sine[:, None, :]
    inner = left_re.shape[1] * left_re.shape[2]
    width = left_re.shape[3]
    left_re = left_re.reshape(2, inner, width)
    left_im = left_im.reshape(2, inner, width)
    right_re = right_re.reshape(inner, width)
    right_im = right_im.reshape(inner, width)
    real_left = jnp.concatenate([left_re, -left_im], axis=1)
    imag_left = jnp.concatenate([left_re, left_im], axis=1)
    real_right = jnp.concatenate([right_re, right_im], axis=0)
    imag_right = jnp.concatenate([right_im, right_re], axis=0)
    return (real_left, imag_left, real_right, imag_right)


def project_rows(factor_set):
    real_left, imag_left, real_right, imag_right = factor_set
    highest = lax.Precision.HIGHEST
    pieces = []
    for kind in range(2):
        real_slice = real_left[kind]
        imag_slice = imag_left[kind]
        pieces.append(jnp.einsum("kr,kw->rw", real_slice, real_right, precision=highest))
        pieces.append(jnp.einsum("kr,kw->rw", imag_slice, imag_right, precision=highest))
    return jnp.concatenate(pieces, axis=1)


def narrow(matrix):
    return matrix.astype(jnp.bfloat16)


def complex_product(left, right):
    left_half = narrow(left)
    right_half = narrow(right)
    real_part = jnp.dot(left_half[0], right_half[0], preferred_element_type=jnp.float32) - jnp.dot(
        left_half[1], right_half[1], preferred_element_type=jnp.float32
    )
    imag_part = jnp.dot(left_half[0], right_half[1], preferred_element_type=jnp.float32) + jnp.dot(
        left_half[1], right_half[0], preferred_element_type=jnp.float32
    )
    return jnp.stack([real_part, imag_part])


def merge_level(state, bit):
    partner = partner_2(state.astype(jnp.bfloat16), "layer", bit).astype(state.dtype)
    is_upper = lax.axis_index("layer") // (1 << bit) % 2 == 0
    upper = jnp.where(is_upper, state, partner)
    lower = jnp.where(is_upper, partner, state)
    refl_a, trans_a, refl_a_back, trans_a_back = (upper[0], upper[1], upper[2], upper[3])
    refl_b, trans_b, refl_b_back, trans_b_back = (lower[0], lower[1], lower[2], lower[3])
    first_left = jnp.where(is_upper, refl_a_back, refl_b)
    first_right = jnp.where(is_upper, refl_b, refl_a_back)
    chain_base = jnp.where(is_upper, trans_a, trans_b_back)
    across = jnp.where(is_upper, trans_b, trans_a_back)
    final_left = jnp.where(is_upper, trans_a_back, trans_b)
    addend = jnp.where(is_upper, refl_a, refl_b_back)
    full_right, full_base = (
        lax.all_gather(narrow(first_right), "sph", axis=1, tiled=True),
        lax.all_gather(narrow(chain_base), "sph", axis=1, tiled=True),
    )
    first_mix = complex_product(first_left, full_right)
    chain = chain_base + complex_product(first_mix, full_base)
    full_chain = lax.all_gather(narrow(chain), "sph", axis=1, tiled=True)
    bounce = complex_product(first_right, full_chain)
    own_trans = complex_product(across, full_chain)
    full_bounce = lax.all_gather(narrow(bounce), "sph", axis=1, tiled=True)
    own_refl = addend + complex_product(final_left, full_bounce)
    mine = jnp.stack([own_trans, own_refl])
    theirs = partner_2(mine.astype(jnp.bfloat16), "layer", bit).astype(mine.dtype)
    trans_new = jnp.where(is_upper, mine[0], theirs[0])
    refl_new = jnp.where(is_upper, mine[1], theirs[1])
    trans_back_new = jnp.where(is_upper, theirs[0], mine[0])
    refl_back_new = jnp.where(is_upper, theirs[1], mine[1])
    return jnp.stack([refl_new, trans_new, refl_back_new, trans_back_new])


def by_rows(out_basis, in_basis, tmatrix, sites, waves, layer_phase):
    width = 2 * waves.shape[1]
    rows = width // lax.axis_size("sph")
    angles = wave_angles(sites[0], waves)
    factor_set = factors(out_basis[0], in_basis[0], tmatrix[0], angles)
    summed = lax.psum_scatter(
        project_rows(factor_set).astype(jnp.bfloat16), "sph", scatter_dimension=0, tiled=True
    ).astype(jnp.float32)
    first_row = lax.axis_index("sph") * rows
    diagonal = ((first_row + jnp.arange(rows))[:, None] == jnp.arange(width)[None, :]).astype(
        jnp.float32
    )
    refl = jnp.stack([summed[:, :width], summed[:, width : 2 * width]])
    trans_re = summed[:, 2 * width : 3 * width] + diagonal * jnp.cos(layer_phase[0])[None, :]
    trans_im = summed[:, 3 * width :] + diagonal * jnp.sin(layer_phase[0])[None, :]
    trans = jnp.stack([trans_re, trans_im])
    state = jnp.stack([refl, trans, refl, trans])
    levels = lax.axis_size("layer").bit_length() - 1
    for bit in range(levels):
        state = merge_level(state, bit)
    columns = width // lax.axis_size("layer")
    first_column = lax.axis_index("layer") * columns
    own_refl = lax.dynamic_slice_in_dim(state[0], first_column, columns, 2)
    own_trans = lax.dynamic_slice_in_dim(state[1], first_column, columns, 2)
    return (own_refl, own_trans)


def mm(left, right):
    return jnp.dot(left, right, preferred_element_type=F32)


def mm_t(left, right):
    return lax.dot_general(left, right, (((0,), (0,)), ((), ())), preferred_element_type=F32)


def cmul(left, right):
    return (
        mm(left[0], right[0]) - mm(left[1], right[1]),
        mm(left[0], right[1]) + mm(left[1], right[0]),
    )


def half(pair):
    return (pair[0].astype(BF16), pair[1].astype(BF16))


def add(one, two):
    return (one[0] + two[0], one[1] + two[1])


def circle(turns):
    turn = turns * (1.0 / LATTICE)
    turn = turn - jnp.floor(turn)
    quarter = jnp.floor(turn * 4.0 + 0.5)
    x = (turn - quarter * 0.25) * TWO_PI
    y = x * x
    sin = x * (1.0 + y * (-1.0 / 6 + y * (1.0 / 120 + y * (-1.0 / 5040 + y * (1.0 / 362880)))))
    cos = 1.0 + y * (-0.5 + y * (1.0 / 24 + y * (-1.0 / 720 + y * (1.0 / 40320))))
    odd = (quarter == 1.0) | (quarter == 3.0)
    cos, sin = jnp.where(odd, sin, cos), jnp.where(odd, cos, sin)
    cos = jnp.where((quarter == 1.0) | (quarter == 2.0), -cos, cos)
    sin = jnp.where((quarter == 2.0) | (quarter == 3.0), -sin, sin)
    return cos, sin


def layer_kernel(count, spheres, multi, last, *refs):
    sent = refs[:count]
    rest = list(refs[count:])
    out_tile, in_pair, waves = rest[:3]
    rest = rest[3:]
    if last:
        prev_hbm, phase_row = rest[:2]
        rest = rest[2:]
    out = rest[0]
    rest = rest[1:]
    sum_1, sum_2, sum_3, cos_t, sin_t = rest[:5]
    left_slots = (rest[5:8], rest[8:11])
    right_slots = (rest[11:14], rest[14:17])
    spread_slots = (rest[17:19], rest[19:21])
    cos_s, sin_s, blocks_here, block_sem = rest[21:25]
    blocks = [blocks_here.at[index] for index in range(count)]
    copies = [
        pltpu.make_async_copy(sent[index], blocks_here.at[index], block_sem.at[index])
        for index in range(count)
    ]
    for copy in copies:
        copy.start()
    if last:
        prev, arrived = rest[25:]
        fetch = pltpu.make_async_copy(prev_hbm, prev, arrived)
        fetch.start()
    depth = spheres * multi
    half_width = waves.shape[1]
    width = 2 * half_width
    lanes = max(128, count * spheres)
    parts = 1
    tall = 2 * width // parts
    few, size = spheres // parts, depth // parts

    for copy in copies:
        copy.wait()
    coords = None
    for index, block in enumerate(blocks):
        row = lax.broadcasted_iota(jnp.int32, (depth, lanes), 0)
        lane = lax.broadcasted_iota(jnp.int32, (depth, lanes), 1)
        pick = (row == (lane - spheres * index) * multi).astype(F32).astype(BF16)
        part = mm(block[2 * multi : 2 * multi + EXTRA, :], pick)
        coords = part if coords is None else coords + part
    turns = mm_t(waves[...], coords.astype(BF16))
    cos_v, sin_v = circle(turns)
    for index in range(count):
        at = slice(spheres * index, spheres * (index + 1))
        cos_s[index] = cos_v[:, at].astype(BF16)
        sin_s[index] = sin_v[:, at].astype(BF16)
        cos_t[index] = cos_v.T[at, :]
        sin_t[index] = sin_v.T[at, :]
    row = lax.broadcasted_iota(jnp.int32, (spheres, depth), 0)
    lane = lax.broadcasted_iota(jnp.int32, (spheres, depth), 1)
    inside = (lane >= row * multi) & (lane < row * multi + multi)
    pick_s = inside.astype(F32).astype(BF16)

    def spread(slot, index, at, many):
        rows = pl.ds(at, many)
        slot[0][rows, :] = mm(cos_s[index, rows, :], pick_s).astype(BF16)
        slot[1][rows, :] = mm(sin_s[index, rows, :], pick_s).astype(BF16)

    def build_left(slot, phases, part, piece):
        low = (piece * tall // 8) % half_width
        many = tall // 8
        c, s = phases[0][low : low + many, :], phases[1][low : low + many, :]
        rows = pl.ds(part * tall + piece * many, many)
        u_re = out_tile[0, rows, :]
        u_im = out_tile[1, rows, :]
        re = u_re * c - u_im * s
        im = u_re * s + u_im * c
        slot[0][rows, :] = re
        slot[1][rows, :] = im
        slot[2][rows, :] = re + im

    def build_right(slot, index, part, piece):
        many = size // 6
        base = part * size + piece * many
        both = mm_t(
            blocks_here[index, 0 : 2 * multi, pl.ds(base, many)], in_pair[...]
        )
        done = 0
        while done < many:
            k = (piece * many + done) // multi
            stop = min((k + 1) * multi - piece * many, many)
            at = part * few + k
            c = cos_t[index, at : at + 1, :]
            s = sin_t[index, at : at + 1, :]
            to = pl.ds(base + done, stop - done)
            for pol in range(2):
                lo = pol * half_width
                g_re = both[done:stop, lo : lo + half_width]
                g_im = both[done:stop, width + lo : width + lo + half_width]
                re = g_re * c + g_im * s
                im = g_im * c - g_re * s
                slot[0][to, lo : lo + half_width] = re.astype(BF16)
                slot[1][to, lo : lo + half_width] = im.astype(BF16)
                slot[2][to, lo : lo + half_width] = (re + im).astype(BF16)
            done = stop

    def tasks_of(slot_left, phases, slot_right, index, part):
        lefts = [
            functools.partial(build_left, slot_left, phases, part, piece)
            for piece in range(8)
        ]
        rights = [
            functools.partial(build_right, slot_right, index, part, piece)
            for piece in range(6)
        ]
        tasks = []
        while lefts or rights:
            tasks += lefts[:1] + rights[:1]
            lefts, rights = lefts[1:], rights[1:]
        return tasks

    spread(spread_slots[0], 0, 0, half_width)
    if count > 1:
        spread(spread_slots[1], 1, 0, half_width)

    for task in tasks_of(left_slots[0], spread_slots[0], right_slots[0], 0, 0):
        task()
    for pair in range(count // 2):
        for now in range(2):
            later = 1 - now
            index = 2 * pair + now
            after = index + 1
            tasks = []
            if after < count:
              tasks = tasks_of(left_slots[later], spread_slots[later], right_slots[later], after, 0)
            after = index + 2
            if after < count:
              tasks.append(functools.partial(spread, spread_slots[now], after, 0, half_width))
            pieces = [
                (total, left, right, slice(lane * 256, (lane + 1) * 256))
                for total, left, right in zip(
                    (sum_1, sum_2, sum_3), left_slots[now], right_slots[now]
                )
                for lane in range(width // 256)
            ]
            for at, (total, left, right, cols) in enumerate(pieces):
                before = total[:, cols]
                product = mm(left[...], right[:, cols])
                total[:, cols] = product if index == 0 else before + product
                share = -(-len(tasks) // (len(pieces) - at))
                for task in tasks[:share]:
                    task()
                tasks = tasks[share:]

    if last:
        fetch.wait()
    for part in range(4):
        kind, pol = part // 2, part % 2
        rows = pl.ds(part * half_width, half_width)
        re = sum_1[rows, :] - sum_2[rows, :]
        im = sum_3[rows, :] - sum_1[rows, :] - sum_2[rows, :]
        if not last:
            out[0, rows, :] = re
            out[1, rows, :] = im
        else:
            re = re + prev[0, rows, :]
            im = im + prev[1, rows, :]
            if kind == 1:
                at = lax.broadcasted_iota(jnp.int32, (half_width, width), 0) + pol * half_width
                lane = lax.broadcasted_iota(jnp.int32, (half_width, width), 1)
                on = at == lane
                re = re + jnp.where(on, jnp.cos(phase_row[...]), 0.0)
                im = im + jnp.where(on, jnp.sin(phase_row[...]), 0.0)
            to = pl.ds(pol * half_width, half_width)
            out[2 * kind, to, :] = re.astype(BF16)
            out[2 * kind + 1, to, :] = im.astype(BF16)


def pack_kernel(tmatrix, sites, out):
    spheres, _, multi, _ = tmatrix.shape
    depth = spheres * multi
    for c in range(2):
        flat = tmatrix[:, c].reshape(depth, multi)
        out[c * multi : (c + 1) * multi, :] = flat.T.astype(BF16)
    row = lax.broadcasted_iota(jnp.int32, (spheres, depth), 0)
    lane = lax.broadcasted_iota(jnp.int32, (spheres, depth), 1)
    inside = (lane >= row * multi) & (lane < row * multi + multi)
    pick = inside.astype(F32).astype(BF16)
    site = sites[...].astype(F32)
    column = jnp.floor((site + 0.5) * (1.0 / LATTICE))
    along = site - LATTICE * column
    both = jnp.concatenate([column, along, jnp.zeros((EXTRA - 2, spheres), F32)], axis=0)
    out[2 * multi : 2 * multi + EXTRA, :] = mm(both.astype(BF16), pick).astype(BF16)


def pack(tmatrix, sites):
    spheres, _, multi, _ = tmatrix.shape
    return pl.pallas_call(
        pack_kernel,
        out_shape=jax.ShapeDtypeStruct((2 * multi + EXTRA, spheres * multi), BF16),
        in_specs=[VMEM, VMEM],
        out_specs=VMEM,
        name="pack",
    )(tmatrix, sites)


def prepare_kernel(depth, out_basis, in_basis, waves, out_tile, in_pair, waves_pad):
    multi, width = in_basis.shape[1], in_basis.shape[2]
    row = lax.broadcasted_iota(jnp.int32, (multi, depth), 0).astype(F32)
    lane = lax.broadcasted_iota(jnp.int32, (multi, depth), 1).astype(F32)
    lane = lane - multi * jnp.floor((lane + 0.5) * (1.0 / multi))
    pick = (row == lane).astype(F32).astype(BF16)
    for kind in range(2):
        for c in range(2):
            tile = mm_t(out_basis[kind, c].astype(BF16), pick)
            out_tile[c, kind * width : (kind + 1) * width, :] = tile.astype(BF16)
    b_re, b_im = in_basis[0].astype(BF16), in_basis[1].astype(BF16)
    in_pair[0:multi, 0:width] = b_re
    in_pair[0:multi, width : 2 * width] = b_im
    in_pair[multi : 2 * multi, 0:width] = -b_im
    in_pair[multi : 2 * multi, width : 2 * width] = b_re
    pads = jnp.zeros((EXTRA - 2, width // 2), F32)
    waves_pad[...] = jnp.concatenate([waves[...].astype(F32), pads], axis=0).astype(BF16)


def prepare(out_basis, in_basis, waves, spheres):
    multi, width = in_basis.shape[1], in_basis.shape[2]
    depth = spheres * multi
    return pl.pallas_call(
        functools.partial(prepare_kernel, depth),
        out_shape=(
            jax.ShapeDtypeStruct((2, 2 * width, depth), BF16),
            jax.ShapeDtypeStruct((2 * multi, 2 * width), BF16),
            jax.ShapeDtypeStruct((EXTRA, width // 2), BF16),
        ),
        in_specs=[VMEM] * 3,
        out_specs=(VMEM,) * 3,
        compiler_params=pltpu.CompilerParams(vmem_limit_bytes=16 * 2**20),
        cost_estimate=pl.CostEstimate(flops=2**31, bytes_accessed=2**22, transcendentals=0),
        name="prepare",
    )(out_basis, in_basis, waves)


def layer_sum(blocks, spheres, multi, out_tile, in_pair, waves, prev=None, phase=None):
    count = len(blocks)
    last = prev is not None
    depth = spheres * multi
    half_width = waves.shape[1]
    width = 2 * half_width
    operands = list(blocks) + [out_tile, in_pair, waves]
    specs = [ANY] * count + [VMEM] * 3
    if last:
        operands += [prev, phase.reshape(1, -1)]
        specs += [ANY, VMEM]
        shape = jax.ShapeDtypeStruct((4, width, width), BF16)
    else:
        shape = jax.ShapeDtypeStruct((2, 2 * width, width), F32)
    scratch = [pltpu.VMEM((2 * width, width), F32)] * 3
    scratch += [pltpu.VMEM((count, spheres, half_width), F32)] * 2
    scratch += [pltpu.VMEM((2 * width, depth), BF16)] * 6
    scratch += [pltpu.VMEM((depth, width), BF16)] * 6
    scratch += [pltpu.VMEM((half_width, depth), BF16)] * 4
    scratch += [pltpu.VMEM((count, half_width, spheres), BF16)] * 2
    scratch += [pltpu.VMEM((count,) + blocks[0].shape, BF16)]
    scratch += [pltpu.SemaphoreType.DMA((count,))]
    if last:
        scratch += [pltpu.VMEM((2, 2 * width, width), F32), pltpu.SemaphoreType.DMA]
    flops = count * 3 * 2 * 2 * width * width * depth
    return pl.pallas_call(
        functools.partial(layer_kernel, count, spheres, multi, last),
        out_shape=shape,
        in_specs=specs,
        out_specs=VMEM,
        scratch_shapes=scratch,
        compiler_params=pltpu.CompilerParams(vmem_limit_bytes=40 * 2**20),
        cost_estimate=pl.CostEstimate(flops=flops, bytes_accessed=2**23, transcendentals=0),
        name="layer_sum",
    )(*operands)


def take_pair(place, own, other, u, v, sems):
    def take(to, source, at):
        return pltpu.make_async_copy(source, to, sems.at[at])

    @pl.when(place[0] == 1)
    def _():
        take(u, own, 0).start()
        take(v, other, 1).start()

    @pl.when(place[0] == 0)
    def _():
        take(u, other, 0).start()
        take(v, own, 1).start()

    take(u, own, 0).wait()
    take(v, own, 1).wait()
    return (u[0], u[1]), (u[2], u[3]), (v[0], v[1]), (v[2], v[3])


def back_kernel(place, own, other, s_out, s_send, u, v, sems):
    side = own.shape[1] // 2
    r_u, t_u, r_v, _ = take_pair(place, own, other, u, v, sems)
    mine = pl.ds(pl.multiple_of(place[1] * side, side), side)
    base = (u[2, :, mine], u[3, :, mine])
    up = cmul(r_v, base)
    again = cmul(r_u, half(up))
    again = cmul(r_v, half(again))
    up = half(add(up, again))
    back = cmul(t_u, up)
    for c in range(2):
        s_out[c] = (u[c, :, mine].astype(F32) + back[c]).astype(BF16)
        s_send[c] = s_out[c, pl.ds(pl.multiple_of(place[4] * side, side), side), :]


def rows_kernel(rows, place, own, other, after, h_near, h_far, u, v, sems):
    del after
    width = own.shape[1]
    quarter = width // 4
    core = place[1]
    r_u, t_u, r_v, _ = take_pair(place, own, other, u, v, sems)
    near = pl.ds(pl.multiple_of(core * quarter, quarter), quarter)
    far = pl.ds(pl.multiple_of((core + 2) * quarter, quarter), quarter)

    def columns(ref, at):
        return jnp.concatenate([ref[at, :, near], ref[at, :, far]], axis=1)

    base = (columns(v, 2), columns(v, 3))
    chain = cmul(r_u, base)
    chain = cmul(r_v, half(chain))
    chain = half((base[0] + chain[0], base[1] + chain[1]))
    here = cmul(t_u, chain)
    my = pl.ds(pl.multiple_of(place[2] * rows, rows), rows)
    row_t = (v[2, my, :], v[3, my, :])
    w_1 = half(cmul(row_t, r_u))
    k_part = cmul(w_1, chain)
    w_2 = cmul(w_1, r_v)
    w_2 = half((row_t[0] + w_2[0], row_t[1] + w_2[1]))
    g_rows = half(cmul(w_2, t_u))
    for side, (to, cols) in enumerate(((h_near, near), (h_far, far))):
        at = slice(side * quarter, (side + 1) * quarter)
        for c in range(2):
            to[c, 0:width, :] = here[c][:, at].astype(BF16)
            k_side = v[c, my, cols].astype(F32) + k_part[c][:, at]
            to[c, width : width + rows, :] = k_side.astype(BF16)
            for q in range(4):
                put = width + rows + q * rows
                to[c, put : put + rows, :] = g_rows[c][:, q * quarter : (q + 1) * quarter]


def form(place, own, other, rows):
    width = own.shape[1]
    scratch = [pltpu.VMEM(own.shape, BF16)] * 2 + [pltpu.SemaphoreType.DMA((2,))]
    params = pltpu.CompilerParams(vmem_limit_bytes=24 * 2**20)
    back, send = pl.pallas_call(
        back_kernel,
        out_shape=(
            jax.ShapeDtypeStruct((2, width, width // 2), BF16),
            jax.ShapeDtypeStruct((2, width // 2, width // 2), BF16),
        ),
        in_specs=[SMEM, ANY, ANY],
        out_specs=(VMEM, VMEM),
        scratch_shapes=scratch,
        compiler_params=params,
        cost_estimate=pl.CostEstimate(flops=2**32, bytes_accessed=2**23, transcendentals=0),
        name="back",
    )(place, own, other)
    shape = jax.ShapeDtypeStruct((2, width + 5 * rows, width // 4), BF16)
    near, far = pl.pallas_call(
        functools.partial(rows_kernel, rows),
        out_shape=(shape, shape),
        in_specs=[SMEM, ANY, ANY, ANY],
        out_specs=(VMEM, VMEM),
        scratch_shapes=scratch,
        compiler_params=params,
        cost_estimate=pl.CostEstimate(flops=2**32, bytes_accessed=2**23, transcendentals=0),
        name="rows",
    )(place, own, other, back)
    return back, send, near, far


def join_kernel(
    rows, place, s_mine, s_side, q_0, q_1, q_2, q_3, h_near, h_sent, refl, trans, sides, h, sems
):
    width = sides.shape[3]
    lower, core = place[3], place[1]
    many = width // 2
    this = pl.ds(pl.multiple_of(place[4] * many, many), many)
    that = pl.ds(pl.multiple_of((1 - place[4]) * many, many), many)
    moves = (
        (s_mine, sides.at[lower, core]),
        (s_side, sides.at[lower, 1 - core]),
        (q_0, sides.at[1 - lower, core, :, this, :]),
        (q_1, sides.at[1 - lower, core, :, that, :]),
        (q_2, sides.at[1 - lower, 1 - core, :, this, :]),
        (q_3, sides.at[1 - lower, 1 - core, :, that, :]),
        (h_near, h.at[lower]),
        (h_sent, h.at[1 - lower]),
    )
    copies = [pltpu.make_async_copy(*move, sems.at[at]) for at, move in enumerate(moves)]
    for copy in copies:
        copy.start()
    for copy in copies:
        copy.wait()

    def rows_of(side):
        return tuple(
            jnp.concatenate(
                [
                    h[side, c, width + rows + q * rows : width + 2 * rows + q * rows, :]
                    for q in range(4)
                ],
                axis=1,
            )
            for c in range(2)
        )

    def times(pair, side):
        parts = [
            cmul(pair, (sides[side, at, 0], sides[side, at, 1]))
            for at in range(2)
        ]
        return tuple(jnp.concatenate([parts[0][c], parts[1][c]], axis=1) for c in range(2))

    from_above = rows_of(0)
    from_below = rows_of(1)
    second = half(times(from_above, 1))
    both = tuple(jnp.concatenate([from_below[c], second[c]], axis=0) for c in range(2))
    chain = times(half(times(both, 0)), 1)
    chain = half(tuple(both[c].astype(F32) + chain[c] for c in range(2)))
    result = cmul(chain, (h[0, 0, 0:width, :], h[0, 1, 0:width, :]))
    for c in range(2):
        trans[c] = result[c][0:rows]
        refl[c] = h[0, c, width : width + rows, :].astype(F32) + result[c][rows : 2 * rows]


def join(place, s_mine, s_side, quarters, h_near, h_sent, rows):
    columns = h_near.shape[2]
    shape = jax.ShapeDtypeStruct((2, rows, columns), F32)
    return pl.pallas_call(
        functools.partial(join_kernel, rows),
        out_shape=(shape, shape),
        in_specs=[SMEM] + [ANY] * 8,
        out_specs=(VMEM, VMEM),
        scratch_shapes=[
            pltpu.VMEM((2, 2) + s_mine.shape, BF16),
            pltpu.VMEM((2,) + h_near.shape, BF16),
            pltpu.SemaphoreType.DMA((8,)),
        ],
        compiler_params=pltpu.CompilerParams(vmem_limit_bytes=20 * 2**20),
        cost_estimate=pl.CostEstimate(flops=2**30, bytes_accessed=2**22, transcendentals=0),
        name="join",
    )(place, s_mine, s_side, *quarters, h_near, h_sent)


def whole_layers(inner, out_basis, in_basis, tmatrix, sites, waves, layer_phase):
    spheres, multi = tmatrix.shape[1], tmatrix.shape[3]
    half_width = waves.shape[1]
    width = 2 * half_width
    groups = lax.axis_size("sph")
    outer = groups // inner
    rows = width // groups
    layer = lax.axis_index("layer")

    block = pack(tmatrix[0], sites)

    def shifted(value, far, side):
        pairs = [
            (g, ((g // inner + far) % outer) * inner + (g % inner + side) % inner)
            for g in range(groups)
        ]
        return lax.ppermute(value, "sph", pairs)

    near = [shifted(block, 0, 1), shifted(block, 1, 0), shifted(block, outer - 1, 0)]
    near = [block, *near]
    tile, pair, waves_pad = prepare(out_basis[0], in_basis[0], waves, spheres)
    late, waves_pad = lax.optimization_barrier((block, waves_pad))
    ready = (tile, pair, waves_pad)
    far = [shifted(late, 2, 0), shifted(near[2], 0, 1), shifted(near[3], 0, 1)]
    far += [shifted(late, 2, 1)]

    part = layer_sum(near, spheres, multi, *ready)
    own = layer_sum(far, spheres, multi, *ready, part, layer_phase[0])

    other = lax.ppermute(own, "layer", [(at, at ^ 1) for at in range(4)])
    core, lower = layer % 2, layer // 2
    mine_is_u = jnp.where(core != lower, 1, 0)
    group = lax.axis_index("sph")
    side = group % inner
    place = jnp.stack([mine_is_u, core, group, lower, side]).astype(jnp.int32)
    s_mine, s_send, h_near, h_far = form(place, own, other, rows)

    def crossed(value, bit):
        return lax.ppermute(value, "layer", [(at, at ^ bit) for at in range(4)])

    s_far = crossed(s_send, 2)
    h_sent = crossed(h_far, 2)
    s_side = crossed(s_mine, 1)
    s_far, h_near = lax.optimization_barrier((s_far, h_near))
    s_next = shifted(s_far, 0, 1)
    quarters = (s_far, s_next, crossed(s_far, 1), crossed(s_next, 1))
    return join(place, s_mine, s_side, quarters, h_near, h_sent, rows)


def solution(mesh):
    in_specs = (
        P("layer", None, None, None, None),
        P("layer", None, None, None),
        P("layer", "sph", None, None, None),
        P("layer", "sph"),
        P(),
        P("layer", None),
    )
    out_specs = (P(None, "sph", "layer"), P(None, "sph", "layer"))
    on_device = by_rows
    if mesh.shape["layer"] == 4 and mesh.shape["sph"] == 8:
        on_device = functools.partial(whole_layers, 2)
    return jax.shard_map(
        on_device, mesh=mesh, in_specs=in_specs, out_specs=out_specs, check_vma=False
    )
```

```python
import functools
import math

import jax
import jax.numpy as jnp
from jax import lax
from jax.experimental import pallas as pl
from jax.experimental.pallas import tpu as pltpu
from jax.sharding import PartitionSpec as P

LATTICE = 32
TWO_PI = 2.0 * math.pi
F32 = jnp.float32
BF16 = jnp.bfloat16
VMEM = pl.BlockSpec(memory_space=pltpu.VMEM)
ANY = pl.BlockSpec(memory_space=pl.ANY)
SMEM = pl.BlockSpec(memory_space=pltpu.SMEM)
EXTRA = 16


def partner_2(value, axis, bit):
    mask = 2**bit
    pairs = [(source, source ^ mask) for source in range(lax.axis_size(axis))]
    return lax.ppermute(value, axis, pairs)


def wave_angles(site_list, waves):
    column = site_list // LATTICE
    along = site_list % LATTICE
    phase_index = (
        waves[0][None, :] * column[:, None] + waves[1][None, :] * along[:, None]
    ) % LATTICE
    angles = phase_index.astype(jnp.float32) * (TWO_PI / LATTICE)
    return jnp.concatenate([angles, angles], axis=1)


def factors(out_layer, in_layer, tm_layer, angles):
    highest = lax.Precision.HIGHEST
    basis_re = out_layer[:, 0]
    basis_im = out_layer[:, 1]
    tmat_re = tm_layer[:, 0]
    tmat_im = tm_layer[:, 1]
    prod_re = jnp.einsum("kjw,sjm->ksmw", basis_re, tmat_re, precision=highest) - jnp.einsum(
        "kjw,sjm->ksmw", basis_im, tmat_im, precision=highest
    )
    prod_im = jnp.einsum("kjw,sjm->ksmw", basis_re, tmat_im, precision=highest) + jnp.einsum(
        "kjw,sjm->ksmw", basis_im, tmat_re, precision=highest
    )
    cosine = jnp.cos(angles)
    sine = jnp.sin(angles)
    left_re = prod_re * cosine[None, :, None, :] - prod_im * sine[None, :, None, :]
    left_im = prod_re * sine[None, :, None, :] + prod_im * cosine[None, :, None, :]
    right_re = in_layer[0][None] * cosine[:, None, :] + in_layer[1][None] * sine[:, None, :]
    right_im = in_layer[1][None] * cosine[:, None, :] - in_layer[0][None] * sine[:, None, :]
    inner = left_re.shape[1] * left_re.shape[2]
    width = left_re.shape[3]
    left_re = left_re.reshape(2, inner, width)
    left_im = left_im.reshape(2, inner, width)
    right_re = right_re.reshape(inner, width)
    right_im = right_im.reshape(inner, width)
    real_left = jnp.concatenate([left_re, -left_im], axis=1)
    imag_left = jnp.concatenate([left_re, left_im], axis=1)
    real_right = jnp.concatenate([right_re, right_im], axis=0)
    imag_right = jnp.concatenate([right_im, right_re], axis=0)
    return (real_left, imag_left, real_right, imag_right)


def project_rows(factor_set):
    real_left, imag_left, real_right, imag_right = factor_set
    highest = lax.Precision.HIGHEST
    pieces = []
    for kind in range(2):
        real_slice = real_left[kind]
        imag_slice = imag_left[kind]
        pieces.append(jnp.einsum("kr,kw->rw", real_slice, real_right, precision=highest))
        pieces.append(jnp.einsum("kr,kw->rw", imag_slice, imag_right, precision=highest))
    return jnp.concatenate(pieces, axis=1)


def narrow(matrix):
    return matrix.astype(jnp.bfloat16)


def complex_product(left, right):
    left_half = narrow(left)
    right_half = narrow(right)
    real_part = jnp.dot(left_half[0], right_half[0], preferred_element_type=jnp.float32) - jnp.dot(
        left_half[1], right_half[1], preferred_element_type=jnp.float32
    )
    imag_part = jnp.dot(left_half[0], right_half[1], preferred_element_type=jnp.float32) + jnp.dot(
        left_half[1], right_half[0], preferred_element_type=jnp.float32
    )
    return jnp.stack([real_part, imag_part])


def merge_level(state, bit):
    partner = partner_2(state.astype(jnp.bfloat16), "layer", bit).astype(state.dtype)
    is_upper = lax.axis_index("layer") // (1 << bit) % 2 == 0
    upper = jnp.where(is_upper, state, partner)
    lower = jnp.where(is_upper, partner, state)
    refl_a, trans_a, refl_a_back, trans_a_back = (upper[0], upper[1], upper[2], upper[3])
    refl_b, trans_b, refl_b_back, trans_b_back = (lower[0], lower[1], lower[2], lower[3])
    first_left = jnp.where(is_upper, refl_a_back, refl_b)
    first_right = jnp.where(is_upper, refl_b, refl_a_back)
    chain_base = jnp.where(is_upper, trans_a, trans_b_back)
    across = jnp.where(is_upper, trans_b, trans_a_back)
    final_left = jnp.where(is_upper, trans_a_back, trans_b)
    addend = jnp.where(is_upper, refl_a, refl_b_back)
    full_right, full_base = (
        lax.all_gather(narrow(first_right), "sph", axis=1, tiled=True),
        lax.all_gather(narrow(chain_base), "sph", axis=1, tiled=True),
    )
    first_mix = complex_product(first_left, full_right)
    chain = chain_base + complex_product(first_mix, full_base)
    full_chain = lax.all_gather(narrow(chain), "sph", axis=1, tiled=True)
    bounce = complex_product(first_right, full_chain)
    own_trans = complex_product(across, full_chain)
    full_bounce = lax.all_gather(narrow(bounce), "sph", axis=1, tiled=True)
    own_refl = addend + complex_product(final_left, full_bounce)
    mine = jnp.stack([own_trans, own_refl])
    theirs = partner_2(mine.astype(jnp.bfloat16), "layer", bit).astype(mine.dtype)
    trans_new = jnp.where(is_upper, mine[0], theirs[0])
    refl_new = jnp.where(is_upper, mine[1], theirs[1])
    trans_back_new = jnp.where(is_upper, theirs[0], mine[0])
    refl_back_new = jnp.where(is_upper, theirs[1], mine[1])
    return jnp.stack([refl_new, trans_new, refl_back_new, trans_back_new])


def by_rows(out_basis, in_basis, tmatrix, sites, waves, layer_phase):
    width = 2 * waves.shape[1]
    rows = width // lax.axis_size("sph")
    angles = wave_angles(sites[0], waves)
    factor_set = factors(out_basis[0], in_basis[0], tmatrix[0], angles)
    summed = lax.psum_scatter(
        project_rows(factor_set).astype(jnp.bfloat16), "sph", scatter_dimension=0, tiled=True
    ).astype(jnp.float32)
    first_row = lax.axis_index("sph") * rows
    diagonal = ((first_row + jnp.arange(rows))[:, None] == jnp.arange(width)[None, :]).astype(
        jnp.float32
    )
    refl = jnp.stack([summed[:, :width], summed[:, width : 2 * width]])
    trans_re = summed[:, 2 * width : 3 * width] + diagonal * jnp.cos(layer_phase[0])[None, :]
    trans_im = summed[:, 3 * width :] + diagonal * jnp.sin(layer_phase[0])[None, :]
    trans = jnp.stack([trans_re, trans_im])
    state = jnp.stack([refl, trans, refl, trans])
    levels = lax.axis_size("layer").bit_length() - 1
    for bit in range(levels):
        state = merge_level(state, bit)
    columns = width // lax.axis_size("layer")
    first_column = lax.axis_index("layer") * columns
    own_refl = lax.dynamic_slice_in_dim(state[0], first_column, columns, 2)
    own_trans = lax.dynamic_slice_in_dim(state[1], first_column, columns, 2)
    return (own_refl, own_trans)


def mm(left, right):
    return jnp.dot(left, right, preferred_element_type=F32)


def mm_t(left, right):
    return lax.dot_general(left, right, (((0,), (0,)), ((), ())), preferred_element_type=F32)


def cmul(left, right):
    return (
        mm(left[0], right[0]) - mm(left[1], right[1]),
        mm(left[0], right[1]) + mm(left[1], right[0]),
    )


def half(pair):
    return (pair[0].astype(BF16), pair[1].astype(BF16))


def add(one, two):
    return (one[0] + two[0], one[1] + two[1])


def circle(turns):
    turn = turns * (1.0 / LATTICE)
    turn = turn - jnp.floor(turn)
    quarter = jnp.floor(turn * 4.0 + 0.5)
    x = (turn - quarter * 0.25) * TWO_PI
    y = x * x
    sin = x * (1.0 + y * (-1.0 / 6 + y * (1.0 / 120 + y * (-1.0 / 5040 + y * (1.0 / 362880)))))
    cos = 1.0 + y * (-0.5 + y * (1.0 / 24 + y * (-1.0 / 720 + y * (1.0 / 40320))))
    odd = (quarter == 1.0) | (quarter == 3.0)
    cos, sin = jnp.where(odd, sin, cos), jnp.where(odd, cos, sin)
    cos = jnp.where((quarter == 1.0) | (quarter == 2.0), -cos, cos)
    sin = jnp.where((quarter == 2.0) | (quarter == 3.0), -sin, sin)
    return cos, sin


def layer_kernel(count, spheres, multi, last, *refs):
    sent = refs[:count]
    rest = list(refs[count:])
    out_tile, in_pair, waves = rest[:3]
    rest = rest[3:]
    if last:
        prev_hbm, phase_row = rest[:2]
        rest = rest[2:]
    out = rest[0]
    rest = rest[1:]
    sum_1, sum_2, sum_3, cos_t, sin_t = rest[:5]
    left_slots = (rest[5:8], rest[8:11])
    right_slots = (rest[11:14], rest[14:17])
    spread_slots = (rest[17:19], rest[19:21])
    cos_s, sin_s, blocks_here, block_sem = rest[21:25]
    blocks = [blocks_here.at[index] for index in range(count)]
    copies = [
        pltpu.make_async_copy(sent[index], blocks_here.at[index], block_sem.at[index])
        for index in range(count)
    ]
    for copy in copies:
        copy.start()
    if last:
        prev, arrived = rest[25:]
        fetch = pltpu.make_async_copy(prev_hbm, prev, arrived)
        fetch.start()
    depth = spheres * multi
    half_width = waves.shape[1]
    width = 2 * half_width
    lanes = max(128, count * spheres)
    parts = 1
    tall = 2 * width // parts
    few, size = spheres // parts, depth // parts

    for copy in copies:
        copy.wait()
    coords = None
    row = lax.broadcasted_iota(jnp.int32, (depth, lanes), 0)
    lane = lax.broadcasted_iota(jnp.int32, (depth, lanes), 1)
    lead = row - lane * multi
    for index, block in enumerate(blocks):
        pick = (lead == -depth * index).astype(F32).astype(BF16)
        part = mm(block[2 * multi : 2 * multi + EXTRA, :], pick)
        coords = part if coords is None else coords + part
    turns = mm_t(waves[...], coords.astype(BF16))
    cos_v, sin_v = circle(turns)
    for index in range(count):
        at = slice(spheres * index, spheres * (index + 1))
        cos_s[index] = cos_v[:, at].astype(BF16)
        sin_s[index] = sin_v[:, at].astype(BF16)
        cos_t[index] = cos_v.T[at, :]
        sin_t[index] = sin_v.T[at, :]
    row = lax.broadcasted_iota(jnp.int32, (spheres, depth), 0)
    lane = lax.broadcasted_iota(jnp.int32, (spheres, depth), 1)
    inside = (lane >= row * multi) & (lane < row * multi + multi)
    pick_s = inside.astype(F32).astype(BF16)

    def spread(slot, index, at, many):
        rows = pl.ds(at, many)
        slot[0][rows, :] = mm(cos_s[index, rows, :], pick_s).astype(BF16)
        slot[1][rows, :] = mm(sin_s[index, rows, :], pick_s).astype(BF16)

    def build_left(slot, phases, part, piece):
        low = (piece * tall // 8) % half_width
        many = tall // 8
        c, s = phases[0][low : low + many, :], phases[1][low : low + many, :]
        rows = pl.ds(part * tall + piece * many, many)
        u_re = out_tile[0, rows, :]
        u_im = out_tile[1, rows, :]
        re = u_re * c - u_im * s
        im = u_re * s + u_im * c
        slot[0][rows, :] = re
        slot[1][rows, :] = im
        slot[2][rows, :] = re + im

    def build_right(slot, index, part, piece):
        many = size // 6
        base = part * size + piece * many
        both = mm_t(
            blocks_here[index, 0 : 2 * multi, pl.ds(base, many)], in_pair[...]
        )
        done = 0
        while done < many:
            k = (piece * many + done) // multi
            stop = min((k + 1) * multi - piece * many, many)
            at = part * few + k
            c = cos_t[index, at : at + 1, :]
            s = sin_t[index, at : at + 1, :]
            to = pl.ds(base + done, stop - done)
            for pol in range(2):
                lo = pol * half_width
                g_re = both[done:stop, lo : lo + half_width]
                g_im = both[done:stop, width + lo : width + lo + half_width]
                re = g_re * c + g_im * s
                im = g_im * c - g_re * s
                slot[0][to, lo : lo + half_width] = re.astype(BF16)
                slot[1][to, lo : lo + half_width] = im.astype(BF16)
                slot[2][to, lo : lo + half_width] = (re + im).astype(BF16)
            done = stop

    def tasks_of(slot_left, phases, slot_right, index, part):
        lefts = [
            functools.partial(build_left, slot_left, phases, part, piece)
            for piece in range(8)
        ]
        rights = [
            functools.partial(build_right, slot_right, index, part, piece)
            for piece in range(6)
        ]
        tasks = []
        while lefts or rights:
            tasks += lefts[:1] + rights[:1]
            lefts, rights = lefts[1:], rights[1:]
        return tasks

    spread(spread_slots[0], 0, 0, half_width)
    if count > 1:
        spread(spread_slots[1], 1, 0, half_width)

    for task in tasks_of(left_slots[0], spread_slots[0], right_slots[0], 0, 0):
        task()
    for pair in range(count // 2):
        for now in range(2):
            later = 1 - now
            index = 2 * pair + now
            after = index + 1
            tasks = []
            if after < count:
              tasks = tasks_of(left_slots[later], spread_slots[later], right_slots[later], after, 0)
            after = index + 2
            if after < count:
              tasks.append(functools.partial(spread, spread_slots[now], after, 0, half_width))
            pieces = [
                (total, left, right, slice(lane * 256, (lane + 1) * 256))
                for total, left, right in zip(
                    (sum_1, sum_2, sum_3), left_slots[now], right_slots[now]
                )
                for lane in range(width // 256)
            ]
            for at, (total, left, right, cols) in enumerate(pieces):
                before = total[:, cols]
                product = mm(left[...], right[:, cols])
                total[:, cols] = product if index == 0 else before + product
                share = -(-len(tasks) // (len(pieces) - at))
                for task in tasks[:share]:
                    task()
                tasks = tasks[share:]

    if last:
        fetch.wait()
    for part in range(4):
        kind, pol = part // 2, part % 2
        rows = pl.ds(part * half_width, half_width)
        re = sum_1[rows, :] - sum_2[rows, :]
        im = sum_3[rows, :] - sum_1[rows, :] - sum_2[rows, :]
        if not last:
            out[0, rows, :] = re
            out[1, rows, :] = im
        else:
            re = re + prev[0, rows, :]
            im = im + prev[1, rows, :]
            if kind == 1:
                at = lax.broadcasted_iota(jnp.int32, (half_width, width), 0) + pol * half_width
                lane = lax.broadcasted_iota(jnp.int32, (half_width, width), 1)
                on = at == lane
                re = re + jnp.where(on, jnp.cos(phase_row[...]), 0.0)
                im = im + jnp.where(on, jnp.sin(phase_row[...]), 0.0)
            to = pl.ds(pol * half_width, half_width)
            out[2 * kind, to, :] = re.astype(BF16)
            out[2 * kind + 1, to, :] = im.astype(BF16)


def pack_kernel(tmatrix, sites, out):
    spheres, _, multi, _ = tmatrix.shape
    depth = spheres * multi
    for c in range(2):
        flat = tmatrix[:, c].reshape(depth, multi)
        out[c * multi : (c + 1) * multi, :] = flat.T.astype(BF16)
    row = lax.broadcasted_iota(jnp.int32, (spheres, depth), 0)
    lane = lax.broadcasted_iota(jnp.int32, (spheres, depth), 1)
    inside = (lane >= row * multi) & (lane < row * multi + multi)
    pick = inside.astype(F32).astype(BF16)
    site = sites[...].astype(F32)
    column = jnp.floor((site + 0.5) * (1.0 / LATTICE))
    along = site - LATTICE * column
    both = jnp.concatenate([column, along, jnp.zeros((EXTRA - 2, spheres), F32)], axis=0)
    out[2 * multi : 2 * multi + EXTRA, :] = mm(both.astype(BF16), pick).astype(BF16)


def pack(tmatrix, sites):
    spheres, _, multi, _ = tmatrix.shape
    return pl.pallas_call(
        pack_kernel,
        out_shape=jax.ShapeDtypeStruct((2 * multi + EXTRA, spheres * multi), BF16),
        in_specs=[VMEM, VMEM],
        out_specs=VMEM,
        name="pack",
    )(tmatrix, sites)


def prepare_kernel(depth, out_basis, in_basis, waves, out_tile, in_pair, waves_pad):
    multi, width = in_basis.shape[1], in_basis.shape[2]
    row = lax.broadcasted_iota(jnp.int32, (multi, depth), 0).astype(F32)
    lane = lax.broadcasted_iota(jnp.int32, (multi, depth), 1).astype(F32)
    lane = lane - multi * jnp.floor((lane + 0.5) * (1.0 / multi))
    pick = (row == lane).astype(F32).astype(BF16)
    for kind in range(2):
        for c in range(2):
            tile = mm_t(out_basis[kind, c].astype(BF16), pick)
            out_tile[c, kind * width : (kind + 1) * width, :] = tile.astype(BF16)
    b_re, b_im = in_basis[0].astype(BF16), in_basis[1].astype(BF16)
    in_pair[0:multi, 0:width] = b_re
    in_pair[0:multi, width : 2 * width] = b_im
    in_pair[multi : 2 * multi, 0:width] = -b_im
    in_pair[multi : 2 * multi, width : 2 * width] = b_re
    pads = jnp.zeros((EXTRA - 2, width // 2), F32)
    waves_pad[...] = jnp.concatenate([waves[...].astype(F32), pads], axis=0).astype(BF16)


def prepare(out_basis, in_basis, waves, spheres):
    multi, width = in_basis.shape[1], in_basis.shape[2]
    depth = spheres * multi
    return pl.pallas_call(
        functools.partial(prepare_kernel, depth),
        out_shape=(
            jax.ShapeDtypeStruct((2, 2 * width, depth), BF16),
            jax.ShapeDtypeStruct((2 * multi, 2 * width), BF16),
            jax.ShapeDtypeStruct((EXTRA, width // 2), BF16),
        ),
        in_specs=[VMEM] * 3,
        out_specs=(VMEM,) * 3,
        compiler_params=pltpu.CompilerParams(vmem_limit_bytes=16 * 2**20),
        cost_estimate=pl.CostEstimate(flops=2**31, bytes_accessed=2**22, transcendentals=0),
        name="prepare",
    )(out_basis, in_basis, waves)


def layer_sum(blocks, spheres, multi, out_tile, in_pair, waves, prev=None, phase=None):
    count = len(blocks)
    last = prev is not None
    depth = spheres * multi
    half_width = waves.shape[1]
    width = 2 * half_width
    operands = list(blocks) + [out_tile, in_pair, waves]
    specs = [ANY] * count + [VMEM] * 3
    if last:
        operands += [prev, phase.reshape(1, -1)]
        specs += [ANY, VMEM]
        shape = jax.ShapeDtypeStruct((4, width, width), BF16)
    else:
        shape = jax.ShapeDtypeStruct((2, 2 * width, width), F32)
    scratch = [pltpu.VMEM((2 * width, width), F32)] * 3
    scratch += [pltpu.VMEM((count, spheres, half_width), F32)] * 2
    scratch += [pltpu.VMEM((2 * width, depth), BF16)] * 6
    scratch += [pltpu.VMEM((depth, width), BF16)] * 6
    scratch += [pltpu.VMEM((half_width, depth), BF16)] * 4
    scratch += [pltpu.VMEM((count, half_width, spheres), BF16)] * 2
    scratch += [pltpu.VMEM((count,) + blocks[0].shape, BF16)]
    scratch += [pltpu.SemaphoreType.DMA((count,))]
    if last:
        scratch += [pltpu.VMEM((2, 2 * width, width), F32), pltpu.SemaphoreType.DMA]
    flops = count * 3 * 2 * 2 * width * width * depth
    return pl.pallas_call(
        functools.partial(layer_kernel, count, spheres, multi, last),
        out_shape=shape,
        in_specs=specs,
        out_specs=VMEM,
        scratch_shapes=scratch,
        compiler_params=pltpu.CompilerParams(vmem_limit_bytes=40 * 2**20),
        cost_estimate=pl.CostEstimate(flops=flops, bytes_accessed=2**23, transcendentals=0),
        name="layer_sum",
    )(*operands)


def take_pair(place, own, other, u, v, sems, order):
    def take(to, source, side, kind):
        at = pl.ds(2 * kind, 2)
        return pltpu.make_async_copy(source.at[at], to.at[at], sems.at[2 * side + kind])

    @pl.when(place[0] == 1)
    def _():
        for side, kind in order:
            take((u, v)[side], (own, other)[side], side, kind).start()

    @pl.when(place[0] == 0)
    def _():
        for side, kind in order:
            take((u, v)[side], (other, own)[side], side, kind).start()

    def arrived(side, kind):
        take((u, v)[side], own, side, kind).wait()
        ref = (u, v)[side]
        return (ref[2 * kind], ref[2 * kind + 1])

    return arrived


def back_kernel(place, own, other, s_out, s_send, u, v, sems):
    side = own.shape[1] // 2
    arrived = take_pair(place, own, other, u, v, sems, ((0, 1), (1, 0), (0, 0)))
    mine = pl.ds(pl.multiple_of(place[1] * side, side), side)
    t_u = arrived(0, 1)
    r_v = arrived(1, 0)
    base = (u[2, :, mine], u[3, :, mine])
    up = cmul(r_v, base)
    r_u = arrived(0, 0)
    again = cmul(r_u, half(up))
    again = cmul(r_v, half(again))
    up = half(add(up, again))
    back = cmul(t_u, up)
    for c in range(2):
        s_out[c] = (u[c, :, mine].astype(F32) + back[c]).astype(BF16)
        s_send[c] = s_out[c, pl.ds(pl.multiple_of(place[4] * side, side), side), :]


def rows_kernel(rows, place, own, other, after, h_near, h_far, u, v, sems):
    del after
    width = own.shape[1]
    quarter = width // 4
    core = place[1]
    arrived = take_pair(place, own, other, u, v, sems, ((1, 1), (0, 0), (1, 0), (0, 1)))
    near = pl.ds(pl.multiple_of(core * quarter, quarter), quarter)
    far = pl.ds(pl.multiple_of((core + 2) * quarter, quarter), quarter)

    def columns(ref, at):
        return jnp.concatenate([ref[at, :, near], ref[at, :, far]], axis=1)

    arrived(1, 1)
    base = (columns(v, 2), columns(v, 3))
    r_u = arrived(0, 0)
    chain = cmul(r_u, base)
    r_v = arrived(1, 0)
    chain = cmul(r_v, half(chain))
    t_u = arrived(0, 1)
    chain = half((base[0] + chain[0], base[1] + chain[1]))
    here = cmul(t_u, chain)
    my = pl.ds(pl.multiple_of(place[2] * rows, rows), rows)
    row_t = (v[2, my, :], v[3, my, :])
    w_1 = half(cmul(row_t, r_u))
    k_part = cmul(w_1, chain)
    w_2 = cmul(w_1, r_v)
    w_2 = half((row_t[0] + w_2[0], row_t[1] + w_2[1]))
    g_rows = half(cmul(w_2, t_u))
    for side, (to, cols) in enumerate(((h_near, near), (h_far, far))):
        at = slice(side * quarter, (side + 1) * quarter)
        for c in range(2):
            to[c, 0:width, :] = here[c][:, at].astype(BF16)
            k_side = v[c, my, cols].astype(F32) + k_part[c][:, at]
            to[c, width : width + rows, :] = k_side.astype(BF16)
            for q in range(4):
                put = width + rows + q * rows
                to[c, put : put + rows, :] = g_rows[c][:, q * quarter : (q + 1) * quarter]


def form(place, own, other, rows):
    width = own.shape[1]
    scratch = [pltpu.VMEM(own.shape, BF16)] * 2 + [pltpu.SemaphoreType.DMA((4,))]
    params = pltpu.CompilerParams(vmem_limit_bytes=24 * 2**20)
    back, send = pl.pallas_call(
        back_kernel,
        out_shape=(
            jax.ShapeDtypeStruct((2, width, width // 2), BF16),
            jax.ShapeDtypeStruct((2, width // 2, width // 2), BF16),
        ),
        in_specs=[SMEM, ANY, ANY],
        out_specs=(VMEM, VMEM),
        scratch_shapes=scratch,
        compiler_params=params,
        cost_estimate=pl.CostEstimate(flops=2**32, bytes_accessed=2**23, transcendentals=0),
        name="back",
    )(place, own, other)
    shape = jax.ShapeDtypeStruct((2, width + 5 * rows, width // 4), BF16)
    near, far = pl.pallas_call(
        functools.partial(rows_kernel, rows),
        out_shape=(shape, shape),
        in_specs=[SMEM, ANY, ANY, ANY],
        out_specs=(VMEM, VMEM),
        scratch_shapes=scratch,
        compiler_params=params,
        cost_estimate=pl.CostEstimate(flops=2**32, bytes_accessed=2**23, transcendentals=0),
        name="rows",
    )(place, own, other, back)
    return back, send, near, far


def join_kernel(
    rows, place, s_mine, s_side, q_0, q_1, q_2, q_3, h_near, h_sent, refl, trans, sides, h, sems
):
    width = sides.shape[3]
    lower, core = place[3], place[1]
    many = width // 2
    this = pl.ds(pl.multiple_of(place[4] * many, many), many)
    that = pl.ds(pl.multiple_of((1 - place[4]) * many, many), many)
    moves = (
        ((h_near, h.at[lower]), 2),
        ((h_sent, h.at[1 - lower]), 2),
        ((s_mine, sides.at[lower, core]), lower),
        ((s_side, sides.at[lower, 1 - core]), lower),
        ((q_0, sides.at[1 - lower, core, :, this, :]), 1 - lower),
        ((q_1, sides.at[1 - lower, core, :, that, :]), 1 - lower),
        ((q_2, sides.at[1 - lower, 1 - core, :, this, :]), 1 - lower),
        ((q_3, sides.at[1 - lower, 1 - core, :, that, :]), 1 - lower),
    )
    for move, at in moves:
        pltpu.make_async_copy(*move, sems.at[at]).start()

    def arrived(ref, at):
        pltpu.make_async_copy(ref, ref, sems.at[at]).wait()

    arrived(h, 2)

    def rows_of(side):
        return tuple(
            jnp.concatenate(
                [
                    h[side, c, width + rows + q * rows : width + 2 * rows + q * rows, :]
                    for q in range(4)
                ],
                axis=1,
            )
            for c in range(2)
        )

    def times(pair, side):
        parts = [
            cmul(pair, (sides[side, at, 0], sides[side, at, 1]))
            for at in range(2)
        ]
        return tuple(jnp.concatenate([parts[0][c], parts[1][c]], axis=1) for c in range(2))

    from_above = rows_of(0)
    from_below = rows_of(1)
    arrived(sides.at[1], 1)
    second = half(times(from_above, 1))
    both = tuple(jnp.concatenate([from_below[c], second[c]], axis=0) for c in range(2))
    arrived(sides.at[0], 0)
    chain = times(half(times(both, 0)), 1)
    chain = half(tuple(both[c].astype(F32) + chain[c] for c in range(2)))
    result = cmul(chain, (h[0, 0, 0:width, :], h[0, 1, 0:width, :]))
    for c in range(2):
        trans[c] = result[c][0:rows]
        refl[c] = h[0, c, width : width + rows, :].astype(F32) + result[c][rows : 2 * rows]


def join(place, s_mine, s_side, quarters, h_near, h_sent, rows):
    columns = h_near.shape[2]
    shape = jax.ShapeDtypeStruct((2, rows, columns), F32)
    return pl.pallas_call(
        functools.partial(join_kernel, rows),
        out_shape=(shape, shape),
        in_specs=[SMEM] + [ANY] * 8,
        out_specs=(VMEM, VMEM),
        scratch_shapes=[
            pltpu.VMEM((2, 2) + s_mine.shape, BF16),
            pltpu.VMEM((2,) + h_near.shape, BF16),
            pltpu.SemaphoreType.DMA((3,)),
        ],
        compiler_params=pltpu.CompilerParams(vmem_limit_bytes=20 * 2**20),
        cost_estimate=pl.CostEstimate(flops=2**30, bytes_accessed=2**22, transcendentals=0),
        name="join",
    )(place, s_mine, s_side, *quarters, h_near, h_sent)


def whole_layers(inner, out_basis, in_basis, tmatrix, sites, waves, layer_phase):
    spheres, multi = tmatrix.shape[1], tmatrix.shape[3]
    half_width = waves.shape[1]
    width = 2 * half_width
    groups = lax.axis_size("sph")
    outer = groups // inner
    rows = width // groups
    layer = lax.axis_index("layer")

    block = pack(tmatrix[0], sites)

    def shifted(value, far, side):
        pairs = [
            (g, ((g // inner + far) % outer) * inner + (g % inner + side) % inner)
            for g in range(groups)
        ]
        return lax.ppermute(value, "sph", pairs)

    near = [shifted(block, 0, 1), shifted(block, 1, 0), shifted(block, outer - 1, 0)]
    near = [block, *near]
    tile, pair, waves_pad = prepare(out_basis[0], in_basis[0], waves, spheres)
    late, waves_pad = lax.optimization_barrier((block, waves_pad))
    ready = (tile, pair, waves_pad)
    far = [shifted(late, 2, 0), shifted(near[2], 0, 1), shifted(near[3], 0, 1)]
    far += [shifted(late, 2, 1)]

    part = layer_sum(near, spheres, multi, *ready)
    own = layer_sum(far, spheres, multi, *ready, part, layer_phase[0])

    other = lax.ppermute(own, "layer", [(at, at ^ 1) for at in range(4)])
    core, lower = layer % 2, layer // 2
    mine_is_u = jnp.where(core != lower, 1, 0)
    group = lax.axis_index("sph")
    side = group % inner
    place = jnp.stack([mine_is_u, core, group, lower, side]).astype(jnp.int32)
    s_mine, s_send, h_near, h_far = form(place, own, other, rows)

    def crossed(value, bit):
        return lax.ppermute(value, "layer", [(at, at ^ bit) for at in range(4)])

    s_far = crossed(s_send, 2)
    h_sent = crossed(h_far, 2)
    s_side = crossed(s_mine, 1)
    s_far, h_near = lax.optimization_barrier((s_far, h_near))
    s_next = shifted(s_far, 0, 1)
    quarters = (s_far, s_next, crossed(s_far, 1), crossed(s_next, 1))
    return join(place, s_mine, s_side, quarters, h_near, h_sent, rows)


def solution(mesh):
    in_specs = (
        P("layer", None, None, None, None),
        P("layer", None, None, None),
        P("layer", "sph", None, None, None),
        P("layer", "sph"),
        P(),
        P("layer", None),
    )
    out_specs = (P(None, "sph", "layer"), P(None, "sph", "layer"))
    on_device = by_rows
    if mesh.shape["layer"] == 4 and mesh.shape["sph"] == 8:
        on_device = functools.partial(whole_layers, 2)
    return jax.shard_map(
        on_device, mesh=mesh, in_specs=in_specs, out_specs=out_specs, check_vma=False
    )
```

```python
import functools
import math

import jax
import jax.numpy as jnp
from jax import lax
from jax.experimental import pallas as pl
from jax.experimental.pallas import tpu as pltpu
from jax.sharding import PartitionSpec as P

LATTICE = 32
TWO_PI = 2.0 * math.pi
F32 = jnp.float32
BF16 = jnp.bfloat16
VMEM = pl.BlockSpec(memory_space=pltpu.VMEM)
ANY = pl.BlockSpec(memory_space=pl.ANY)
SMEM = pl.BlockSpec(memory_space=pltpu.SMEM)
EXTRA = 16


def partner_2(value, axis, bit):
    mask = 2**bit
    pairs = [(source, source ^ mask) for source in range(lax.axis_size(axis))]
    return lax.ppermute(value, axis, pairs)


def wave_angles(site_list, waves):
    column = site_list // LATTICE
    along = site_list % LATTICE
    phase_index = (
        waves[0][None, :] * column[:, None] + waves[1][None, :] * along[:, None]
    ) % LATTICE
    angles = phase_index.astype(jnp.float32) * (TWO_PI / LATTICE)
    return jnp.concatenate([angles, angles], axis=1)


def factors(out_layer, in_layer, tm_layer, angles):
    highest = lax.Precision.HIGHEST
    basis_re = out_layer[:, 0]
    basis_im = out_layer[:, 1]
    tmat_re = tm_layer[:, 0]
    tmat_im = tm_layer[:, 1]
    prod_re = jnp.einsum("kjw,sjm->ksmw", basis_re, tmat_re, precision=highest) - jnp.einsum(
        "kjw,sjm->ksmw", basis_im, tmat_im, precision=highest
    )
    prod_im = jnp.einsum("kjw,sjm->ksmw", basis_re, tmat_im, precision=highest) + jnp.einsum(
        "kjw,sjm->ksmw", basis_im, tmat_re, precision=highest
    )
    cosine = jnp.cos(angles)
    sine = jnp.sin(angles)
    left_re = prod_re * cosine[None, :, None, :] - prod_im * sine[None, :, None, :]
    left_im = prod_re * sine[None, :, None, :] + prod_im * cosine[None, :, None, :]
    right_re = in_layer[0][None] * cosine[:, None, :] + in_layer[1][None] * sine[:, None, :]
    right_im = in_layer[1][None] * cosine[:, None, :] - in_layer[0][None] * sine[:, None, :]
    inner = left_re.shape[1] * left_re.shape[2]
    width = left_re.shape[3]
    left_re = left_re.reshape(2, inner, width)
    left_im = left_im.reshape(2, inner, width)
    right_re = right_re.reshape(inner, width)
    right_im = right_im.reshape(inner, width)
    real_left = jnp.concatenate([left_re, -left_im], axis=1)
    imag_left = jnp.concatenate([left_re, left_im], axis=1)
    real_right = jnp.concatenate([right_re, right_im], axis=0)
    imag_right = jnp.concatenate([right_im, right_re], axis=0)
    return (real_left, imag_left, real_right, imag_right)


def project_rows(factor_set):
    real_left, imag_left, real_right, imag_right = factor_set
    highest = lax.Precision.HIGHEST
    pieces = []
    for kind in range(2):
        real_slice = real_left[kind]
        imag_slice = imag_left[kind]
        pieces.append(jnp.einsum("kr,kw->rw", real_slice, real_right, precision=highest))
        pieces.append(jnp.einsum("kr,kw->rw", imag_slice, imag_right, precision=highest))
    return jnp.concatenate(pieces, axis=1)


def narrow(matrix):
    return matrix.astype(jnp.bfloat16)


def complex_product(left, right):
    left_half = narrow(left)
    right_half = narrow(right)
    real_part = jnp.dot(left_half[0], right_half[0], preferred_element_type=jnp.float32) - jnp.dot(
        left_half[1], right_half[1], preferred_element_type=jnp.float32
    )
    imag_part = jnp.dot(left_half[0], right_half[1], preferred_element_type=jnp.float32) + jnp.dot(
        left_half[1], right_half[0], preferred_element_type=jnp.float32
    )
    return jnp.stack([real_part, imag_part])


def merge_level(state, bit):
    partner = partner_2(state.astype(jnp.bfloat16), "layer", bit).astype(state.dtype)
    is_upper = lax.axis_index("layer") // (1 << bit) % 2 == 0
    upper = jnp.where(is_upper, state, partner)
    lower = jnp.where(is_upper, partner, state)
    refl_a, trans_a, refl_a_back, trans_a_back = (upper[0], upper[1], upper[2], upper[3])
    refl_b, trans_b, refl_b_back, trans_b_back = (lower[0], lower[1], lower[2], lower[3])
    first_left = jnp.where(is_upper, refl_a_back, refl_b)
    first_right = jnp.where(is_upper, refl_b, refl_a_back)
    chain_base = jnp.where(is_upper, trans_a, trans_b_back)
    across = jnp.where(is_upper, trans_b, trans_a_back)
    final_left = jnp.where(is_upper, trans_a_back, trans_b)
    addend = jnp.where(is_upper, refl_a, refl_b_back)
    full_right, full_base = (
        lax.all_gather(narrow(first_right), "sph", axis=1, tiled=True),
        lax.all_gather(narrow(chain_base), "sph", axis=1, tiled=True),
    )
    first_mix = complex_product(first_left, full_right)
    chain = chain_base + complex_product(first_mix, full_base)
    full_chain = lax.all_gather(narrow(chain), "sph", axis=1, tiled=True)
    bounce = complex_product(first_right, full_chain)
    own_trans = complex_product(across, full_chain)
    full_bounce = lax.all_gather(narrow(bounce), "sph", axis=1, tiled=True)
    own_refl = addend + complex_product(final_left, full_bounce)
    mine = jnp.stack([own_trans, own_refl])
    theirs = partner_2(mine.astype(jnp.bfloat16), "layer", bit).astype(mine.dtype)
    trans_new = jnp.where(is_upper, mine[0], theirs[0])
    refl_new = jnp.where(is_upper, mine[1], theirs[1])
    trans_back_new = jnp.where(is_upper, theirs[0], mine[0])
    refl_back_new = jnp.where(is_upper, theirs[1], mine[1])
    return jnp.stack([refl_new, trans_new, refl_back_new, trans_back_new])


def by_rows(out_basis, in_basis, tmatrix, sites, waves, layer_phase):
    width = 2 * waves.shape[1]
    rows = width // lax.axis_size("sph")
    angles = wave_angles(sites[0], waves)
    factor_set = factors(out_basis[0], in_basis[0], tmatrix[0], angles)
    summed = lax.psum_scatter(
        project_rows(factor_set).astype(jnp.bfloat16), "sph", scatter_dimension=0, tiled=True
    ).astype(jnp.float32)
    first_row = lax.axis_index("sph") * rows
    diagonal = ((first_row + jnp.arange(rows))[:, None] == jnp.arange(width)[None, :]).astype(
        jnp.float32
    )
    refl = jnp.stack([summed[:, :width], summed[:, width : 2 * width]])
    trans_re = summed[:, 2 * width : 3 * width] + diagonal * jnp.cos(layer_phase[0])[None, :]
    trans_im = summed[:, 3 * width :] + diagonal * jnp.sin(layer_phase[0])[None, :]
    trans = jnp.stack([trans_re, trans_im])
    state = jnp.stack([refl, trans, refl, trans])
    levels = lax.axis_size("layer").bit_length() - 1
    for bit in range(levels):
        state = merge_level(state, bit)
    columns = width // lax.axis_size("layer")
    first_column = lax.axis_index("layer") * columns
    own_refl = lax.dynamic_slice_in_dim(state[0], first_column, columns, 2)
    own_trans = lax.dynamic_slice_in_dim(state[1], first_column, columns, 2)
    return (own_refl, own_trans)


def mm(left, right):
    return jnp.dot(left, right, preferred_element_type=F32)


def mm_t(left, right):
    return lax.dot_general(left, right, (((0,), (0,)), ((), ())), preferred_element_type=F32)


def cmul(left, right):
    one = mm(left[0], right[0])
    two = mm(left[1], right[1])
    both = mm(left[0] + left[1], right[0] + right[1])
    return (one - two, both - one - two)


def half(pair):
    return (pair[0].astype(BF16), pair[1].astype(BF16))


def add(one, two):
    return (one[0] + two[0], one[1] + two[1])


def circle(turns):
    turn = turns * (1.0 / LATTICE)
    turn = turn - jnp.floor(turn)
    quarter = jnp.floor(turn * 4.0 + 0.5)
    x = (turn - quarter * 0.25) * TWO_PI
    y = x * x
    sin = x * (1.0 + y * (-1.0 / 6 + y * (1.0 / 120 + y * (-1.0 / 5040 + y * (1.0 / 362880)))))
    cos = 1.0 + y * (-0.5 + y * (1.0 / 24 + y * (-1.0 / 720 + y * (1.0 / 40320))))
    odd = (quarter == 1.0) | (quarter == 3.0)
    cos, sin = jnp.where(odd, sin, cos), jnp.where(odd, cos, sin)
    cos = jnp.where((quarter == 1.0) | (quarter == 2.0), -cos, cos)
    sin = jnp.where((quarter == 2.0) | (quarter == 3.0), -sin, sin)
    return cos, sin


def layer_kernel(count, spheres, multi, last, *refs):
    sent = refs[:count]
    rest = list(refs[count:])
    out_tile, in_pair, waves = rest[:3]
    rest = rest[3:]
    if last:
        prev_hbm, phase_row = rest[:2]
        rest = rest[2:]
    out = rest[0]
    rest = rest[1:]
    sum_1, sum_2, sum_3, cos_t, sin_t = rest[:5]
    left_slots = (rest[5:8], rest[8:11])
    right_slots = (rest[11:14], rest[14:17])
    spread_slots = (rest[17:19], rest[19:21])
    cos_s, sin_s, blocks_here, block_sem = rest[21:25]
    blocks = [blocks_here.at[index] for index in range(count)]
    copies = [
        pltpu.make_async_copy(sent[index], blocks_here.at[index], block_sem.at[index])
        for index in range(count)
    ]
    for copy in copies:
        copy.start()
    if last:
        prev, arrived = rest[25:]
        fetch = pltpu.make_async_copy(prev_hbm, prev, arrived)
        fetch.start()
    depth = spheres * multi
    half_width = waves.shape[1]
    width = 2 * half_width
    lanes = max(128, count * spheres)
    parts = 1
    tall = 2 * width // parts
    few, size = spheres // parts, depth // parts

    for copy in copies:
        copy.wait()
    coords = None
    row = lax.broadcasted_iota(jnp.int32, (depth, lanes), 0)
    lane = lax.broadcasted_iota(jnp.int32, (depth, lanes), 1)
    lead = row - lane * multi
    for index, block in enumerate(blocks):
        pick = (lead == -depth * index).astype(F32).astype(BF16)
        part = mm(block[2 * multi : 2 * multi + EXTRA, :], pick)
        coords = part if coords is None else coords + part
    turns = mm_t(waves[...], coords.astype(BF16))
    cos_v, sin_v = circle(turns)
    for index in range(count):
        at = slice(spheres * index, spheres * (index + 1))
        cos_s[index] = cos_v[:, at].astype(BF16)
        sin_s[index] = sin_v[:, at].astype(BF16)
        cos_t[index] = cos_v.T[at, :]
        sin_t[index] = sin_v.T[at, :]
    row = lax.broadcasted_iota(jnp.int32, (spheres, depth), 0)
    lane = lax.broadcasted_iota(jnp.int32, (spheres, depth), 1)
    inside = (lane >= row * multi) & (lane < row * multi + multi)
    pick_s = inside.astype(F32).astype(BF16)

    def spread(slot, index, at, many):
        rows = pl.ds(at, many)
        slot[0][rows, :] = mm(cos_s[index, rows, :], pick_s).astype(BF16)
        slot[1][rows, :] = mm(sin_s[index, rows, :], pick_s).astype(BF16)

    def build_left(slot, phases, part, piece):
        low = (piece * tall // 8) % half_width
        many = tall // 8
        c, s = phases[0][low : low + many, :], phases[1][low : low + many, :]
        rows = pl.ds(part * tall + piece * many, many)
        u_re = out_tile[0, rows, :]
        u_im = out_tile[1, rows, :]
        re = u_re * c - u_im * s
        im = u_re * s + u_im * c
        slot[0][rows, :] = re
        slot[1][rows, :] = im
        slot[2][rows, :] = re + im

    def build_right(slot, index, part, piece):
        many = size // 6
        base = part * size + piece * many
        both = mm_t(
            blocks_here[index, 0 : 2 * multi, pl.ds(base, many)], in_pair[...]
        )
        done = 0
        while done < many:
            k = (piece * many + done) // multi
            stop = min((k + 1) * multi - piece * many, many)
            at = part * few + k
            c = cos_t[index, at : at + 1, :]
            s = sin_t[index, at : at + 1, :]
            to = pl.ds(base + done, stop - done)
            for pol in range(2):
                lo = pol * half_width
                g_re = both[done:stop, lo : lo + half_width]
                g_im = both[done:stop, width + lo : width + lo + half_width]
                re = g_re * c + g_im * s
                im = g_im * c - g_re * s
                slot[0][to, lo : lo + half_width] = re.astype(BF16)
                slot[1][to, lo : lo + half_width] = im.astype(BF16)
                slot[2][to, lo : lo + half_width] = (re + im).astype(BF16)
            done = stop

    def tasks_of(slot_left, phases, slot_right, index, part):
        lefts = [
            functools.partial(build_left, slot_left, phases, part, piece)
            for piece in range(8)
        ]
        rights = [
            functools.partial(build_right, slot_right, index, part, piece)
            for piece in range(6)
        ]
        tasks = []
        while lefts or rights:
            tasks += lefts[:1] + rights[:1]
            lefts, rights = lefts[1:], rights[1:]
        return tasks

    spread(spread_slots[0], 0, 0, half_width)
    if count > 1:
        spread(spread_slots[1], 1, 0, half_width)

    for task in tasks_of(left_slots[0], spread_slots[0], right_slots[0], 0, 0):
        task()
    for pair in range(count // 2):
        for now in range(2):
            later = 1 - now
            index = 2 * pair + now
            after = index + 1
            tasks = []
            if after < count:
              tasks = tasks_of(left_slots[later], spread_slots[later], right_slots[later], after, 0)
            after = index + 2
            if after < count:
              tasks.append(functools.partial(spread, spread_slots[now], after, 0, half_width))
            pieces = [
                (total, left, right, slice(lane * 256, (lane + 1) * 256))
                for total, left, right in zip(
                    (sum_1, sum_2, sum_3), left_slots[now], right_slots[now]
                )
                for lane in range(width // 256)
            ]
            for at, (total, left, right, cols) in enumerate(pieces):
                before = total[:, cols]
                product = mm(left[...], right[:, cols])
                total[:, cols] = product if index == 0 else before + product
                share = -(-len(tasks) // (len(pieces) - at))
                for task in tasks[:share]:
                    task()
                tasks = tasks[share:]

    if last:
        fetch.wait()
    for part in range(4):
        kind, pol = part // 2, part % 2
        rows = pl.ds(part * half_width, half_width)
        re = sum_1[rows, :] - sum_2[rows, :]
        im = sum_3[rows, :] - sum_1[rows, :] - sum_2[rows, :]
        if not last:
            out[0, rows, :] = re
            out[1, rows, :] = im
        else:
            re = re + prev[0, rows, :]
            im = im + prev[1, rows, :]
            if kind == 1:
                at = lax.broadcasted_iota(jnp.int32, (half_width, width), 0) + pol * half_width
                lane = lax.broadcasted_iota(jnp.int32, (half_width, width), 1)
                on = at == lane
                re = re + jnp.where(on, jnp.cos(phase_row[...]), 0.0)
                im = im + jnp.where(on, jnp.sin(phase_row[...]), 0.0)
            to = pl.ds(pol * half_width, half_width)
            out[2 * kind, to, :] = re.astype(BF16)
            out[2 * kind + 1, to, :] = im.astype(BF16)


def pack_kernel(tmatrix, sites, out):
    spheres, _, multi, _ = tmatrix.shape
    depth = spheres * multi
    for c in range(2):
        flat = tmatrix[:, c].reshape(depth, multi)
        out[c * multi : (c + 1) * multi, :] = flat.T.astype(BF16)
    row = lax.broadcasted_iota(jnp.int32, (spheres, depth), 0)
    lane = lax.broadcasted_iota(jnp.int32, (spheres, depth), 1)
    inside = (lane >= row * multi) & (lane < row * multi + multi)
    pick = inside.astype(F32).astype(BF16)
    site = sites[...].astype(F32)
    column = jnp.floor((site + 0.5) * (1.0 / LATTICE))
    along = site - LATTICE * column
    both = jnp.concatenate([column, along, jnp.zeros((EXTRA - 2, spheres), F32)], axis=0)
    out[2 * multi : 2 * multi + EXTRA, :] = mm(both.astype(BF16), pick).astype(BF16)


def pack(tmatrix, sites):
    spheres, _, multi, _ = tmatrix.shape
    return pl.pallas_call(
        pack_kernel,
        out_shape=jax.ShapeDtypeStruct((2 * multi + EXTRA, spheres * multi), BF16),
        in_specs=[VMEM, VMEM],
        out_specs=VMEM,
        name="pack",
    )(tmatrix, sites)


def prepare_kernel(depth, out_basis, in_basis, waves, out_tile, in_pair, waves_pad):
    multi, width = in_basis.shape[1], in_basis.shape[2]
    row = lax.broadcasted_iota(jnp.int32, (multi, depth), 0).astype(F32)
    lane = lax.broadcasted_iota(jnp.int32, (multi, depth), 1).astype(F32)
    lane = lane - multi * jnp.floor((lane + 0.5) * (1.0 / multi))
    pick = (row == lane).astype(F32).astype(BF16)
    for kind in range(2):
        for c in range(2):
            tile = mm_t(out_basis[kind, c].astype(BF16), pick)
            out_tile[c, kind * width : (kind + 1) * width, :] = tile.astype(BF16)
    b_re, b_im = in_basis[0].astype(BF16), in_basis[1].astype(BF16)
    in_pair[0:multi, 0:width] = b_re
    in_pair[0:multi, width : 2 * width] = b_im
    in_pair[multi : 2 * multi, 0:width] = -b_im
    in_pair[multi : 2 * multi, width : 2 * width] = b_re
    pads = jnp.zeros((EXTRA - 2, width // 2), F32)
    waves_pad[...] = jnp.concatenate([waves[...].astype(F32), pads], axis=0).astype(BF16)


def prepare(out_basis, in_basis, waves, spheres):
    multi, width = in_basis.shape[1], in_basis.shape[2]
    depth = spheres * multi
    return pl.pallas_call(
        functools.partial(prepare_kernel, depth),
        out_shape=(
            jax.ShapeDtypeStruct((2, 2 * width, depth), BF16),
            jax.ShapeDtypeStruct((2 * multi, 2 * width), BF16),
            jax.ShapeDtypeStruct((EXTRA, width // 2), BF16),
        ),
        in_specs=[VMEM] * 3,
        out_specs=(VMEM,) * 3,
        compiler_params=pltpu.CompilerParams(vmem_limit_bytes=16 * 2**20),
        cost_estimate=pl.CostEstimate(flops=2**31, bytes_accessed=2**22, transcendentals=0),
        name="prepare",
    )(out_basis, in_basis, waves)


def layer_sum(blocks, spheres, multi, out_tile, in_pair, waves, prev=None, phase=None):
    count = len(blocks)
    last = prev is not None
    depth = spheres * multi
    half_width = waves.shape[1]
    width = 2 * half_width
    operands = list(blocks) + [out_tile, in_pair, waves]
    specs = [ANY] * count + [VMEM] * 3
    if last:
        operands += [prev, phase.reshape(1, -1)]
        specs += [ANY, VMEM]
        shape = jax.ShapeDtypeStruct((4, width, width), BF16)
    else:
        shape = jax.ShapeDtypeStruct((2, 2 * width, width), F32)
    scratch = [pltpu.VMEM((2 * width, width), F32)] * 3
    scratch += [pltpu.VMEM((count, spheres, half_width), F32)] * 2
    scratch += [pltpu.VMEM((2 * width, depth), BF16)] * 6
    scratch += [pltpu.VMEM((depth, width), BF16)] * 6
    scratch += [pltpu.VMEM((half_width, depth), BF16)] * 4
    scratch += [pltpu.VMEM((count, half_width, spheres), BF16)] * 2
    scratch += [pltpu.VMEM((count,) + blocks[0].shape, BF16)]
    scratch += [pltpu.SemaphoreType.DMA((count,))]
    if last:
        scratch += [pltpu.VMEM((2, 2 * width, width), F32), pltpu.SemaphoreType.DMA]
    flops = count * 3 * 2 * 2 * width * width * depth
    return pl.pallas_call(
        functools.partial(layer_kernel, count, spheres, multi, last),
        out_shape=shape,
        in_specs=specs,
        out_specs=VMEM,
        scratch_shapes=scratch,
        compiler_params=pltpu.CompilerParams(vmem_limit_bytes=40 * 2**20),
        cost_estimate=pl.CostEstimate(flops=flops, bytes_accessed=2**23, transcendentals=0),
        name="layer_sum",
    )(*operands)


def take_pair(place, own, other, u, v, sems, order):
    def take(to, source, side, kind):
        at = pl.ds(2 * kind, 2)
        return pltpu.make_async_copy(source.at[at], to.at[at], sems.at[2 * side + kind])

    @pl.when(place[0] == 1)
    def _():
        for side, kind in order:
            take((u, v)[side], (own, other)[side], side, kind).start()

    @pl.when(place[0] == 0)
    def _():
        for side, kind in order:
            take((u, v)[side], (other, own)[side], side, kind).start()

    def arrived(side, kind):
        take((u, v)[side], own, side, kind).wait()
        ref = (u, v)[side]
        return (ref[2 * kind], ref[2 * kind + 1])

    return arrived


def back_kernel(place, own, other, s_out, s_send, u, v, sems):
    side = own.shape[1] // 2
    arrived = take_pair(place, own, other, u, v, sems, ((0, 1), (1, 0), (0, 0)))
    mine = pl.ds(pl.multiple_of(place[1] * side, side), side)
    t_u = arrived(0, 1)
    r_v = arrived(1, 0)
    base = (u[2, :, mine], u[3, :, mine])
    up = cmul(r_v, base)
    r_u = arrived(0, 0)
    again = cmul(r_u, half(up))
    again = cmul(r_v, half(again))
    up = half(add(up, again))
    back = cmul(t_u, up)
    for c in range(2):
        s_out[c] = (u[c, :, mine].astype(F32) + back[c]).astype(BF16)
        s_send[c] = s_out[c, pl.ds(pl.multiple_of(place[4] * side, side), side), :]


def rows_kernel(rows, place, own, other, after, h_near, h_far, u, v, sems):
    del after
    width = own.shape[1]
    quarter = width // 4
    core = place[1]
    arrived = take_pair(place, own, other, u, v, sems, ((1, 1), (0, 0), (1, 0), (0, 1)))
    near = pl.ds(pl.multiple_of(core * quarter, quarter), quarter)
    far = pl.ds(pl.multiple_of((core + 2) * quarter, quarter), quarter)

    def columns(ref, at):
        return jnp.concatenate([ref[at, :, near], ref[at, :, far]], axis=1)

    arrived(1, 1)
    base = (columns(v, 2), columns(v, 3))
    r_u = arrived(0, 0)
    chain = cmul(r_u, base)
    r_v = arrived(1, 0)
    chain = cmul(r_v, half(chain))
    t_u = arrived(0, 1)
    chain = half((base[0] + chain[0], base[1] + chain[1]))
    here = cmul(t_u, chain)
    my = pl.ds(pl.multiple_of(place[2] * rows, rows), rows)
    row_t = (v[2, my, :], v[3, my, :])
    w_1 = half(cmul(row_t, r_u))
    k_part = cmul(w_1, chain)
    w_2 = cmul(w_1, r_v)
    w_2 = half((row_t[0] + w_2[0], row_t[1] + w_2[1]))
    g_rows = half(cmul(w_2, t_u))
    for side, (to, cols) in enumerate(((h_near, near), (h_far, far))):
        at = slice(side * quarter, (side + 1) * quarter)
        for c in range(2):
            to[c, 0:width, :] = here[c][:, at].astype(BF16)
            k_side = v[c, my, cols].astype(F32) + k_part[c][:, at]
            to[c, width : width + rows, :] = k_side.astype(BF16)
            for q in range(4):
                put = width + rows + q * rows
                to[c, put : put + rows, :] = g_rows[c][:, q * quarter : (q + 1) * quarter]


def form(place, own, other, rows):
    width = own.shape[1]
    scratch = [pltpu.VMEM(own.shape, BF16)] * 2 + [pltpu.SemaphoreType.DMA((4,))]
    params = pltpu.CompilerParams(vmem_limit_bytes=24 * 2**20)
    back, send = pl.pallas_call(
        back_kernel,
        out_shape=(
            jax.ShapeDtypeStruct((2, width, width // 2), BF16),
            jax.ShapeDtypeStruct((2, width // 2, width // 2), BF16),
        ),
        in_specs=[SMEM, ANY, ANY],
        out_specs=(VMEM, VMEM),
        scratch_shapes=scratch,
        compiler_params=params,
        cost_estimate=pl.CostEstimate(flops=2**32, bytes_accessed=2**23, transcendentals=0),
        name="back",
    )(place, own, other)
    shape = jax.ShapeDtypeStruct((2, width + 5 * rows, width // 4), BF16)
    near, far = pl.pallas_call(
        functools.partial(rows_kernel, rows),
        out_shape=(shape, shape),
        in_specs=[SMEM, ANY, ANY, ANY],
        out_specs=(VMEM, VMEM),
        scratch_shapes=scratch,
        compiler_params=params,
        cost_estimate=pl.CostEstimate(flops=2**32, bytes_accessed=2**23, transcendentals=0),
        name="rows",
    )(place, own, other, back)
    return back, send, near, far


def join_kernel(
    rows, place, s_mine, s_side, q_0, q_1, q_2, q_3, h_near, h_sent, refl, trans, sides, h, sems
):
    width = sides.shape[3]
    lower, core = place[3], place[1]
    many = width // 2
    this = pl.ds(pl.multiple_of(place[4] * many, many), many)
    that = pl.ds(pl.multiple_of((1 - place[4]) * many, many), many)
    moves = (
        ((h_near, h.at[lower]), 2),
        ((h_sent, h.at[1 - lower]), 2),
        ((s_mine, sides.at[lower, core]), lower),
        ((s_side, sides.at[lower, 1 - core]), lower),
        ((q_0, sides.at[1 - lower, core, :, this, :]), 1 - lower),
        ((q_1, sides.at[1 - lower, core, :, that, :]), 1 - lower),
        ((q_2, sides.at[1 - lower, 1 - core, :, this, :]), 1 - lower),
        ((q_3, sides.at[1 - lower, 1 - core, :, that, :]), 1 - lower),
    )
    for move, at in moves:
        pltpu.make_async_copy(*move, sems.at[at]).start()

    def arrived(ref, at):
        pltpu.make_async_copy(ref, ref, sems.at[at]).wait()

    arrived(h, 2)

    def rows_of(side):
        return tuple(
            jnp.concatenate(
                [
                    h[side, c, width + rows + q * rows : width + 2 * rows + q * rows, :]
                    for q in range(4)
                ],
                axis=1,
            )
            for c in range(2)
        )

    def times(pair, side):
        parts = [
            cmul(pair, (sides[side, at, 0], sides[side, at, 1]))
            for at in range(2)
        ]
        return tuple(jnp.concatenate([parts[0][c], parts[1][c]], axis=1) for c in range(2))

    from_above = rows_of(0)
    from_below = rows_of(1)
    arrived(sides.at[1], 1)
    second = half(times(from_above, 1))
    both = tuple(jnp.concatenate([from_below[c], second[c]], axis=0) for c in range(2))
    arrived(sides.at[0], 0)
    chain = times(half(times(both, 0)), 1)
    chain = half(tuple(both[c].astype(F32) + chain[c] for c in range(2)))
    result = cmul(chain, (h[0, 0, 0:width, :], h[0, 1, 0:width, :]))
    for c in range(2):
        trans[c] = result[c][0:rows]
        refl[c] = h[0, c, width : width + rows, :].astype(F32) + result[c][rows : 2 * rows]


def join(place, s_mine, s_side, quarters, h_near, h_sent, rows):
    columns = h_near.shape[2]
    shape = jax.ShapeDtypeStruct((2, rows, columns), F32)
    return pl.pallas_call(
        functools.partial(join_kernel, rows),
        out_shape=(shape, shape),
        in_specs=[SMEM] + [ANY] * 8,
        out_specs=(VMEM, VMEM),
        scratch_shapes=[
            pltpu.VMEM((2, 2) + s_mine.shape, BF16),
            pltpu.VMEM((2,) + h_near.shape, BF16),
            pltpu.SemaphoreType.DMA((3,)),
        ],
        compiler_params=pltpu.CompilerParams(vmem_limit_bytes=20 * 2**20),
        cost_estimate=pl.CostEstimate(flops=2**30, bytes_accessed=2**22, transcendentals=0),
        name="join",
    )(place, s_mine, s_side, *quarters, h_near, h_sent)


def whole_layers(inner, out_basis, in_basis, tmatrix, sites, waves, layer_phase):
    spheres, multi = tmatrix.shape[1], tmatrix.shape[3]
    half_width = waves.shape[1]
    width = 2 * half_width
    groups = lax.axis_size("sph")
    outer = groups // inner
    rows = width // groups
    layer = lax.axis_index("layer")

    block = pack(tmatrix[0], sites)

    def shifted(value, far, side):
        pairs = [
            (g, ((g // inner + far) % outer) * inner + (g % inner + side) % inner)
            for g in range(groups)
        ]
        return lax.ppermute(value, "sph", pairs)

    near = [shifted(block, 0, 1), shifted(block, 1, 0), shifted(block, outer - 1, 0)]
    near = [block, *near]
    tile, pair, waves_pad = prepare(out_basis[0], in_basis[0], waves, spheres)
    late, waves_pad = lax.optimization_barrier((block, waves_pad))
    ready = (tile, pair, waves_pad)
    far = [shifted(late, 2, 0), shifted(near[2], 0, 1), shifted(near[3], 0, 1)]
    far += [shifted(late, 2, 1)]

    part = layer_sum(near, spheres, multi, *ready)
    own = layer_sum(far, spheres, multi, *ready, part, layer_phase[0])

    other = lax.ppermute(own, "layer", [(at, at ^ 1) for at in range(4)])
    core, lower = layer % 2, layer // 2
    mine_is_u = jnp.where(core != lower, 1, 0)
    group = lax.axis_index("sph")
    side = group % inner
    place = jnp.stack([mine_is_u, core, group, lower, side]).astype(jnp.int32)
    s_mine, s_send, h_near, h_far = form(place, own, other, rows)

    def crossed(value, bit):
        return lax.ppermute(value, "layer", [(at, at ^ bit) for at in range(4)])

    s_far = crossed(s_send, 2)
    h_sent = crossed(h_far, 2)
    s_side = crossed(s_mine, 1)
    s_far, h_near = lax.optimization_barrier((s_far, h_near))
    s_next = shifted(s_far, 0, 1)
    quarters = (s_far, s_next, crossed(s_far, 1), crossed(s_next, 1))
    return join(place, s_mine, s_side, quarters, h_near, h_sent, rows)


def solution(mesh):
    in_specs = (
        P("layer", None, None, None, None),
        P("layer", None, None, None),
        P("layer", "sph", None, None, None),
        P("layer", "sph"),
        P(),
        P("layer", None),
    )
    out_specs = (P(None, "sph", "layer"), P(None, "sph", "layer"))
    on_device = by_rows
    if mesh.shape["layer"] == 4 and mesh.shape["sph"] == 8:
        on_device = functools.partial(whole_layers, 2)
    return jax.shard_map(
        on_device, mesh=mesh, in_specs=in_specs, out_specs=out_specs, check_vma=False
    )
```
